256 devices in a mesh: gx: 16 (over y, x), gy: 16 (over z, core).
Axes of the slice: x: 4, y: 4, z: 8, core: 2. Of those that a mesh axis runs over, the one named last changes fastest.
Arguments:
- pressure_source: float32 [16, 512, 2048], P(None, 'gx', 'gy'), may hold values from -0.5 to 1.5
- density: float32 [16, 512, 2048], P(None, 'gx', 'gy'), may hold values from 0.5 to 4
Outputs:
- pressure: float32 [16, 512, 2048], P(None, 'gx', 'gy')
The draws below stay inside these ranges and needn't reach their ends.
All inputs are finite; a program needn't handle non-finite values.
Results may differ from the reference program's by a relative error of at most 0.0001.
Values sent between devices are 32-bit elements; how exact they have to be, the bound alone decides.
No kernel may reach another device: no remote copies, remote signals or barrier semaphores. Data moves between devices by JAX's collectives and lax.ppermute only.
A program may use at most 128 MiB of HBM per device.

```python
import math
import jax
import jax.numpy as jnp

NZ = 16
LEVELS = 4
COARSE_SWEEPS = 6
NX = 512
NY = 2048


def steps_of(key, extent, pieces, low, high):
    gain, own = 1.0, jax.random.fold_in(key, 6)
    for position, blocks in pieces:
        heights = jnp.exp(jax.random.uniform(jax.random.fold_in(own, position), (blocks,), jnp.float32, low / len(pieces), high / len(pieces)))
        gain = gain * jnp.repeat(heights, extent[position] // blocks).reshape([-1 if axis == position else 1 for axis in range(len(extent))])
    return gain


def setup_inputs(seed: int = 0) -> dict:
    seeds = jax.random.split(jax.random.key(seed), 3)
    pressure_source = jnp.clip(-0.5 + 2.0 * jax.random.uniform(seeds[0], (NZ, NX, NY), jnp.float32) ** steps_of(seeds[0], (NZ, NX, NY), ((1, 16), (2, 16)), -0.2, 0.2), -0.5, 1.5)
    density = jnp.clip(jnp.exp(math.log(4.0) - 2.0794415 * jax.random.uniform(seeds[1], (NZ, NX, NY), jnp.float32) ** steps_of(seeds[1], (NZ, NX, NY), ((1, 16), (2, 16)), -0.2, 0.2)), 0.5, 4.0)
    return {"pressure_source": pressure_source, "density": density}


damping = 0.8
vertical_weight = 0.015625


def face_factors(padded_rho, spacing_factor):
    center_rho = padded_rho[:, 1:-1, 1:-1]
    across_x = spacing_factor * 2.0 / (padded_rho[:, :-1, 1:-1] + padded_rho[:, 1:, 1:-1])
    across_y = spacing_factor * 2.0 / (padded_rho[:, 1:-1, :-1] + padded_rho[:, 1:-1, 1:])
    above_rho = jnp.concatenate([jnp.zeros_like(center_rho[:1]), center_rho[:-1]], axis=0)
    above_face = vertical_weight * 2.0 / (above_rho + center_rho)
    below_face = jnp.concatenate([above_face[1:], jnp.zeros_like(above_face[:1])], axis=0)
    center_sum = across_x[:, :-1] + across_x[:, 1:] + across_y[:, :, :-1] + across_y[:, :, 1:] + above_face + below_face
    return across_x, across_y, above_face, below_face, center_sum


def horizontal_pull(padded_values, factors):
    across_x, across_y = factors[0], factors[1]
    total = across_x[:, :-1] * padded_values[:, :-2, 1:-1] + across_x[:, 1:] * padded_values[:, 2:, 1:-1]
    return total + across_y[:, :, :-1] * padded_values[:, 1:-1, :-2] + across_y[:, :, 1:] * padded_values[:, 1:-1, 2:]


def column_solve(factors, target):
    above_face, below_face, center_sum = factors[2], factors[3], factors[4]
    layers = target.shape[0]
    ratios = []
    partial_sums = []
    pivot = center_sum[0]
    ratios.append(-below_face[0] / pivot)
    partial_sums.append(target[0] / pivot)
    for layer in range(1, layers):
        pivot = center_sum[layer] + above_face[layer] * ratios[layer - 1]
        ratios.append(-below_face[layer] / pivot)
        partial_sums.append((target[layer] + above_face[layer] * partial_sums[layer - 1]) / pivot)
    solved = [None] * layers
    solved[layers - 1] = partial_sums[layers - 1]
    for layer in range(layers - 2, -1, -1):
        solved[layer] = partial_sums[layer] - ratios[layer] * solved[layer + 1]
    return jnp.stack(solved, axis=0)


def relax_from_zero(factors, source):
    return damping * column_solve(factors, source)


def relax(values, padded_values, factors, source):
    solved = column_solve(factors, source + horizontal_pull(padded_values, factors))
    return values + damping * (solved - values)


def residual_of(values, padded_values, factors, source):
    above_values = jnp.concatenate([jnp.zeros_like(values[:1]), values[:-1]], axis=0)
    below_values = jnp.concatenate([values[1:], jnp.zeros_like(values[:1])], axis=0)
    applied = factors[4] * values - horizontal_pull(padded_values, factors) - factors[2] * above_values - factors[3] * below_values
    return source - applied


def coarsen(array_in):
    layers, rows, cols = array_in.shape
    return array_in.reshape(layers, rows // 2, 2, cols // 2, 2).mean(axis=(2, 4))


def prolong(array_in):
    return jnp.repeat(jnp.repeat(array_in, 2, axis=1), 2, axis=2)


def extend(array_in):
    return jnp.pad(array_in, ((0, 0), (1, 1), (1, 1)))


def reference(pressure_source, density):
    densities = [density]
    for level_index in range(LEVELS):
        densities.append(coarsen(densities[-1]))
    all_factors = [face_factors(extend(densities[level_index]), 0.25 ** level_index) for level_index in range(LEVELS + 1)]

    def cycle(level_index, source):
        factors = all_factors[level_index]
        if level_index == LEVELS:
            values = relax_from_zero(factors, source)
            for sweep in range(COARSE_SWEEPS - 1):
                values = relax(values, extend(values), factors, source)
            remains = residual_of(values, extend(values), factors, source)
            shift = jnp.sum(remains, axis=(1, 2)) / jnp.sum(factors[4], axis=(1, 2))
            return values + shift[:, None, None]
        values = relax_from_zero(factors, source)
        values = relax(values, extend(values), factors, source)
        remains = residual_of(values, extend(values), factors, source)
        values = values + prolong(cycle(level_index + 1, coarsen(remains)))
        for sweep in range(2):
            values = relax(values, extend(values), factors, source)
        return values

    return cycle(0, pressure_source)
```

```python
import jax
import jax.numpy as jnp
from jax import lax
from jax.experimental import pallas as pl
from jax.experimental.pallas import tpu as pltpu
from jax.sharding import PartitionSpec as P

NZ = 16
LANES = 128
SWEEPS = 6
VERTICAL = 0.015625
TINY = 2.0**-20
VMEM_BYTES = 48 * 1024 * 1024

ROW0 = (16, 8, 16, 8)
ROWS = (64, 32, 40, 24)
LANE0 = (0, 32, 16, 8)


def spacing(level):
    return 2.0 * 0.25**level


def lanes_of(shape=(8, LANES)):
    return lax.broadcasted_iota(jnp.int32, shape, 1)


def rows_of(shape=(8, LANES)):
    return lax.broadcasted_iota(jnp.int32, shape, 0)


def rcp(x):
    guess = pl.reciprocal(x, approx=True)
    return guess * (2.0 - x * guess)


def from_left(xs):
    rolled = [pltpu.roll(x, 1, 1) for x in xs]
    if len(xs) == 1:
        return rolled
    edge = lanes_of() == 0
    return [jnp.where(edge, rolled[1], rolled[0]), jnp.where(edge, rolled[0], rolled[1])]


def from_right(xs):
    rolled = [pltpu.roll(x, LANES - 1, 1) for x in xs]
    if len(xs) == 1:
        return rolled
    edge = lanes_of() == LANES - 1
    return [jnp.where(edge, rolled[1], rolled[0]), jnp.where(edge, rolled[0], rolled[1])]


def split_dot(x, matrix):
    high = x.astype(jnp.bfloat16)
    rest = x - high.astype(jnp.float32)
    middle = rest.astype(jnp.bfloat16)
    low = (rest - middle.astype(jnp.float32)).astype(jnp.bfloat16)
    dot = lambda part: jnp.dot(part, matrix, preferred_element_type=jnp.float32)
    return dot(high) + dot(middle) + dot(low)


def one_hot(rows, test, value):
    shape = (rows, LANES)
    source, target = lax.broadcasted_iota(jnp.int32, shape, 0), lax.broadcasted_iota(jnp.int32, shape, 1)
    return jnp.where(test(source, target), value, 0.0).astype(jnp.bfloat16)


def block_loop(starts, body):
    if len(starts) <= 3:
        for start in starts:
            body(start)
        return
    first, last = starts[0], starts[-1]

    def step(index, carry):
        body(jnp.minimum(first + 8 * index, last))
        return carry

    lax.fori_loop(0, len(starts), step, 0)


def starts_for(low, high):
    starts = list(range(low, high - 6, 8))
    if starts[-1] + 7 < high:
        starts.append(high - 7)
    return [min(s, high - 7) for s in starts]


class Level:
    def __init__(self, level, rho, ax, ay, d, e, g):
        self.level, self.rho, self.ax, self.ay, self.d, self.e, self.g = level, rho, ax, ay, d, e, g
        self.parts = range(len(ax))

    def faces(self, starts):
        scale = spacing(self.level)

        def body(r):
            for k in range(NZ):
                here = [ref[k, pl.ds(r, 8), :] for ref in self.rho]
                above = [ref[k, pl.ds(r - 1, 8), :] for ref in self.rho]
                left = from_left(here)
                for p in self.parts:
                    self.ax[p][k, pl.ds(r, 8), :] = scale * rcp(jnp.maximum(here[p] + above[p], TINY))
                    self.ay[p][k, pl.ds(r, 8), :] = scale * rcp(jnp.maximum(here[p] + left[p], TINY))

        block_loop(starts, body)

    def factor_and_first(self, starts, inside, f, v):
        def body(r):
            masks = [inside(r, p) for p in self.parts]
            ratio = [None for p in self.parts]
            partial = [[] for p in self.parts]
            ratios = [[] for p in self.parts]
            upper = [None for p in self.parts]
            rho = [ref[0, pl.ds(r, 8), :] for ref in self.rho]
            for p in self.parts:
                upper[p] = (2.0 * VERTICAL) * rcp(jnp.maximum(rho[p], TINY))
            for k in range(NZ):
                if k + 1 < NZ:
                    below = [ref[k + 1, pl.ds(r, 8), :] for ref in self.rho]
                    lower = [
                        (2.0 * VERTICAL) * rcp(jnp.maximum(rho[p] + below[p], TINY)) for p in self.parts
                    ]
                ay = [ref[k, pl.ds(r, 8), :] for ref in self.ay]
                right = from_right(ay)
                for p in self.parts:
                    center = (
                        self.ax[p][k, pl.ds(r, 8), :]
                        + self.ax[p][k, pl.ds(r + 1, 8), :]
                        + ay[p]
                        + right[p]
                        + upper[p]
                    )
                    if k + 1 < NZ:
                        center = center + lower[p]
                    pivot = center if k == 0 else center - upper[p] * ratio[p]
                    inverse = jnp.where(masks[p], rcp(pivot), 0.0)
                    scaled = 0.8 * inverse
                    self.d[p][k, pl.ds(r, 8), :] = scaled
                    value = scaled * f[p][k, pl.ds(r, 8), :]
                    if k > 0:
                        weight = upper[p] * inverse
                        self.e[p][k, pl.ds(r, 8), :] = weight
                        value = value + weight * partial[p][-1]
                    partial[p].append(value)
                    if k + 1 < NZ:
                        ratio[p] = lower[p] * inverse
                        self.g[p][k, pl.ds(r, 8), :] = ratio[p]
                        ratios[p].append(ratio[p])
                if k + 1 < NZ:
                    rho, upper = below, lower
            for p in self.parts:
                w = partial[p][-1]
                v[p][NZ - 1, pl.ds(r, 8), :] = w
                for k in range(NZ - 2, -1, -1):
                    w = partial[p][k] + ratios[p][k] * w
                    v[p][k, pl.ds(r, 8), :] = w

        block_loop(starts, body)

    def pull(self, v, k, r, wanted):
        here = [ref[k, pl.ds(r, 8), :] for ref in v]
        ay = [ref[k, pl.ds(r, 8), :] for ref in self.ay]
        left = from_left(here)
        right = from_right([a * x for a, x in zip(ay, here)])
        return here, [
            self.ax[p][k, pl.ds(r, 8), :] * v[p][k, pl.ds(r - 1, 8), :]
            + self.ax[p][k, pl.ds(r + 1, 8), :] * v[p][k, pl.ds(r + 1, 8), :]
            + ay[p] * left[p]
            + right[p]
            for p in wanted
        ]

    def relax(self, starts, f, v, out, u=None, wanted=None, shift=0):
        wanted = self.parts if wanted is None else wanted

        def body(r):
            partial = [[] for p in wanted]
            for k in range(NZ):
                _, pulls = self.pull(v, k, r, wanted)
                for n, p in enumerate(wanted):
                    value = self.d[p][k, pl.ds(r, 8), :] * (f[p][k, pl.ds(r, 8), :] + pulls[n])
                    if k > 0:
                        value = value + self.e[p][k, pl.ds(r, 8), :] * partial[n][-1]
                    partial[n].append(value)
            for n, p in enumerate(wanted):
                w = None
                for k in range(NZ - 1, -1, -1):
                    w = partial[n][k] if w is None else partial[n][k] + self.g[p][k, pl.ds(r, 8), :] * w
                    old = v[p][k, pl.ds(r, 8), :]
                    out[p][k, pl.ds(r - shift, 8), :] = 0.2 * old + w
                    if u is not None:
                        u[p][k, pl.ds(r, 8), :] = w - 0.6 * old

        block_loop(starts, body)

    def residual(self, starts, f, u, out):
        def body(r):
            for k in range(NZ):
                _, pulls = self.pull(u, k, r, self.parts)
                for p in self.parts:
                    out[p][k, pl.ds(r, 8), :] = 0.04 * f[p][k, pl.ds(r, 8), :] + pulls[p]

        block_loop(starts, body)


def inside_of(level, ix, iy, shape):
    grid_rows, grid_lanes, tile_rows, tile_lanes = shape
    lane = lanes_of()
    if level == 0:
        low_side = jnp.logical_and(lane < 64, iy * tile_lanes + tile_lanes < grid_lanes)
        sides = [None, jnp.logical_or(low_side, jnp.logical_and(lane >= 64, iy > 0))]
    else:
        column = iy * tile_lanes + lane - LANE0[level]
        sides = [jnp.logical_and(column >= 0, column < grid_lanes)]

    def inside(r, part):
        row = rows_of() + (r + ix * tile_rows - ROW0[level])
        good = jnp.logical_and(row >= 0, row < grid_rows)
        return good if sides[part] is None else jnp.logical_and(good, sides[part])

    return inside


def pair_rows(ref, k, start, count):
    layer = ref.at[k]
    return layer[pl.ds(start, count, stride=2), :] + layer[pl.ds(start + 1, count, stride=2), :]


def stack_rows(blocks):
    return jnp.concatenate(blocks, axis=0)


def down_kernel(ref, level, f, v, u, res, plan, inside):
    ref.faces(plan["faces"])
    ref.factor_and_first(plan["first"], inside, f, u)
    ref.relax(plan["second"], f, u, v, u=res)


def edges_kernel(f_ref, rho_ref, up_ref, dn_ref, left_ref, right_ref):
    lane = lanes_of()
    slot = lane // 16
    for field, own in enumerate((f_ref, rho_ref)):
        for block in range(8):
            for half in range(2):
                lefts, rights = None, None
                for q in range(8):
                    k = half * 8 + q
                    if block < 2:
                        x = up_ref[field * NZ + k, pl.ds(block * 8, 8), :]
                    elif block < 6:
                        x = own[k, pl.ds(block * 8 - 16, 8), :]
                    else:
                        x = dn_ref[field * NZ + k, pl.ds(block * 8 - 48, 8), :]
                    a = x if q == 0 else pltpu.roll(x, 16 * q, 1)
                    b = pltpu.roll(x, 16 * q + 16, 1) if q < 7 else x
                    lefts = a if q == 0 else jnp.where(slot == q, a, lefts)
                    rights = b if q == 0 else jnp.where(slot == q, b, rights)
                left_ref[field * 2 + half, pl.ds(block * 8, 8), :] = lefts
                right_ref[field * 2 + half, pl.ds(block * 8, 8), :] = rights


def fine_kernel(
    grid, index_ref, f_ref, rho_ref, up_ref, dn_ref, from_left_ref, from_right_ref,
    pack_ref, fm, fh, vm, vh, axm, axh, aym, ayh, dm, dh, em, eh, gm, gh, f1, v1, ax1, ay1, d1, e1, g1,
    rm, rh, firstm, firsth, um, uh, rho1, first1, u1, res1,
):
    ix, iy = index_ref[0], index_ref[1]
    grid_rows, grid_lanes = grid
    lane = lanes_of()
    inside = inside_of(0, ix, iy, (grid_rows, grid_lanes, 32, 128))

    for field, (own, main, side) in enumerate(((f_ref, fm, fh), (rho_ref, rm, rh))):
        for block in range(8):
            good = [inside(block * 8, part) for part in range(2)]
            for k in range(NZ):
                if block < 2:
                    x = up_ref[field * NZ + k, pl.ds(block * 8, 8), :]
                elif block < 6:
                    x = own[k, pl.ds(block * 8 - 16, 8), :]
                else:
                    x = dn_ref[field * NZ + k, pl.ds(block * 8 - 48, 8), :]
                q, half = k % 8, k // 8
                a = from_right_ref[field * 2 + half, pl.ds(block * 8, 8), :]
                a = a if q == 0 else pltpu.roll(a, LANES - 16 * q, 1)
                b = from_left_ref[field * 2 + half, pl.ds(block * 8, 8), :]
                b = b if q == 7 else pltpu.roll(b, 112 - 16 * q, 1)
                y = jnp.where(lane < 16, a, jnp.where(lane >= 112, b, 0.0))
                if field == 1:
                    y = jnp.where(good[1], y, 0.0)
                    if block < 2 or block >= 6:
                        x = jnp.where(good[0], x, 0.0)
                main[k, pl.ds(block * 8, 8), :] = x
                side[k, pl.ds(block * 8, 8), :] = y

    fine = Level(0, [rm, rh], [axm, axh], [aym, ayh], [dm, dh], [em, eh], [gm, gh])
    fine.faces(starts_for(6, 58))
    fine.factor_and_first(starts_for(6, 57), inside, [fm, fh], [firstm, firsth])
    fine.relax(starts_for(7, 56), [fm, fh], [firstm, firsth], [vm, vh], u=[um, uh])
    fine.residual(starts_for(8, 55), [fm, fh], [um, uh], [firstm, firsth])

    main_matrix = one_hot(LANES, lambda s, t: s // 2 + 32 == t, 0.25)
    side_matrix = one_hot(
        LANES,
        lambda s, t: jnp.logical_or(
            jnp.logical_and(s < 64, s // 2 + 96 == t), jnp.logical_and(s >= 64, s // 2 - 32 == t)
        ),
        0.25,
    )
    for first in range(0, NZ, 4):
        ks = range(first, first + 4)
        total = split_dot(stack_rows([pair_rows(firstm, k, 8, 24) for k in ks]), main_matrix)
        total = total + split_dot(stack_rows([pair_rows(firsth, k, 8, 24) for k in ks]), side_matrix)
        for n, k in enumerate(ks):
            f1[k, pl.ds(4, 24), :] = total[n * 24 : (n + 1) * 24]
        total = split_dot(stack_rows([pair_rows(rm, k, 0, 32) for k in ks]), main_matrix)
        total = total + split_dot(stack_rows([pair_rows(rh, k, 0, 32) for k in ks]), side_matrix)
        for n, k in enumerate(ks):
            rho1[k, :, :] = total[n * 32 : (n + 1) * 32]

    middle = Level(1, [rho1], [ax1], [ay1], [d1], [e1], [g1])
    inside = inside_of(1, ix, iy, (grid_rows // 2, grid_lanes // 2, 16, 64))
    middle.faces(starts_for(4, 28))
    middle.factor_and_first(starts_for(4, 27), inside, [f1], [first1])
    middle.relax(starts_for(5, 26), [f1], [first1], [v1], u=[u1])
    middle.residual(starts_for(8, 23), [f1], [u1], [res1])

    pack_matrix = one_hot(
        4 * LANES,
        lambda s, t: jnp.logical_and(
            (s % LANES) // 2 - 16 + 32 * (s // LANES) == t,
            jnp.logical_and(s % LANES >= 32, s % LANES < 96),
        ),
        0.25,
    )
    blocks = []
    for ref in (res1, rho1):
        for group in range(4):
            blocks.append(jnp.concatenate([pair_rows(ref, 4 * group + q, 8, 8) for q in range(4)], axis=1))
    packed = split_dot(stack_rows(blocks), pack_matrix)
    for n in range(8):
        pack_ref[n, :, :] = packed[n * 8 : (n + 1) * 8]


def coarser_kernel(
    grid, index_ref, own_ref, from_left_ref, from_right_ref,
    pack_ref, f2, v2, ax2, ay2, d2, e2, g2, f3, v3, ax3, ay3, d3, e3, g3,
    rho2, first2, u2, res2, rho3, first3, u3, res3,
):
    ix, iy = index_ref[0], index_ref[1]
    grid_rows, grid_lanes = grid
    lane = lanes_of()
    inside = inside_of(2, ix, iy, (grid_rows // 4, grid_lanes // 4, 8, 32))

    for field, target in enumerate((f2, rho2)):
        for block in range(5):
            good = inside(block * 8, 0)
            for k in range(NZ):
                group, q = field * 4 + k // 4, k % 4
                rolled = []
                for ref, amount in (
                    (from_left_ref, LANES - q * 32 - 16),
                    (own_ref, LANES + 16 - 32 * q),
                    (from_right_ref, LANES + 48 - 32 * q),
                ):
                    x = ref[group, pl.ds(block * 8, 8), :]
                    rolled.append(pltpu.roll(x, amount % LANES, 1))
                y = jnp.where(lane < 16, rolled[0], jnp.where(lane < 48, rolled[1], rolled[2]))
                if field == 1:
                    y = jnp.where(good, y, 0.0)
                target[k, pl.ds(block * 8, 8), :] = jnp.where(lane < 64, y, 0.0)

    level2 = Level(2, [rho2], [ax2], [ay2], [d2], [e2], [g2])
    level2.faces(starts_for(4, 36))
    level2.factor_and_first(starts_for(4, 35), inside, [f2], [first2])
    level2.relax(starts_for(5, 34), [f2], [first2], [v2], u=[u2])
    level2.residual(starts_for(6, 33), [f2], [u2], [res2])

    halve = one_hot(LANES, lambda s, t: s // 2 == t, 0.25)
    for ref, target, first, count in ((res2, f3, 4, 16), (rho2, rho3, 4, 16)):
        total = split_dot(stack_rows([pair_rows(ref, k, first, count) for k in range(NZ)]), halve)
        for k in range(NZ):
            target[k, pl.ds(first // 2, count), :] = total[k * count : (k + 1) * count]

    level3 = Level(3, [rho3], [ax3], [ay3], [d3], [e3], [g3])
    inside = inside_of(3, ix, iy, (grid_rows // 8, grid_lanes // 8, 4, 16))
    level3.faces(starts_for(3, 17))
    level3.factor_and_first(starts_for(3, 16), inside, [f3], [first3])
    level3.relax(starts_for(4, 15), [f3], [first3], [v3], u=[u3])
    level3.residual([6], [f3], [u3], [res3])

    spread = one_hot(
        LANES,
        lambda s, t: jnp.logical_and(s // 2 - 4 == t % 8, jnp.logical_and(s >= 8, s < 24)),
        0.25,
    )
    for field, ref in enumerate((res3, rho3)):
        total = split_dot(stack_rows([pair_rows(ref, k, 8, 8) for k in range(NZ)]), spread)
        merged = total[0:8]
        for k in range(1, NZ):
            merged = jnp.where(lane // 8 == k, total[k * 8 : (k + 1) * 8], merged)
        pack_ref[pl.ds(2 * field, 2), :] = merged[0:2]


def prolong(coarse, first_row, count, ref, old, target, target_row, matrix):
    rows = stack_rows([coarse(k) for k in range(NZ)])
    for part in range(len(target)):
        fine = split_dot(rows, matrix[part])
        for k in range(NZ):
            x = fine[k * count : (k + 1) * count]
            for odd in range(2):
                where = pl.ds(target_row + odd, count, stride=2)
                target[part].at[k][where, :] = old[part].at[k][where, :] + x


def top_kernel(
    grid, tiles, index_ref, gathered, fm, fh, vm, vh, axm, axh, aym, ayh, dm, dh, em, eh, gm, gh,
    f1, v1, ax1, ay1, d1, e1, g1, f2, v2, ax2, ay2, d2, e2, g2, f3, v3, ax3, ay3, d3, e3, g3,
    out_ref,
    rho4, f4, ax4, ay4, d4, e4, g4, q4, va4, vb4, va3, vb3, va2, vb2, va1, vb1, vam, vah, vbm, vbh,
):
    ix, iy = index_ref[0], index_ref[1]
    grid_rows, grid_lanes = grid
    lane = lanes_of()
    rows4 = grid_rows // 16
    tiles_x, tiles_y = tiles

    zero = jnp.zeros((8, LANES), jnp.float32)
    for ref in (rho4, va4, vb4):
        for k in range(NZ):
            ref[k, pl.ds(0, 8), :] = zero
            ref[k, pl.ds(8 + rows4, 8), :] = zero

    count = min(8, tiles_x)
    for field, target in enumerate((f4, rho4)):
        for r in range(2):
            for base in range(0, tiles_x, count):
                xs = [
                    gathered[pl.ds((base * tiles_y + t) * 4 + field * 2 + r, count, stride=4 * tiles_y), :]
                    for t in range(16)
                ]
                column = lax.broadcasted_iota(jnp.int32, (count, LANES), 1) // 8
                for bit in (1, 2, 4, 8):
                    high = (column & bit) != 0
                    for i in range(16):
                        if i & bit:
                            continue
                        a, b = xs[i], xs[i | bit]
                        xs[i] = jnp.where(high, pltpu.roll(b, 8 * bit, 1), a)
                        xs[i | bit] = jnp.where(high, b, pltpu.roll(a, LANES - 8 * bit, 1))
                for k in range(NZ):
                    target.at[k][pl.ds(8 + 2 * base + r, count, stride=2), :] = xs[k]

    scale = spacing(4)
    first_lane, last_lane = lane == 0, lane == LANES - 1
    starts = list(range(8, 8 + rows4, 8))
    for r in starts + [rows4 + 1]:
        for k in range(NZ):
            here = rho4[k, pl.ds(r, 8), :]
            above = rho4[k, pl.ds(r - 1, 8), :]
            left = jnp.where(first_lane, 0.0, pltpu.roll(here, 1, 1))
            ax4[k, pl.ds(r, 8), :] = scale * rcp(jnp.maximum(here + above, TINY))
            if r in starts:
                ay4[k, pl.ds(r, 8), :] = scale * rcp(jnp.maximum(here + left, TINY))

    centers = [None] * NZ
    for r in starts:
        rho = rho4[0, pl.ds(r, 8), :]
        upper = (2.0 * VERTICAL) * rcp(rho)
        partial, ratios, ratio = [], [], None
        for k in range(NZ):
            ay = ay4[k, pl.ds(r, 8), :]
            right = jnp.where(last_lane, scale * rcp(rho), pltpu.roll(ay, LANES - 1, 1))
            center = ax4[k, pl.ds(r, 8), :] + ax4[k, pl.ds(r + 1, 8), :] + ay + right + upper
            if k + 1 < NZ:
                below = rho4[k + 1, pl.ds(r, 8), :]
                lower = (2.0 * VERTICAL) * rcp(rho + below)
                center = center + lower
            centers[k] = center if centers[k] is None else centers[k] + center
            pivot = center if k == 0 else center - upper * ratio
            inverse = rcp(pivot)
            scaled = 0.8 * inverse
            d4[k, pl.ds(r, 8), :] = scaled
            source = f4[k, pl.ds(r, 8), :]
            q4[k, pl.ds(r, 8), :] = 0.8 * source
            value = scaled * source
            if k > 0:
                weight = upper * inverse
                e4[k, pl.ds(r, 8), :] = weight
                value = value + weight * partial[-1]
            partial.append(value)
            if k + 1 < NZ:
                ratio = lower * inverse
                g4[k, pl.ds(r, 8), :] = ratio
                ratios.append(ratio)
                rho, upper = below, lower
        w = partial[-1]
        va4[NZ - 1, pl.ds(r, 8), :] = w
        for k in range(NZ - 2, -1, -1):
            w = partial[k] + ratios[k] * w
            va4[k, pl.ds(r, 8), :] = w

    def pull4(v, k, r):
        here = v[k, pl.ds(r, 8), :]
        ay = ay4[k, pl.ds(r, 8), :]
        left = jnp.where(first_lane, 0.0, pltpu.roll(here, 1, 1))
        right = jnp.where(last_lane, 0.0, pltpu.roll(ay * here, LANES - 1, 1))
        return (
            f4[k, pl.ds(r, 8), :]
            + ax4[k, pl.ds(r, 8), :] * v[k, pl.ds(r - 1, 8), :]
            + ax4[k, pl.ds(r + 1, 8), :] * v[k, pl.ds(r + 1, 8), :]
            + ay * left
            + right
        )

    def sweep(v, out):
        for r in starts:
            partial = []
            for k in range(NZ):
                pulled = pull4(v, k, r)
                q4[k, pl.ds(r, 8), :] = 0.2 * q4[k, pl.ds(r, 8), :] + 0.8 * pulled
                value = d4[k, pl.ds(r, 8), :] * pulled
                if k > 0:
                    value = value + e4[k, pl.ds(r, 8), :] * partial[-1]
                partial.append(value)
            w = None
            for k in range(NZ - 1, -1, -1):
                w = partial[k] if w is None else partial[k] + g4[k, pl.ds(r, 8), :] * w
                out[k, pl.ds(r, 8), :] = 0.2 * v[k, pl.ds(r, 8), :] + w

    ends = [va4, vb4]
    for number in range(SWEEPS - 1):
        sweep(ends[number % 2], ends[(number + 1) % 2])
    final = ends[(SWEEPS - 1) % 2]
    shifts = []
    for k in range(NZ):
        total = None
        for r in starts:
            part = pull4(final, k, r) - q4[k, pl.ds(r, 8), :]
            total = part if total is None else total + part
        raised = jnp.sum(total, axis=(0, 1), keepdims=True)
        shifts.append(raised / jnp.sum(centers[k], axis=(0, 1), keepdims=True))

    row = rows_of() + (ix * 2 - 4)
    column = lane + (iy * 8 - 4)
    good = jnp.logical_and(
        jnp.logical_and(row >= 0, row < rows4),
        jnp.logical_and(jnp.logical_and(column >= 0, column < grid_lanes // 16), lane < 16),
    )
    amount = lax.rem(132 - iy * 8, LANES)

    def coarsest(k):
        x = final[k, pl.ds(4 + 2 * ix, 8), :] + shifts[k]
        return jnp.where(good, pltpu.roll(x, amount, 1), 0.0)

    repeat = one_hot(LANES, lambda s, t: s == t // 2, 1.0)
    prolong(coarsest, 0, 8, None, [v3], [va3], 0, [repeat])
    level3 = Level(3, None, [ax3], [ay3], [d3], [e3], [g3])
    level3.relax(starts_for(5, 14), [f3], [va3], [vb3])
    level3.relax([6], [f3], [vb3], [va3])

    prolong(lambda k: va3[k, pl.ds(6, 8), :], 0, 8, None, [v2], [va2], 12, [repeat])
    level2 = Level(2, None, [ax2], [ay2], [d2], [e2], [g2])
    level2.relax(starts_for(13, 26), [f2], [va2], [vb2])
    level2.relax(starts_for(14, 25), [f2], [vb2], [va2])

    prolong(lambda k: va2[k, pl.ds(12, 16), :], 0, 16, None, [v1], [va1], 0, [repeat])
    level1 = Level(1, None, [ax1], [ay1], [d1], [e1], [g1])
    level1.relax(starts_for(6, 25), [f1], [va1], [vb1])
    level1.relax(starts_for(7, 24), [f1], [vb1], [va1])

    to_main = one_hot(LANES, lambda s, t: s == t // 2 + 32, 1.0)
    to_side = one_hot(
        LANES,
        lambda s, t: jnp.logical_or(
            jnp.logical_and(t < 64, s == t // 2 + 96), jnp.logical_and(t >= 64, s == t // 2 - 32)
        ),
        1.0,
    )
    prolong(lambda k: va1[k, pl.ds(4, 24), :], 0, 24, None, [vm, vh], [vam, vah], 8, [to_main, to_side])
    fine = Level(0, None, [axm, axh], [aym, ayh], [dm, dh], [em, eh], [gm, gh])
    fine.relax(starts_for(15, 48), [fm, fh], [vam, vah], [vbm, vbh])
    fine.relax(starts_for(16, 47), [fm, fh], [vbm, vbh], [out_ref], wanted=[0], shift=16)


def ring(x, axis, step):
    size = lax.axis_size(axis)
    return lax.ppermute(x, axis, [(i, (i + step) % size) for i in range(size)])


def array(*shape):
    return jax.ShapeDtypeStruct(shape, jnp.float32)


def call(kernel, name, outs, scratch, index, *operands):
    vmem = pl.BlockSpec(memory_space=pltpu.VMEM)
    ins = [vmem] * len(operands)
    if index is not None:
        ins, operands = [pl.BlockSpec(memory_space=pltpu.SMEM)] + ins, (index,) + operands
    return pl.pallas_call(
        kernel,
        out_shape=outs,
        in_specs=ins,
        out_specs=[vmem] * len(outs),
        scratch_shapes=[pltpu.VMEM(shape, jnp.float32) for shape in scratch],
        compiler_params=pltpu.CompilerParams(vmem_limit_bytes=VMEM_BYTES),
        name=name,
    )(*operands)


def solution(mesh):
    tiles_x, tiles_y = mesh.shape["gx"], mesh.shape["gy"]
    grid = (32 * tiles_x, 128 * tiles_y)
    big = [array(NZ, ROWS[level], LANES) for level in range(4)]

    def on_device(source, rho):
        index = jnp.stack([lax.axis_index("gx"), lax.axis_index("gy")]).astype(jnp.int32)

        lows = jnp.concatenate([source[:, :16], rho[:, :16]], axis=0)
        highs = jnp.concatenate([source[:, 16:], rho[:, 16:]], axis=0)
        up = ring(highs, "gx", 1)
        dn = ring(lows, "gx", -1)
        strip = array(4, ROWS[0], LANES)
        lefts, rights = call(edges_kernel, "edges", [strip, strip], [], None, source, rho, up, dn)
        from_left_strip = ring(rights, "gy", 1)
        from_right_strip = ring(lefts, "gy", -1)

        s0, s1, s2, s3 = [x.shape for x in big]
        fine = call(
            lambda *refs: fine_kernel(grid, *refs),
            "fine",
            [array(8, 8, LANES)] + [big[0]] * 14 + [big[1]] * 7,
            [s0] * 6 + [s1] * 4,
            index, source, rho, up, dn, from_left_strip, from_right_strip,
        )
        tile = fine[0]
        pieces = [ring(tile, "gx", 2), ring(tile, "gx", 1), tile, ring(tile, "gx", -1), ring(tile, "gx", -2)]
        column = jnp.concatenate(pieces, axis=1)
        from_left_column = ring(column, "gy", 1)
        from_right_column = ring(column, "gy", -1)
        coarser = call(
            lambda *refs: coarser_kernel(grid, *refs),
            "coarser",
            [array(4, LANES)] + [big[2]] * 7 + [big[3]] * 7,
            [s2] * 4 + [s3] * 4,
            index, column, from_left_column, from_right_column,
        )
        devices = tiles_x * tiles_y
        blocks = jnp.broadcast_to(coarser[0][None], (devices, 4, LANES))
        gathered = lax.all_to_all(blocks, ("gx", "gy"), 0, 0).reshape(devices * 4, LANES)

        s4 = (NZ, 16 + 2 * tiles_x, LANES)
        (pressure,) = call(
            lambda *refs: top_kernel(grid, (tiles_x, tiles_y), *refs),
            "top",
            [array(NZ, 32, LANES)],
            [s4] * 10 + [s3] * 2 + [s2] * 2 + [s1] * 2 + [s0] * 4,
            index, gathered, *fine[1:], *coarser[1:],
        )
        return pressure

    return jax.shard_map(
        on_device,
        mesh=mesh,
        in_specs=(P(None, "gx", "gy"), P(None, "gx", "gy")),
        out_specs=P(None, "gx", "gy"),
        check_vma=False,
    )
```

```python
import jax
import jax.numpy as jnp
from jax import lax
from jax.experimental import pallas as pl
from jax.experimental.pallas import tpu as pltpu
from jax.sharding import PartitionSpec as P

NZ = 16
LANES = 128
SWEEPS = 6
VERTICAL = 0.015625
TINY = 2.0**-20
VMEM_BYTES = 24 * 1024 * 1024

ROW0 = (16, 8, 16, 8)
ROWS = (64, 32, 40, 24)
LANE0 = (0, 32, 16, 8)


def spacing(level):
    return 2.0 * 0.25**level


def lanes_of(shape=(8, LANES)):
    return lax.broadcasted_iota(jnp.int32, shape, 1)


def rows_of(shape=(8, LANES)):
    return lax.broadcasted_iota(jnp.int32, shape, 0)


def rcp(x):
    guess = pl.reciprocal(x, approx=True)
    return guess * (2.0 - x * guess)


def from_left(xs):
    rolled = [pltpu.roll(x, 1, 1) for x in xs]
    if len(xs) == 1:
        return rolled
    edge = lanes_of(xs[0].shape) == 0
    return [jnp.where(edge, rolled[1], rolled[0]), jnp.where(edge, rolled[0], rolled[1])]


def from_right(xs):
    rolled = [pltpu.roll(x, LANES - 1, 1) for x in xs]
    if len(xs) == 1:
        return rolled
    edge = lanes_of(xs[0].shape) == LANES - 1
    return [jnp.where(edge, rolled[1], rolled[0]), jnp.where(edge, rolled[0], rolled[1])]


def split_dot(x, matrix, pieces=2):
    total = None
    for piece in range(pieces):
        part = x.astype(jnp.bfloat16)
        product = jnp.dot(part, matrix, preferred_element_type=jnp.float32)
        total = product if total is None else total + product
        if piece + 1 < pieces:
            x = x - part.astype(jnp.float32)
    return total


def one_hot(rows, test, value, lanes=LANES):
    shape = (rows, lanes)
    source, target = lax.broadcasted_iota(jnp.int32, shape, 0), lax.broadcasted_iota(jnp.int32, shape, 1)
    return jnp.where(test(source, target), value, 0.0).astype(jnp.bfloat16)


def run_blocks(blocks, body):
    for block in blocks:
        if len(block) == 2:
            body(*block)
        else:
            first, height, count = block

            def step(index, carry):
                body(first + height * index, height)
                return carry

            lax.fori_loop(0, count, step, 0)


class Level:
    def __init__(self, level, rho, ax, ay, d, e, g):
        self.level, self.rho, self.ax, self.ay, self.d, self.e, self.g = level, rho, ax, ay, d, e, g
        self.parts = range(len(ax))

    def faces(self, blocks):
        scale = spacing(self.level)

        def body(r, h):
            for k in range(NZ):
                here = [ref[k, pl.ds(r, h), :] for ref in self.rho]
                above = [ref[k, pl.ds(r - 1, h), :] for ref in self.rho]
                left = from_left(here)
                for p in self.parts:
                    self.ax[p][k, pl.ds(r, h), :] = scale * rcp(jnp.maximum(here[p] + above[p], TINY))
                    self.ay[p][k, pl.ds(r, h), :] = scale * rcp(jnp.maximum(here[p] + left[p], TINY))

        run_blocks(blocks, body)

    def factor_and_first(self, blocks, inside, f, v):
        def body(r, h):
            masks = [inside(r, h, p) for p in self.parts]
            ratio = [None for p in self.parts]
            partial = [[] for p in self.parts]
            upper = [None for p in self.parts]
            rho = [ref[0, pl.ds(r, h), :] for ref in self.rho]
            for p in self.parts:
                upper[p] = (2.0 * VERTICAL) * rcp(jnp.maximum(rho[p], TINY))
            for k in range(NZ):
                if k + 1 < NZ:
                    below = [ref[k + 1, pl.ds(r, h), :] for ref in self.rho]
                    lower = [
                        (2.0 * VERTICAL) * rcp(jnp.maximum(rho[p] + below[p], TINY)) for p in self.parts
                    ]
                ay = [ref[k, pl.ds(r, h), :] for ref in self.ay]
                right = from_right(ay)
                for p in self.parts:
                    center = (
                        self.ax[p][k, pl.ds(r, h), :]
                        + self.ax[p][k, pl.ds(r + 1, h), :]
                        + ay[p]
                        + right[p]
                        + upper[p]
                    )
                    if k + 1 < NZ:
                        center = center + lower[p]
                    pivot = center if k == 0 else center - upper[p] * ratio[p]
                    inverse = jnp.where(masks[p], rcp(pivot), 0.0)
                    scaled = 0.8 * inverse
                    self.d[p][k, pl.ds(r, h), :] = scaled
                    value = scaled * f[p][k, pl.ds(r, h), :]
                    if k > 0:
                        weight = upper[p] * inverse
                        self.e[p][k, pl.ds(r, h), :] = weight
                        value = value + weight * partial[p][-1]
                    partial[p].append(value)
                    if k + 1 < NZ:
                        ratio[p] = lower[p] * inverse
                        self.g[p][k, pl.ds(r, h), :] = ratio[p]
                if k + 1 < NZ:
                    rho, upper = below, lower
            for p in self.parts:
                w = partial[p][-1]
                v[p][NZ - 1, pl.ds(r, h), :] = w
                for k in range(NZ - 2, -1, -1):
                    w = partial[p][k] + self.g[p][k, pl.ds(r, h), :] * w
                    v[p][k, pl.ds(r, h), :] = w

        run_blocks(blocks, body)

    def pull(self, v, k, r, h, wanted):
        here = [ref[k, pl.ds(r, h), :] for ref in v]
        ay = [ref[k, pl.ds(r, h), :] for ref in self.ay]
        left = from_left(here)
        right = from_right([a * x for a, x in zip(ay, here)])
        return [
            self.ax[p][k, pl.ds(r, h), :] * v[p][k, pl.ds(r - 1, h), :]
            + self.ax[p][k, pl.ds(r + 1, h), :] * v[p][k, pl.ds(r + 1, h), :]
            + ay[p] * left[p]
            + right[p]
            for p in wanted
        ]

    def relax(self, blocks, f, v, out, u=None, wanted=None, shift=0):
        wanted = self.parts if wanted is None else wanted

        def body(r, h):
            partial = [[] for p in wanted]
            for k in range(NZ):
                pulls = self.pull(v, k, r, h, wanted)
                for n, p in enumerate(wanted):
                    value = self.d[p][k, pl.ds(r, h), :] * (f[p][k, pl.ds(r, h), :] + pulls[n])
                    if k > 0:
                        value = value + self.e[p][k, pl.ds(r, h), :] * partial[n][-1]
                    partial[n].append(value)
            for n, p in enumerate(wanted):
                w = None
                for k in range(NZ - 1, -1, -1):
                    w = partial[n][k] if w is None else partial[n][k] + self.g[p][k, pl.ds(r, h), :] * w
                    old = v[p][k, pl.ds(r, h), :]
                    out[p][k, pl.ds(r - shift, h), :] = 0.2 * old + w
                    if u is not None:
                        u[p][k, pl.ds(r, h), :] = w - 0.6 * old

        run_blocks(blocks, body)

    def residual(self, blocks, f, u, out):
        def body(r, h):
            for k in range(NZ):
                pulls = self.pull(u, k, r, h, self.parts)
                for p in self.parts:
                    out[p][k, pl.ds(r, h), :] = 0.04 * f[p][k, pl.ds(r, h), :] + pulls[p]

        run_blocks(blocks, body)


def inside_of(level, ix, iy, shape):
    grid_rows, grid_lanes, tile_rows, tile_lanes = shape

    def inside(r, h, part):
        row, lane = rows_of((h, LANES)) + (r + ix * tile_rows - ROW0[level]), lanes_of((h, LANES))
        good = jnp.logical_and(row >= 0, row < grid_rows)
        if level == 0 and part == 0:
            return good
        if level == 0:
            right = jnp.logical_and(lane < 64, iy * tile_lanes + tile_lanes < grid_lanes)
            side = jnp.logical_or(right, jnp.logical_and(lane >= 64, iy > 0))
        else:
            column = iy * tile_lanes + lane - LANE0[level]
            side = jnp.logical_and(column >= 0, column < grid_lanes)
        return jnp.logical_and(good, side)

    return inside


def pair_rows(ref, k, start, count):
    layer = ref.at[k]
    return layer[pl.ds(start, count, stride=2), :] + layer[pl.ds(start + 1, count, stride=2), :]


def stack_rows(blocks):
    return jnp.concatenate(blocks, axis=0)


def edges_kernel(f_ref, rho_ref, up_ref, dn_ref, left_ref, right_ref):
    lane = lanes_of()
    slot = lane // 16
    for field, own in enumerate((f_ref, rho_ref)):
        for block in range(8):
            for half in range(2):
                lefts, rights = None, None
                for q in range(8):
                    k = half * 8 + q
                    if block < 2:
                        x = up_ref[field * NZ + k, pl.ds(block * 8, 8), :]
                    elif block < 6:
                        x = own[k, pl.ds(block * 8 - 16, 8), :]
                    else:
                        x = dn_ref[field * NZ + k, pl.ds(block * 8 - 48, 8), :]
                    a = x if q == 0 else pltpu.roll(x, 16 * q, 1)
                    b = pltpu.roll(x, 16 * q + 16, 1) if q < 7 else x
                    lefts = a if q == 0 else jnp.where(slot == q, a, lefts)
                    rights = b if q == 0 else jnp.where(slot == q, b, rights)
                left_ref[field * 2 + half, pl.ds(block * 8, 8), :] = lefts
                right_ref[field * 2 + half, pl.ds(block * 8, 8), :] = rights


def fine_kernel(
    grid, index_ref, f_ref, rho_ref, up_ref, dn_ref, from_left_ref, from_right_ref,
    pack_ref, fm, fh, vm, vh, axm, axh, aym, ayh, dm, dh, em, eh, gm, gh, f1, v1, ax1, ay1, d1, e1, g1,
    rm, rh, firstm, firsth, um, uh, rho1, first1, u1, res1,
):
    ix, iy = index_ref[0], index_ref[1]
    grid_rows, grid_lanes = grid
    inside = inside_of(0, ix, iy, (grid_rows, grid_lanes, 32, 128))

    unpack = one_hot(
        2 * LANES,
        lambda s, t: jnp.logical_or(
            jnp.logical_and(s < LANES, (t // LANES) * 16 == s - t % LANES) & (t % LANES < 16),
            jnp.logical_and(s >= LANES, (t // LANES) * 16 == s - t % LANES - 16) & (t % LANES >= 112),
        ),
        1.0,
        8 * LANES,
    )
    for field, (own, main, side) in enumerate(((f_ref, fm, fh), (rho_ref, rm, rh))):
        for k in range(NZ):
            for first, count, source, shift in (
                (0, 16, up_ref, 0),
                (16, 32, own, -16),
                (48, 16, dn_ref, -48),
            ):
                layer = k if source is own else field * NZ + k
                x = source[layer, pl.ds(first + shift, count), :]
                if field == 1 and source is not own:
                    x = jnp.where(inside(first, count, 0), x, 0.0)
                main[k, pl.ds(first, count), :] = x
        for half in range(2):
            strips = jnp.concatenate([from_right_ref[field * 2 + half], from_left_ref[field * 2 + half]], axis=1)
            wide = split_dot(strips, unpack, 3)
            for q in range(8):
                y = wide[:, q * LANES : (q + 1) * LANES]
                if field == 1:
                    y = jnp.where(inside(0, 64, 1), y, 0.0)
                side[half * 8 + q, :, :] = y

    fine = Level(0, [rm, rh], [axm, axh], [aym, ayh], [dm, dh], [em, eh], [gm, gh])
    fine.faces([(6, 16, 3), (51, 8)])
    fine.factor_and_first([(6, 16, 3), (50, 8)], inside, [fm, fh], [firstm, firsth])
    fine.relax([(7, 16, 3), (49, 8)], [fm, fh], [firstm, firsth], [vm, vh], u=[um, uh])
    fine.residual([(8, 16, 3)], [fm, fh], [um, uh], [firstm, firsth])

    main_matrix = one_hot(LANES, lambda s, t: s // 2 + 32 == t, 0.25)
    side_matrix = one_hot(
        LANES,
        lambda s, t: jnp.logical_or(
            jnp.logical_and(s < 64, s // 2 + 96 == t), jnp.logical_and(s >= 64, s // 2 - 32 == t)
        ),
        0.25,
    )
    for first in range(0, NZ, 4):
        ks = range(first, first + 4)
        total = split_dot(stack_rows([pair_rows(firstm, k, 8, 24) for k in ks]), main_matrix)
        total = total + split_dot(stack_rows([pair_rows(firsth, k, 8, 24) for k in ks]), side_matrix)
        for n, k in enumerate(ks):
            f1[k, pl.ds(4, 24), :] = total[n * 24 : (n + 1) * 24]
        total = split_dot(stack_rows([pair_rows(rm, k, 0, 32) for k in ks]), main_matrix)
        total = total + split_dot(stack_rows([pair_rows(rh, k, 0, 32) for k in ks]), side_matrix)
        for n, k in enumerate(ks):
            rho1[k, :, :] = total[n * 32 : (n + 1) * 32]

    middle = Level(1, [rho1], [ax1], [ay1], [d1], [e1], [g1])
    inside = inside_of(1, ix, iy, (grid_rows // 2, grid_lanes // 2, 16, 64))
    middle.faces([(4, 24), (21, 8)])
    middle.factor_and_first([(4, 24)], inside, [f1], [first1])
    middle.relax([(4, 24)], [f1], [first1], [v1], u=[u1])
    middle.residual([(8, 16)], [f1], [u1], [res1])

    pack_matrix = one_hot(
        4 * LANES,
        lambda s, t: jnp.logical_and(
            (s % LANES) // 2 - 16 + 32 * (s // LANES) == t,
            jnp.logical_and(s % LANES >= 32, s % LANES < 96),
        ),
        0.25,
    )
    blocks = []
    for ref in (res1, rho1):
        for group in range(4):
            blocks.append(jnp.concatenate([pair_rows(ref, 4 * group + q, 8, 8) for q in range(4)], axis=1))
    packed = split_dot(stack_rows(blocks), pack_matrix)
    for n in range(8):
        pack_ref[n, :, :] = packed[n * 8 : (n + 1) * 8]


def coarser_kernel(
    grid, index_ref, own_ref, from_left_ref, from_right_ref,
    pack_ref, f2, v2, ax2, ay2, d2, e2, g2, f3, v3, ax3, ay3, d3, e3, g3,
    rho2, first2, u2, res2, rho3, first3, u3, res3,
):
    ix, iy = index_ref[0], index_ref[1]
    grid_rows, grid_lanes = grid
    lane = lanes_of()
    inside = inside_of(2, ix, iy, (grid_rows // 4, grid_lanes // 4, 8, 32))

    unpack = [
        one_hot(
            LANES,
            lambda s, t: jnp.logical_and(t % LANES < 64, (t % LANES + 64 * (t // LANES) + odd * 32) % LANES == s),
            1.0,
            2 * LANES,
        )
        for odd in range(2)
    ]
    good = inside(0, 40, 0)
    for field, target in enumerate((f2, rho2)):
        for group in range(4):
            own = pltpu.roll(own_ref[field * 4 + group], 16, 1)
            left = pltpu.roll(from_left_ref[field * 4 + group], LANES - 16, 1)
            right = pltpu.roll(from_right_ref[field * 4 + group], 48, 1)
            for odd in range(2):
                place = (lanes_of((40, LANES)) + 32 * odd) % 64
                merged = jnp.where(place < 16, left, jnp.where(place < 48, own, right))
                wide = split_dot(merged, unpack[odd], 3)
                for n in range(2):
                    y = wide[:, n * LANES : (n + 1) * LANES]
                    if field == 1:
                        y = jnp.where(good, y, 0.0)
                    target[4 * group + 2 * n + odd, :, :] = y

    level2 = Level(2, [rho2], [ax2], [ay2], [d2], [e2], [g2])
    level2.faces([(4, 16, 2), (29, 8)])
    level2.factor_and_first([(4, 16, 2)], inside, [f2], [first2])
    level2.relax([(4, 16, 2)], [f2], [first2], [v2], u=[u2])
    level2.residual([(4, 16, 2)], [f2], [u2], [res2])

    halve = one_hot(LANES, lambda s, t: s // 2 == t, 0.25)
    for ref, target, first, count in ((res2, f3, 4, 16), (rho2, rho3, 4, 16)):
        total = split_dot(stack_rows([pair_rows(ref, k, first, count) for k in range(NZ)]), halve)
        for k in range(NZ):
            target[k, pl.ds(first // 2, count), :] = total[k * count : (k + 1) * count]

    level3 = Level(3, [rho3], [ax3], [ay3], [d3], [e3], [g3])
    inside = inside_of(3, ix, iy, (grid_rows // 8, grid_lanes // 8, 4, 16))
    level3.faces([(2, 16)])
    level3.factor_and_first([(2, 16)], inside, [f3], [first3])
    level3.relax([(2, 16)], [f3], [first3], [v3], u=[u3])
    level3.residual([(6, 8)], [f3], [u3], [res3])

    spread = one_hot(
        LANES,
        lambda s, t: jnp.logical_and(s // 2 - 4 == t % 8, jnp.logical_and(s >= 8, s < 24)),
        0.25,
    )
    for field, ref in enumerate((res3, rho3)):
        total = split_dot(stack_rows([pair_rows(ref, k, 8, 8) for k in range(NZ)]), spread)
        merged = total[0:8]
        for k in range(1, NZ):
            merged = jnp.where(lane // 8 == k, total[k * 8 : (k + 1) * 8], merged)
        pack_ref[pl.ds(2 * field, 2), :] = merged[0:2]


def prolong(coarse, first_row, count, ref, old, target, target_row, matrix):
    rows = stack_rows([coarse(k) for k in range(NZ)])
    for part in range(len(target)):
        fine = split_dot(rows, matrix[part])
        for k in range(NZ):
            x = fine[k * count : (k + 1) * count]
            for odd in range(2):
                where = pl.ds(target_row + odd, count, stride=2)
                target[part].at[k][where, :] = old[part].at[k][where, :] + x


def top_kernel(
    grid, tiles, index_ref, gathered, fm, fh, vm, vh, axm, axh, aym, ayh, dm, dh, em, eh, gm, gh,
    f1, v1, ax1, ay1, d1, e1, g1, f2, v2, ax2, ay2, d2, e2, g2, f3, v3, ax3, ay3, d3, e3, g3,
    out_ref,
    rho4, f4, ax4, ay4, d4, e4, g4, c4, a4, va4, vb4, va3, vb3, va2, vb2, va1, vb1, vam, vah, vbm, vbh,
):
    ix, iy = index_ref[0], index_ref[1]
    grid_rows, grid_lanes = grid
    lane = lanes_of()
    rows4 = grid_rows // 16
    tiles_x, tiles_y = tiles

    zero = jnp.zeros((8, LANES), jnp.float32)
    for ref in (rho4, va4, vb4):
        for k in range(NZ):
            ref[k, pl.ds(0, 8), :] = zero
            ref[k, pl.ds(8 + rows4, 8), :] = zero

    count = min(8, tiles_x)
    for field, target in enumerate((f4, rho4)):
        for r in range(2):
            for base in range(0, tiles_x, count):
                xs = [
                    gathered[pl.ds((base * tiles_y + t) * 4 + field * 2 + r, count, stride=4 * tiles_y), :]
                    for t in range(16)
                ]
                column = lax.broadcasted_iota(jnp.int32, (count, LANES), 1) // 8
                for bit in (1, 2, 4, 8):
                    high = (column & bit) != 0
                    for i in range(16):
                        if i & bit:
                            continue
                        a, b = xs[i], xs[i | bit]
                        xs[i] = jnp.where(high, pltpu.roll(b, 8 * bit, 1), a)
                        xs[i | bit] = jnp.where(high, b, pltpu.roll(a, LANES - 8 * bit, 1))
                for k in range(NZ):
                    target.at[k][pl.ds(8 + 2 * base + r, count, stride=2), :] = xs[k]

    scale = spacing(4)
    h = min(16, rows4)
    first_lane, last_lane = lanes_of((h, LANES)) == 0, lanes_of((h, LANES)) == LANES - 1
    starts = list(range(8, 8 + rows4, h))

    def faces_x(r, h):
        for k in range(NZ):
            total = rho4[k, pl.ds(r, h), :] + rho4[k, pl.ds(r - 1, h), :]
            ax4[k, pl.ds(r, h), :] = scale * rcp(jnp.maximum(total, TINY))

    for r in starts:
        faces_x(r, h)
    faces_x(rows4 + 1, 8)

    def first_sweep(r):
        rho = rho4[0, pl.ds(r, h), :]
        upper = (2.0 * VERTICAL) * rcp(rho)
        partial, ratio = [], None
        for k in range(NZ):
            here = rho4[k, pl.ds(r, h), :]
            left = jnp.where(first_lane, 0.0, pltpu.roll(here, 1, 1))
            ay = scale * rcp(here + left)
            right = jnp.where(last_lane, scale * rcp(here), pltpu.roll(ay, LANES - 1, 1))
            ay4[k, pl.ds(r, h), :] = jnp.where(first_lane, 0.0, ay)
            center = ax4[k, pl.ds(r, h), :] + ax4[k, pl.ds(r + 1, h), :] + ay + right + upper
            if k + 1 < NZ:
                lower = (2.0 * VERTICAL) * rcp(here + rho4[k + 1, pl.ds(r, h), :])
                center = center + lower
            c4[k, pl.ds(r, h), :] = center
            a4[k, pl.ds(r, h), :] = upper
            pivot = center if k == 0 else center - upper * ratio
            inverse = rcp(pivot)
            scaled = 0.8 * inverse
            d4[k, pl.ds(r, h), :] = scaled
            value = scaled * f4[k, pl.ds(r, h), :]
            if k > 0:
                weight = upper * inverse
                e4[k, pl.ds(r, h), :] = weight
                value = value + weight * partial[-1]
            partial.append(value)
            if k + 1 < NZ:
                ratio = lower * inverse
                g4[k, pl.ds(r, h), :] = ratio
                upper = lower
        w = partial[-1]
        va4[NZ - 1, pl.ds(r, h), :] = w
        for k in range(NZ - 2, -1, -1):
            w = partial[k] + g4[k, pl.ds(r, h), :] * w
            va4[k, pl.ds(r, h), :] = w

    for r in starts:
        first_sweep(r)

    def pulled4(v, k, r):
        here = v[k, pl.ds(r, h), :]
        ay = ay4[k, pl.ds(r, h), :]
        return (
            f4[k, pl.ds(r, h), :]
            + ax4[k, pl.ds(r, h), :] * v[k, pl.ds(r - 1, h), :]
            + ax4[k, pl.ds(r + 1, h), :] * v[k, pl.ds(r + 1, h), :]
            + ay * pltpu.roll(here, 1, 1)
            + pltpu.roll(ay * here, LANES - 1, 1)
        )

    def sweep(v, out):
        for r in starts:
            partial = []
            for k in range(NZ):
                value = d4[k, pl.ds(r, h), :] * pulled4(v, k, r)
                if k > 0:
                    value = value + e4[k, pl.ds(r, h), :] * partial[-1]
                partial.append(value)
            w = None
            for k in range(NZ - 1, -1, -1):
                w = partial[k] if w is None else partial[k] + g4[k, pl.ds(r, h), :] * w
                out[k, pl.ds(r, h), :] = 0.2 * v[k, pl.ds(r, h), :] + w

    ends = [va4, vb4]
    for number in range(SWEEPS - 1):
        sweep(ends[number % 2], ends[(number + 1) % 2])
    final = ends[(SWEEPS - 1) % 2]
    shifts = []
    for k in range(NZ):
        left_over, weights = None, None
        for r in starts:
            center = c4[k, pl.ds(r, h), :]
            part = pulled4(final, k, r) - center * final[k, pl.ds(r, h), :]
            if k > 0:
                part = part + a4[k, pl.ds(r, h), :] * final[k - 1, pl.ds(r, h), :]
            if k + 1 < NZ:
                part = part + a4[k + 1, pl.ds(r, h), :] * final[k + 1, pl.ds(r, h), :]
            left_over = part if left_over is None else left_over + part
            weights = center if weights is None else weights + center
        raised = jnp.sum(left_over, axis=(0, 1), keepdims=True)
        shifts.append(raised / jnp.sum(weights, axis=(0, 1), keepdims=True))

    row = rows_of() + (ix * 2 - 4)
    column = lane + (iy * 8 - 4)
    good = jnp.logical_and(
        jnp.logical_and(row >= 0, row < rows4),
        jnp.logical_and(jnp.logical_and(column >= 0, column < grid_lanes // 16), lane < 16),
    )
    amount = lax.rem(132 - iy * 8, LANES)

    def coarsest(k):
        x = final[k, pl.ds(4 + 2 * ix, 8), :] + shifts[k]
        return jnp.where(good, pltpu.roll(x, amount, 1), 0.0)

    repeat = one_hot(LANES, lambda s, t: s == t // 2, 1.0)
    prolong(coarsest, 0, 8, None, [v3], [va3], 0, [repeat])
    level3 = Level(3, None, [ax3], [ay3], [d3], [e3], [g3])
    level3.relax([(2, 16)], [f3], [va3], [vb3])
    level3.relax([(6, 8)], [f3], [vb3], [va3])

    prolong(lambda k: va3[k, pl.ds(6, 8), :], 0, 8, None, [v2], [va2], 12, [repeat])
    level2 = Level(2, None, [ax2], [ay2], [d2], [e2], [g2])
    level2.relax([(12, 16)], [f2], [va2], [vb2])
    level2.relax([(12, 16)], [f2], [vb2], [va2])

    prolong(lambda k: va2[k, pl.ds(12, 16), :], 0, 16, None, [v1], [va1], 0, [repeat])
    level1 = Level(1, None, [ax1], [ay1], [d1], [e1], [g1])
    level1.relax([(4, 24)], [f1], [va1], [vb1])
    level1.relax([(4, 24)], [f1], [vb1], [va1])

    to_main = one_hot(LANES, lambda s, t: s == t // 2 + 32, 1.0)
    to_side = one_hot(
        LANES,
        lambda s, t: jnp.logical_or(
            jnp.logical_and(t < 64, s == t // 2 + 96), jnp.logical_and(t >= 64, s == t // 2 - 32)
        ),
        1.0,
    )
    prolong(lambda k: va1[k, pl.ds(4, 24), :], 0, 24, None, [vm, vh], [vam, vah], 8, [to_main, to_side])
    fine = Level(0, None, [axm, axh], [aym, ayh], [dm, dh], [em, eh], [gm, gh])
    fine.relax([(15, 16, 2), (41, 8)], [fm, fh], [vam, vah], [vbm, vbh])
    fine.relax([(16, 16, 2)], [fm, fh], [vbm, vbh], [out_ref], wanted=[0], shift=16)


def ring(x, axis, step):
    size = lax.axis_size(axis)
    return lax.ppermute(x, axis, [(i, (i + step) % size) for i in range(size)])


def gather(x, axis):
    size = lax.axis_size(axis)
    blocks = jnp.broadcast_to(x[None], (size,) + x.shape)
    return lax.all_to_all(blocks, axis, 0, 0).reshape(size * x.shape[0], LANES)


def array(*shape):
    return jax.ShapeDtypeStruct(shape, jnp.float32)


def call(kernel, name, outs, scratch, index, *operands):
    vmem = pl.BlockSpec(memory_space=pltpu.VMEM)
    ins = [vmem] * len(operands)
    if index is not None:
        ins, operands = [pl.BlockSpec(memory_space=pltpu.SMEM)] + ins, (index,) + operands
    return pl.pallas_call(
        kernel,
        out_shape=outs,
        in_specs=ins,
        out_specs=[vmem] * len(outs),
        scratch_shapes=[pltpu.VMEM(shape, jnp.float32) for shape in scratch],
        compiler_params=pltpu.CompilerParams(vmem_limit_bytes=VMEM_BYTES),
        name=name,
    )(*operands)


def solution(mesh):
    tiles_x, tiles_y = mesh.shape["gx"], mesh.shape["gy"]
    grid = (32 * tiles_x, 128 * tiles_y)
    big = [array(NZ, ROWS[level], LANES) for level in range(4)]

    def on_device(source, rho):
        index = jnp.stack([lax.axis_index("gx"), lax.axis_index("gy")]).astype(jnp.int32)

        lows = jnp.concatenate([source[:, :16], rho[:, :16]], axis=0)
        highs = jnp.concatenate([source[:, 16:], rho[:, 16:]], axis=0)
        up = ring(highs, "gx", 1)
        dn = ring(lows, "gx", -1)
        strip = array(4, ROWS[0], LANES)
        lefts, rights = call(edges_kernel, "edges", [strip, strip], [], None, source, rho, up, dn)
        from_left_strip = ring(rights, "gy", 1)
        from_right_strip = ring(lefts, "gy", -1)

        s0, s1, s2, s3 = [x.shape for x in big]
        fine = call(
            lambda *refs: fine_kernel(grid, *refs),
            "fine",
            [array(8, 8, LANES)] + [big[0]] * 14 + [big[1]] * 7,
            [s0] * 6 + [s1] * 4,
            index, source, rho, up, dn, from_left_strip, from_right_strip,
        )
        tile = fine[0]
        pieces = [ring(tile, "gx", 2), ring(tile, "gx", 1), tile, ring(tile, "gx", -1), ring(tile, "gx", -2)]
        column = jnp.concatenate(pieces, axis=1)
        from_left_column = ring(column, "gy", 1)
        from_right_column = ring(column, "gy", -1)
        coarser = call(
            lambda *refs: coarser_kernel(grid, *refs),
            "coarser",
            [array(4, LANES)] + [big[2]] * 7 + [big[3]] * 7,
            [s2] * 4 + [s3] * 4,
            index, column, from_left_column, from_right_column,
        )
        gathered = gather(gather(coarser[0], "gy"), "gx")

        s4 = (NZ, 16 + 2 * tiles_x, LANES)
        (pressure,) = call(
            lambda *refs: top_kernel(grid, (tiles_x, tiles_y), *refs),
            "top",
            [array(NZ, 32, LANES)],
            [s4] * 11 + [s3] * 2 + [s2] * 2 + [s1] * 2 + [s0] * 4,
            index, gathered, *fine[1:], *coarser[1:],
        )
        return pressure

    return jax.shard_map(
        on_device,
        mesh=mesh,
        in_specs=(P(None, "gx", "gy"), P(None, "gx", "gy")),
        out_specs=P(None, "gx", "gy"),
        check_vma=False,
    )
```

```python
import jax
import jax.numpy as jnp
from jax import lax
from jax.experimental import pallas as pl
from jax.experimental.pallas import tpu as pltpu
from jax.sharding import PartitionSpec as P

NZ = 16
LANES = 128
SWEEPS = 6
VERTICAL = 0.015625
TINY = 2.0**-20
VMEM_BYTES = 24 * 1024 * 1024

ROW0 = (16, 8, 16, 8)
ROWS = (64, 32, 40, 24)
LANE0 = (0, 32, 16, 8)


def spacing(level):
    return 2.0 * 0.25**level


def lanes_of(shape=(8, LANES)):
    return lax.broadcasted_iota(jnp.int32, shape, 1)


def rows_of(shape=(8, LANES)):
    return lax.broadcasted_iota(jnp.int32, shape, 0)


def rcp(x):
    guess = pl.reciprocal(x, approx=True)
    return guess * (2.0 - x * guess)


def from_left(xs):
    rolled = [pltpu.roll(x, 1, 1) for x in xs]
    if len(xs) == 1:
        return rolled
    edge = lanes_of(xs[0].shape) == 0
    return [jnp.where(edge, rolled[1], rolled[0]), jnp.where(edge, rolled[0], rolled[1])]


def from_right(xs):
    rolled = [pltpu.roll(x, LANES - 1, 1) for x in xs]
    if len(xs) == 1:
        return rolled
    edge = lanes_of(xs[0].shape) == LANES - 1
    return [jnp.where(edge, rolled[1], rolled[0]), jnp.where(edge, rolled[0], rolled[1])]


def split_dot(x, matrix, pieces=2):
    total = None
    for piece in range(pieces):
        part = x.astype(jnp.bfloat16)
        product = jnp.dot(part, matrix, preferred_element_type=jnp.float32)
        total = product if total is None else total + product
        if piece + 1 < pieces:
            x = x - part.astype(jnp.float32)
    return total


def one_hot(rows, test, value, lanes=LANES):
    shape = (rows, lanes)
    source, target = lax.broadcasted_iota(jnp.int32, shape, 0), lax.broadcasted_iota(jnp.int32, shape, 1)
    return jnp.where(test(source, target), value, 0.0).astype(jnp.bfloat16)


def run_blocks(blocks, body):
    for block in blocks:
        if len(block) == 2:
            body(*block)
        else:
            first, height, count = block

            def step(index, carry):
                body(first + height * index, height)
                return carry

            lax.fori_loop(0, count, step, 0)


class Level:
    def __init__(self, level, rho, ax, ay, d, e, g):
        self.level, self.rho, self.ax, self.ay, self.d, self.e, self.g = level, rho, ax, ay, d, e, g
        self.parts = range(len(ax))

    def faces(self, blocks):
        scale = spacing(self.level)

        def body(r, h):
            for k in range(NZ):
                here = [ref[k, pl.ds(r, h), :] for ref in self.rho]
                above = [ref[k, pl.ds(r - 1, h), :] for ref in self.rho]
                left = from_left(here)
                for p in self.parts:
                    self.ax[p][k, pl.ds(r, h), :] = scale * rcp(jnp.maximum(here[p] + above[p], TINY))
                    self.ay[p][k, pl.ds(r, h), :] = scale * rcp(jnp.maximum(here[p] + left[p], TINY))

        run_blocks(blocks, body)

    def factor_and_first(self, blocks, inside, f, v):
        def body(r, h):
            masks = [inside(r, h, p) for p in self.parts]
            ratio = [None for p in self.parts]
            partial = [[] for p in self.parts]
            upper = [None for p in self.parts]
            rho = [ref[0, pl.ds(r, h), :] for ref in self.rho]
            for p in self.parts:
                upper[p] = (2.0 * VERTICAL) * rcp(jnp.maximum(rho[p], TINY))
            for k in range(NZ):
                if k + 1 < NZ:
                    below = [ref[k + 1, pl.ds(r, h), :] for ref in self.rho]
                    lower = [
                        (2.0 * VERTICAL) * rcp(jnp.maximum(rho[p] + below[p], TINY)) for p in self.parts
                    ]
                ay = [ref[k, pl.ds(r, h), :] for ref in self.ay]
                right = from_right(ay)
                for p in self.parts:
                    center = (
                        self.ax[p][k, pl.ds(r, h), :]
                        + self.ax[p][k, pl.ds(r + 1, h), :]
                        + ay[p]
                        + right[p]
                        + upper[p]
                    )
                    if k + 1 < NZ:
                        center = center + lower[p]
                    pivot = center if k == 0 else center - upper[p] * ratio[p]
                    inverse = jnp.where(masks[p], rcp(pivot), 0.0)
                    scaled = 0.8 * inverse
                    self.d[p][k, pl.ds(r, h), :] = scaled
                    value = scaled * f[p][k, pl.ds(r, h), :]
                    if k > 0:
                        weight = upper[p] * inverse
                        self.e[p][k, pl.ds(r, h), :] = weight
                        value = value + weight * partial[p][-1]
                    partial[p].append(value)
                    if k + 1 < NZ:
                        ratio[p] = lower[p] * inverse
                        self.g[p][k, pl.ds(r, h), :] = ratio[p]
                if k + 1 < NZ:
                    rho, upper = below, lower
            for p in self.parts:
                w = partial[p][-1]
                v[p][NZ - 1, pl.ds(r, h), :] = w
                for k in range(NZ - 2, -1, -1):
                    w = partial[p][k] + self.g[p][k, pl.ds(r, h), :] * w
                    v[p][k, pl.ds(r, h), :] = w

        run_blocks(blocks, body)

    def pull(self, v, k, r, h, wanted):
        here = [ref[k, pl.ds(r, h), :] for ref in v]
        ay = [ref[k, pl.ds(r, h), :] for ref in self.ay]
        left = from_left(here)
        right = from_right([a * x for a, x in zip(ay, here)])
        return [
            self.ax[p][k, pl.ds(r, h), :] * v[p][k, pl.ds(r - 1, h), :]
            + self.ax[p][k, pl.ds(r + 1, h), :] * v[p][k, pl.ds(r + 1, h), :]
            + ay[p] * left[p]
            + right[p]
            for p in wanted
        ]

    def relax(self, blocks, f, v, out, u=None, wanted=None, shift=0):
        wanted = self.parts if wanted is None else wanted

        def body(r, h):
            partial = [[] for p in wanted]
            for k in range(NZ):
                pulls = self.pull(v, k, r, h, wanted)
                for n, p in enumerate(wanted):
                    value = self.d[p][k, pl.ds(r, h), :] * (f[p][k, pl.ds(r, h), :] + pulls[n])
                    if k > 0:
                        value = value + self.e[p][k, pl.ds(r, h), :] * partial[n][-1]
                    partial[n].append(value)
            for n, p in enumerate(wanted):
                w = None
                for k in range(NZ - 1, -1, -1):
                    w = partial[n][k] if w is None else partial[n][k] + self.g[p][k, pl.ds(r, h), :] * w
                    old = v[p][k, pl.ds(r, h), :]
                    out[p][k, pl.ds(r - shift, h), :] = 0.2 * old + w
                    if u is not None:
                        u[p][k, pl.ds(r, h), :] = w - 0.6 * old

        run_blocks(blocks, body)

    def residual(self, blocks, f, u, out):
        def body(r, h):
            for k in range(NZ):
                pulls = self.pull(u, k, r, h, self.parts)
                for p in self.parts:
                    out[p][k, pl.ds(r, h), :] = 0.04 * f[p][k, pl.ds(r, h), :] + pulls[p]

        run_blocks(blocks, body)


def inside_of(level, ix, iy, shape):
    grid_rows, grid_lanes, tile_rows, tile_lanes = shape

    def inside(r, h, part):
        row, lane = rows_of((h, LANES)) + (r + ix * tile_rows - ROW0[level]), lanes_of((h, LANES))
        good = jnp.logical_and(row >= 0, row < grid_rows)
        if level == 0 and part == 0:
            return good
        if level == 0:
            right = jnp.logical_and(lane < 64, iy * tile_lanes + tile_lanes < grid_lanes)
            side = jnp.logical_or(right, jnp.logical_and(lane >= 64, iy > 0))
        else:
            column = iy * tile_lanes + lane - LANE0[level]
            side = jnp.logical_and(column >= 0, column < grid_lanes)
        return jnp.logical_and(good, side)

    return inside


def pair_rows(ref, k, start, count):
    layer = ref.at[k]
    return layer[pl.ds(start, count, stride=2), :] + layer[pl.ds(start + 1, count, stride=2), :]


def stack_rows(blocks):
    return jnp.concatenate(blocks, axis=0)


PIECES = ((5, 8, "up", 0), (8, 8, "up", 3), (16, 32, "own", 0), (48, 8, "down", 0), (51, 8, "down", 3))
REACH = 11


def piece_of(piece, field, k, own, up, down):
    first, count, source, start = piece
    if source == "own":
        return own[k, :, :]
    ref = up if source == "up" else down
    return ref[pl.ds(start * 2 * NZ + field * NZ + k, count, stride=2 * NZ), :]


def edges_kernel(f_ref, rho_ref, up_ref, dn_ref, left_ref, right_ref):
    for field, own in enumerate((f_ref, rho_ref)):
        for piece in PIECES:
            first, count = piece[:2]
            slot = lanes_of((count, LANES)) // 16
            for half in range(2):
                lefts, rights = None, None
                for q in range(8):
                    x = piece_of(piece, field, half * 8 + q, own, up_ref, dn_ref)
                    a = x if q == 0 else pltpu.roll(x, 16 * q, 1)
                    b = pltpu.roll(x, 16 * q + 16, 1) if q < 7 else x
                    lefts = a if q == 0 else jnp.where(slot == q, a, lefts)
                    rights = b if q == 0 else jnp.where(slot == q, b, rights)
                left_ref[field * 2 + half, pl.ds(first, count), :] = lefts
                right_ref[field * 2 + half, pl.ds(first, count), :] = rights


def fine_kernel(
    grid, index_ref, f_ref, rho_ref, up_ref, dn_ref, from_left_ref, from_right_ref,
    pack_ref, fm, fh, vm, vh, axm, axh, aym, ayh, dm, dh, em, eh, gm, gh, f1, v1, ax1, ay1, d1, e1, g1,
    rm, rh, firstm, firsth, um, uh, rho1, first1, u1, res1,
):
    ix, iy = index_ref[0], index_ref[1]
    grid_rows, grid_lanes = grid
    inside = inside_of(0, ix, iy, (grid_rows, grid_lanes, 32, 128))

    for field, (own, main, side) in enumerate(((f_ref, fm, fh), (rho_ref, rm, rh))):
        for k in range(NZ):
            for piece in PIECES:
                first, count, source, _ = piece
                x = piece_of(piece, field, k, own, up_ref, dn_ref)
                if field == 1 and source != "own":
                    x = jnp.where(inside(first, count, 0), x, 0.0)
                main[k, pl.ds(first, count), :] = x
        for first in (5, 16, 32, 43):
            slot = lanes_of((16, LANES)) // 16
            good = inside(first, 16, 1)
            for half in range(2):
                right = from_right_ref[field * 2 + half, pl.ds(first, 16), :]
                left = pltpu.roll(from_left_ref[field * 2 + half, pl.ds(first, 16), :], LANES - 16, 1)
                merged = [jnp.where(slot % 2 == odd, right, left) for odd in range(2)]
                for q in range(8):
                    y = merged[q % 2]
                    y = y if q == 0 else pltpu.roll(y, LANES - 16 * q, 1)
                    if field == 1:
                        y = jnp.where(good, y, 0.0)
                    side[half * 8 + q, pl.ds(first, 16), :] = y

    fine = Level(0, [rm, rh], [axm, axh], [aym, ayh], [dm, dh], [em, eh], [gm, gh])
    fine.faces([(6, 16, 3), (51, 8)])
    fine.factor_and_first([(6, 16, 3), (50, 8)], inside, [fm, fh], [firstm, firsth])
    fine.relax([(7, 16, 3), (49, 8)], [fm, fh], [firstm, firsth], [vm, vh], u=[um, uh])
    fine.residual([(8, 16, 3)], [fm, fh], [um, uh], [firstm, firsth])

    main_matrix = one_hot(LANES, lambda s, t: s // 2 + 32 == t, 0.25)
    side_matrix = one_hot(
        LANES,
        lambda s, t: jnp.logical_or(
            jnp.logical_and(s < 64, s // 2 + 96 == t), jnp.logical_and(s >= 64, s // 2 - 32 == t)
        ),
        0.25,
    )
    for first in range(0, NZ, 4):
        ks = range(first, first + 4)
        total = split_dot(stack_rows([pair_rows(firstm, k, 8, 24) for k in ks]), main_matrix)
        total = total + split_dot(stack_rows([pair_rows(firsth, k, 8, 24) for k in ks]), side_matrix)
        for n, k in enumerate(ks):
            f1[k, pl.ds(4, 24), :] = total[n * 24 : (n + 1) * 24]
        total = split_dot(stack_rows([pair_rows(rm, k, 0, 32) for k in ks]), main_matrix)
        total = total + split_dot(stack_rows([pair_rows(rh, k, 0, 32) for k in ks]), side_matrix)
        for n, k in enumerate(ks):
            rho1[k, :, :] = total[n * 32 : (n + 1) * 32]

    middle = Level(1, [rho1], [ax1], [ay1], [d1], [e1], [g1])
    inside = inside_of(1, ix, iy, (grid_rows // 2, grid_lanes // 2, 16, 64))
    middle.faces([(4, 24), (21, 8)])
    middle.factor_and_first([(4, 24)], inside, [f1], [first1])
    middle.relax([(4, 24)], [f1], [first1], [v1], u=[u1])
    middle.residual([(8, 16)], [f1], [u1], [res1])

    pack_matrix = one_hot(
        LANES,
        lambda s, t: jnp.logical_and(
            s // 2 - 16 == (t // LANES) * 16 + t % 16, jnp.logical_and(s >= 32, s < 96)
        ),
        0.25,
        2 * LANES,
    )
    slot = lanes_of() // 16
    for field, ref in enumerate((res1, rho1)):
        wide = split_dot(stack_rows([pair_rows(ref, k, 8, 8) for k in range(NZ)]), pack_matrix)
        for side in range(2):
            for half in range(2):
                packed = None
                for q in range(8):
                    k = half * 8 + q
                    x = wide[k * 8 : (k + 1) * 8, side * LANES : (side + 1) * LANES]
                    packed = x if q == 0 else jnp.where(slot == q, x, packed)
                pack_ref[side * 4 + field * 2 + half, :, :] = packed


def coarser_kernel(
    grid, index_ref, own_left_ref, own_right_ref, from_left_ref, from_right_ref,
    pack_ref, f2, v2, ax2, ay2, d2, e2, g2, f3, v3, ax3, ay3, d3, e3, g3,
    rho2, first2, u2, res2, rho3, first3, u3, res3,
):
    ix, iy = index_ref[0], index_ref[1]
    grid_rows, grid_lanes = grid
    lane = lanes_of()
    inside = inside_of(2, ix, iy, (grid_rows // 4, grid_lanes // 4, 8, 32))

    lane40 = lanes_of((40, LANES))
    good = inside(0, 40, 0)
    for field, target in enumerate((f2, rho2)):
        for half in range(2):
            g = field * 2 + half
            tiles = [
                from_left_ref[g],
                pltpu.roll(own_left_ref[g], 16, 1),
                pltpu.roll(own_right_ref[g], 32, 1),
                pltpu.roll(from_right_ref[g], 48, 1),
            ]
            for m in range(4):
                place = (lane40 - 16 * m) % 64
                merged = jnp.where(
                    place < 32,
                    jnp.where(place < 16, tiles[0], tiles[1]),
                    jnp.where(place < 48, tiles[2], tiles[3]),
                )
                for q in (m, m + 4):
                    y = merged if q == 0 else pltpu.roll(merged, LANES - 16 * q, 1)
                    if field == 1:
                        y = jnp.where(good, y, 0.0)
                    target[half * 8 + q, :, :] = y

    level2 = Level(2, [rho2], [ax2], [ay2], [d2], [e2], [g2])
    level2.faces([(4, 16, 2), (29, 8)])
    level2.factor_and_first([(4, 16, 2)], inside, [f2], [first2])
    level2.relax([(4, 16, 2)], [f2], [first2], [v2], u=[u2])
    level2.residual([(4, 16, 2)], [f2], [u2], [res2])

    halve = one_hot(LANES, lambda s, t: s // 2 == t, 0.25)
    for ref, target, first, count in ((res2, f3, 4, 16), (rho2, rho3, 4, 16)):
        total = split_dot(stack_rows([pair_rows(ref, k, first, count) for k in range(NZ)]), halve)
        for k in range(NZ):
            target[k, pl.ds(first // 2, count), :] = total[k * count : (k + 1) * count]

    level3 = Level(3, [rho3], [ax3], [ay3], [d3], [e3], [g3])
    inside = inside_of(3, ix, iy, (grid_rows // 8, grid_lanes // 8, 4, 16))
    level3.faces([(2, 16)])
    level3.factor_and_first([(2, 16)], inside, [f3], [first3])
    level3.relax([(2, 16)], [f3], [first3], [v3], u=[u3])
    level3.residual([(6, 8)], [f3], [u3], [res3])

    spread = one_hot(
        LANES,
        lambda s, t: jnp.logical_and(s // 2 - 4 == t % 8, jnp.logical_and(s >= 8, s < 24)),
        0.25,
    )
    for field, ref in enumerate((res3, rho3)):
        total = split_dot(stack_rows([pair_rows(ref, k, 8, 8) for k in range(NZ)]), spread)
        merged = total[0:8]
        for k in range(1, NZ):
            merged = jnp.where(lane // 8 == k, total[k * 8 : (k + 1) * 8], merged)
        pack_ref[pl.ds(2 * field, 2), :] = pltpu.roll(merged, 8 * iy, 1)[0:2]


def prolong(coarse, first_row, count, ref, old, target, target_row, matrix):
    rows = stack_rows([coarse(k) for k in range(NZ)])
    for part in range(len(target)):
        fine = split_dot(rows, matrix[part])
        for k in range(NZ):
            x = fine[k * count : (k + 1) * count]
            for odd in range(2):
                where = pl.ds(target_row + odd, count, stride=2)
                target[part].at[k][where, :] = old[part].at[k][where, :] + x


def top_kernel(
    grid, tiles, index_ref, gathered, fm, fh, vm, vh, axm, axh, aym, ayh, dm, dh, em, eh, gm, gh,
    f1, v1, ax1, ay1, d1, e1, g1, f2, v2, ax2, ay2, d2, e2, g2, f3, v3, ax3, ay3, d3, e3, g3,
    out_ref,
    rho4, f4, ax4, ay4, d4, e4, g4, c4, a4, va4, vb4, va3, vb3, va2, vb2, va1, vb1, vam, vah, vbm, vbh,
):
    ix, iy = index_ref[0], index_ref[1]
    grid_rows, grid_lanes = grid
    lane = lanes_of()
    rows4 = grid_rows // 16
    tiles_x, tiles_y = tiles

    zero = jnp.zeros((8, LANES), jnp.float32)
    for ref in (rho4, va4, vb4):
        for k in range(NZ):
            ref[k, pl.ds(0, 8), :] = zero
            ref[k, pl.ds(8 + rows4, 8), :] = zero

    count = min(8, tiles_x)
    for field, target in enumerate((f4, rho4)):
        for r in range(2):
            for base in range(0, tiles_x, count):
                xs = [
                    gathered[pl.ds((base * tiles_y + t) * 4 + field * 2 + r, count, stride=4 * tiles_y), :]
                    for t in range(16)
                ]
                block = lanes_of((count, LANES)) // 8
                for bit in (1, 2, 4, 8):
                    moved = (block & bit) != 0
                    xs = [jnp.where(moved, xs[(i + bit) % 16], xs[i]) for i in range(16)]
                for k in range(NZ):
                    x = xs[-k % 16]
                    x = x if k == 0 else pltpu.roll(x, LANES - 8 * k, 1)
                    target.at[k][pl.ds(8 + 2 * base + r, count, stride=2), :] = x

    scale = spacing(4)
    h = min(16, rows4)
    first_lane, last_lane = lanes_of((h, LANES)) == 0, lanes_of((h, LANES)) == LANES - 1
    starts = list(range(8, 8 + rows4, h))

    def faces_x(r, h):
        for k in range(NZ):
            total = rho4[k, pl.ds(r, h), :] + rho4[k, pl.ds(r - 1, h), :]
            ax4[k, pl.ds(r, h), :] = scale * rcp(jnp.maximum(total, TINY))

    for r in starts:
        faces_x(r, h)
    faces_x(rows4 + 1, 8)

    def first_sweep(r):
        rho = rho4[0, pl.ds(r, h), :]
        upper = (2.0 * VERTICAL) * rcp(rho)
        partial, ratio = [], None
        for k in range(NZ):
            here = rho4[k, pl.ds(r, h), :]
            left = jnp.where(first_lane, 0.0, pltpu.roll(here, 1, 1))
            ay = scale * rcp(here + left)
            right = jnp.where(last_lane, scale * rcp(here), pltpu.roll(ay, LANES - 1, 1))
            ay4[k, pl.ds(r, h), :] = jnp.where(first_lane, 0.0, ay)
            center = ax4[k, pl.ds(r, h), :] + ax4[k, pl.ds(r + 1, h), :] + ay + right + upper
            if k + 1 < NZ:
                lower = (2.0 * VERTICAL) * rcp(here + rho4[k + 1, pl.ds(r, h), :])
                center = center + lower
            c4[k, pl.ds(r, h), :] = center
            a4[k, pl.ds(r, h), :] = upper
            pivot = center if k == 0 else center - upper * ratio
            inverse = rcp(pivot)
            scaled = 0.8 * inverse
            d4[k, pl.ds(r, h), :] = scaled
            value = scaled * f4[k, pl.ds(r, h), :]
            if k > 0:
                weight = upper * inverse
                e4[k, pl.ds(r, h), :] = weight
                value = value + weight * partial[-1]
            partial.append(value)
            if k + 1 < NZ:
                ratio = lower * inverse
                g4[k, pl.ds(r, h), :] = ratio
                upper = lower
        w = partial[-1]
        va4[NZ - 1, pl.ds(r, h), :] = w
        for k in range(NZ - 2, -1, -1):
            w = partial[k] + g4[k, pl.ds(r, h), :] * w
            va4[k, pl.ds(r, h), :] = w

    for r in starts:
        first_sweep(r)

    def pulled4(v, k, r):
        here = v[k, pl.ds(r, h), :]
        ay = ay4[k, pl.ds(r, h), :]
        return (
            f4[k, pl.ds(r, h), :]
            + ax4[k, pl.ds(r, h), :] * v[k, pl.ds(r - 1, h), :]
            + ax4[k, pl.ds(r + 1, h), :] * v[k, pl.ds(r + 1, h), :]
            + ay * pltpu.roll(here, 1, 1)
            + pltpu.roll(ay * here, LANES - 1, 1)
        )

    def sweep(v, out):
        for r in starts:
            partial = []
            for k in range(NZ):
                value = d4[k, pl.ds(r, h), :] * pulled4(v, k, r)
                if k > 0:
                    value = value + e4[k, pl.ds(r, h), :] * partial[-1]
                partial.append(value)
            w = None
            for k in range(NZ - 1, -1, -1):
                w = partial[k] if w is None else partial[k] + g4[k, pl.ds(r, h), :] * w
                out[k, pl.ds(r, h), :] = 0.2 * v[k, pl.ds(r, h), :] + w

    ends = [va4, vb4]
    for number in range(SWEEPS - 1):
        sweep(ends[number % 2], ends[(number + 1) % 2])
    final = ends[(SWEEPS - 1) % 2]
    shifts = []
    for k in range(NZ):
        left_over, weights = None, None
        for r in starts:
            center = c4[k, pl.ds(r, h), :]
            part = pulled4(final, k, r) - center * final[k, pl.ds(r, h), :]
            if k > 0:
                part = part + a4[k, pl.ds(r, h), :] * final[k - 1, pl.ds(r, h), :]
            if k + 1 < NZ:
                part = part + a4[k + 1, pl.ds(r, h), :] * final[k + 1, pl.ds(r, h), :]
            left_over = part if left_over is None else left_over + part
            weights = center if weights is None else weights + center
        raised = jnp.sum(left_over, axis=(0, 1), keepdims=True)
        shifts.append(raised / jnp.sum(weights, axis=(0, 1), keepdims=True))

    row = rows_of() + (ix * 2 - 4)
    column = lane + (iy * 8 - 4)
    good = jnp.logical_and(
        jnp.logical_and(row >= 0, row < rows4),
        jnp.logical_and(jnp.logical_and(column >= 0, column < grid_lanes // 16), lane < 16),
    )
    amount = lax.rem(132 - iy * 8, LANES)

    def coarsest(k):
        x = final[k, pl.ds(4 + 2 * ix, 8), :] + shifts[k]
        return jnp.where(good, pltpu.roll(x, amount, 1), 0.0)

    repeat = one_hot(LANES, lambda s, t: s == t // 2, 1.0)
    prolong(coarsest, 0, 8, None, [v3], [va3], 0, [repeat])
    level3 = Level(3, None, [ax3], [ay3], [d3], [e3], [g3])
    level3.relax([(2, 16)], [f3], [va3], [vb3])
    level3.relax([(6, 8)], [f3], [vb3], [va3])

    prolong(lambda k: va3[k, pl.ds(6, 8), :], 0, 8, None, [v2], [va2], 12, [repeat])
    level2 = Level(2, None, [ax2], [ay2], [d2], [e2], [g2])
    level2.relax([(12, 16)], [f2], [va2], [vb2])
    level2.relax([(12, 16)], [f2], [vb2], [va2])

    prolong(lambda k: va2[k, pl.ds(12, 16), :], 0, 16, None, [v1], [va1], 0, [repeat])
    level1 = Level(1, None, [ax1], [ay1], [d1], [e1], [g1])
    level1.relax([(4, 24)], [f1], [va1], [vb1])
    level1.relax([(4, 24)], [f1], [vb1], [va1])

    to_main = one_hot(LANES, lambda s, t: s == t // 2 + 32, 1.0)
    to_side = one_hot(
        LANES,
        lambda s, t: jnp.logical_or(
            jnp.logical_and(t < 64, s == t // 2 + 96), jnp.logical_and(t >= 64, s == t // 2 - 32)
        ),
        1.0,
    )
    prolong(lambda k: va1[k, pl.ds(4, 24), :], 0, 24, None, [vm, vh], [vam, vah], 8, [to_main, to_side])
    fine = Level(0, None, [axm, axh], [aym, ayh], [dm, dh], [em, eh], [gm, gh])
    fine.relax([(15, 16, 2), (41, 8)], [fm, fh], [vam, vah], [vbm, vbh])
    fine.relax([(16, 16, 2)], [fm, fh], [vbm, vbh], [out_ref], wanted=[0], shift=16)


def ring(x, axis, step):
    size = lax.axis_size(axis)
    return lax.ppermute(x, axis, [(i, (i + step) % size) for i in range(size)])


def gather(x, axis):
    size = lax.axis_size(axis)
    blocks = jnp.broadcast_to(x[None], (size,) + x.shape)
    return lax.all_to_all(blocks, axis, 0, 0).reshape(size * x.shape[0], LANES)


def array(*shape):
    return jax.ShapeDtypeStruct(shape, jnp.float32)


def call(kernel, name, outs, scratch, index, *operands):
    vmem = pl.BlockSpec(memory_space=pltpu.VMEM)
    ins = [vmem] * len(operands)
    if index is not None:
        ins, operands = [pl.BlockSpec(memory_space=pltpu.SMEM)] + ins, (index,) + operands
    return pl.pallas_call(
        kernel,
        out_shape=outs,
        in_specs=ins,
        out_specs=[vmem] * len(outs),
        scratch_shapes=[pltpu.VMEM(shape, jnp.float32) for shape in scratch],
        compiler_params=pltpu.CompilerParams(vmem_limit_bytes=VMEM_BYTES),
        name=name,
    )(*operands)


def solution(mesh):
    tiles_x, tiles_y = mesh.shape["gx"], mesh.shape["gy"]
    grid = (32 * tiles_x, 128 * tiles_y)
    big = [array(NZ, ROWS[level], LANES) for level in range(4)]

    def on_device(source, rho):
        index = jnp.stack([lax.axis_index("gx"), lax.axis_index("gy")]).astype(jnp.int32)

        both = jnp.concatenate([source, rho], axis=0).transpose(1, 0, 2)
        lows = both[:REACH].reshape(REACH * 2 * NZ, LANES)
        highs = both[-REACH:].reshape(REACH * 2 * NZ, LANES)
        up = ring(highs, "gx", 1)
        dn = ring(lows, "gx", -1)
        strip = array(4, ROWS[0], LANES)
        lefts, rights = call(edges_kernel, "edges", [strip, strip], [], None, source, rho, up, dn)
        from_left_strip = ring(rights, "gy", 1)
        from_right_strip = ring(lefts, "gy", -1)

        s0, s1, s2, s3 = [x.shape for x in big]
        fine = call(
            lambda *refs: fine_kernel(grid, *refs),
            "fine",
            [array(8, 8, LANES)] + [big[0]] * 14 + [big[1]] * 7,
            [s0] * 6 + [s1] * 4,
            index, source, rho, up, dn, from_left_strip, from_right_strip,
        )
        tile = fine[0]
        pieces = [ring(tile, "gx", 2), ring(tile, "gx", 1), tile, ring(tile, "gx", -1), ring(tile, "gx", -2)]
        own_left = jnp.concatenate([piece[:4] for piece in pieces], axis=1)
        own_right = jnp.concatenate([piece[4:] for piece in pieces], axis=1)
        from_left_column = ring(own_right, "gy", 1)
        from_right_column = ring(own_left, "gy", -1)
        coarser = call(
            lambda *refs: coarser_kernel(grid, *refs),
            "coarser",
            [array(4, LANES)] + [big[2]] * 7 + [big[3]] * 7,
            [s2] * 4 + [s3] * 4,
            index, own_left, own_right, from_left_column, from_right_column,
        )
        gathered = gather(gather(coarser[0], "gy"), "gx")

        s4 = (NZ, 16 + 2 * tiles_x, LANES)
        (pressure,) = call(
            lambda *refs: top_kernel(grid, (tiles_x, tiles_y), *refs),
            "top",
            [array(NZ, 32, LANES)],
            [s4] * 11 + [s3] * 2 + [s2] * 2 + [s1] * 2 + [s0] * 4,
            index, gathered, *fine[1:], *coarser[1:],
        )
        return pressure

    return jax.shard_map(
        on_device,
        mesh=mesh,
        in_specs=(P(None, "gx", "gy"), P(None, "gx", "gy")),
        out_specs=P(None, "gx", "gy"),
        check_vma=False,
    )
```

```python
import jax
import jax.numpy as jnp
from jax import lax
from jax.experimental import pallas as pl
from jax.experimental.pallas import tpu as pltpu
from jax.sharding import PartitionSpec as P

NZ = 16
LANES = 128
SWEEPS = 6
VERTICAL = 0.015625
TINY = 2.0**-20
VMEM_BYTES = 16 * 1024 * 1024

SPLIT = 24
SIDE_ROWS = 40
ROW0 = (16, 8, 16, 8)
ROWS = (64, 32, 40, 24)
LANE0 = (0, 32, 16, 8)


def spacing(level):
    return 2.0 * 0.25**level


def lanes_of(shape=(8, LANES)):
    return lax.broadcasted_iota(jnp.int32, shape, 1)


def rows_of(shape=(8, LANES)):
    return lax.broadcasted_iota(jnp.int32, shape, 0)


def rcp(x):
    guess = pl.reciprocal(x, approx=True)
    return guess * (2.0 - x * guess)


def from_left(xs):
    rolled = [pltpu.roll(x, 1, 1) for x in xs]
    if len(xs) == 1:
        return rolled
    edge = lanes_of(xs[0].shape) == 0
    return [jnp.where(edge, rolled[1], rolled[0]), jnp.where(edge, rolled[0], rolled[1])]


def from_right(xs):
    rolled = [pltpu.roll(x, LANES - 1, 1) for x in xs]
    if len(xs) == 1:
        return rolled
    edge = lanes_of(xs[0].shape) == LANES - 1
    return [jnp.where(edge, rolled[1], rolled[0]), jnp.where(edge, rolled[0], rolled[1])]


def split_dot(x, matrix, pieces=2):
    total = None
    for piece in range(pieces):
        part = x.astype(jnp.bfloat16)
        product = jnp.dot(part, matrix, preferred_element_type=jnp.float32)
        total = product if total is None else total + product
        if piece + 1 < pieces:
            x = x - part.astype(jnp.float32)
    return total


def one_hot(rows, test, value, lanes=LANES):
    shape = (rows, lanes)
    source, target = lax.broadcasted_iota(jnp.int32, shape, 0), lax.broadcasted_iota(jnp.int32, shape, 1)
    return jnp.where(test(source, target), value, 0.0).astype(jnp.bfloat16)


def run_blocks(blocks, body):
    for block in blocks:
        if len(block) == 2:
            body(*block)
        else:
            first, height, count = block

            def step(index, carry):
                body(first + height * index, height)
                return carry

            lax.fori_loop(0, count, step, 0)


class Level:
    def __init__(self, level, rho, ax, ay, d, e, g):
        self.level, self.rho, self.ax, self.ay, self.d, self.e, self.g = level, rho, ax, ay, d, e, g
        self.parts = range(len(ax))

    def faces(self, blocks):
        scale = spacing(self.level)

        def body(r, h):
            for k in range(NZ):
                here = [ref[k, pl.ds(r, h), :] for ref in self.rho]
                above = [ref[k, pl.ds(r - 1, h), :] for ref in self.rho]
                left = from_left(here)
                for p in self.parts:
                    self.ax[p][k, pl.ds(r, h), :] = scale * rcp(jnp.maximum(here[p] + above[p], TINY))
                    self.ay[p][k, pl.ds(r, h), :] = scale * rcp(jnp.maximum(here[p] + left[p], TINY))

        run_blocks(blocks, body)

    def factor_and_first(self, blocks, inside, f, v):
        def body(r, h):
            masks = None if inside is None else [inside(r, h) for p in self.parts]
            ratio = [None for p in self.parts]
            partial = [[] for p in self.parts]
            upper = [None for p in self.parts]
            rho = [ref[0, pl.ds(r, h), :] for ref in self.rho]
            for p in self.parts:
                upper[p] = (2.0 * VERTICAL) * rcp(jnp.maximum(rho[p], TINY))
            for k in range(NZ):
                if k + 1 < NZ:
                    below = [ref[k + 1, pl.ds(r, h), :] for ref in self.rho]
                    lower = [
                        (2.0 * VERTICAL) * rcp(jnp.maximum(rho[p] + below[p], TINY)) for p in self.parts
                    ]
                ay = [ref[k, pl.ds(r, h), :] for ref in self.ay]
                right = from_right(ay)
                for p in self.parts:
                    center = (
                        self.ax[p][k, pl.ds(r, h), :]
                        + self.ax[p][k, pl.ds(r + 1, h), :]
                        + ay[p]
                        + right[p]
                        + upper[p]
                    )
                    if k + 1 < NZ:
                        center = center + lower[p]
                    pivot = center if k == 0 else center - upper[p] * ratio[p]
                    inverse = rcp(pivot) if masks is None else jnp.where(masks[p], rcp(pivot), 0.0)
                    scaled = 0.8 * inverse
                    self.d[p][k, pl.ds(r, h), :] = scaled
                    value = scaled * f[p][k, pl.ds(r, h), :]
                    if k > 0:
                        weight = upper[p] * inverse
                        self.e[p][k, pl.ds(r, h), :] = weight
                        value = value + weight * partial[p][-1]
                    partial[p].append(value)
                    if k + 1 < NZ:
                        ratio[p] = lower[p] * inverse
                        self.g[p][k, pl.ds(r, h), :] = ratio[p]
                if k + 1 < NZ:
                    rho, upper = below, lower
            for p in self.parts:
                w = partial[p][-1]
                v[p][NZ - 1, pl.ds(r, h), :] = w
                for k in range(NZ - 2, -1, -1):
                    w = partial[p][k] + self.g[p][k, pl.ds(r, h), :] * w
                    v[p][k, pl.ds(r, h), :] = w

        run_blocks(blocks, body)

    def pull(self, v, k, r, h, wanted):
        here = [ref[k, pl.ds(r, h), :] for ref in v]
        ay = [ref[k, pl.ds(r, h), :] for ref in self.ay]
        left = from_left(here)
        right = from_right([a * x for a, x in zip(ay, here)])
        return [
            self.ax[p][k, pl.ds(r, h), :] * v[p][k, pl.ds(r - 1, h), :]
            + self.ax[p][k, pl.ds(r + 1, h), :] * v[p][k, pl.ds(r + 1, h), :]
            + ay[p] * left[p]
            + right[p]
            for p in wanted
        ]

    def relax(self, blocks, f, v, out, u=None, wanted=None, shift=0):
        wanted = self.parts if wanted is None else wanted

        def body(r, h):
            partial = [[] for p in wanted]
            for k in range(NZ):
                pulls = self.pull(v, k, r, h, wanted)
                for n, p in enumerate(wanted):
                    value = self.d[p][k, pl.ds(r, h), :] * (f[p][k, pl.ds(r, h), :] + pulls[n])
                    if k > 0:
                        value = value + self.e[p][k, pl.ds(r, h), :] * partial[n][-1]
                    partial[n].append(value)
            for n, p in enumerate(wanted):
                w = None
                for k in range(NZ - 1, -1, -1):
                    w = partial[n][k] if w is None else partial[n][k] + self.g[p][k, pl.ds(r, h), :] * w
                    old = v[p][k, pl.ds(r, h), :]
                    out[p][k, pl.ds(r - shift, h), :] = 0.2 * old + w
                    if u is not None:
                        u[p][k, pl.ds(r, h), :] = w - 0.6 * old

        run_blocks(blocks, body)

    def residual(self, blocks, f, u, out):
        def body(r, h):
            for k in range(NZ):
                pulls = self.pull(u, k, r, h, self.parts)
                for p in self.parts:
                    out[p][k, pl.ds(r, h), :] = 0.04 * f[p][k, pl.ds(r, h), :] + pulls[p]

        run_blocks(blocks, body)


def inside_of(level, ix, iy, shape, part=0):
    grid_rows, grid_lanes, tile_rows, tile_lanes = shape

    def inside(r, h):
        row, lane = rows_of((h, LANES)) + (r + ix * tile_rows - ROW0[level]), lanes_of((h, LANES))
        if level == 0 and part == 1:
            row = row + jnp.where(lane < 64, 0, SPLIT)
            lane = lane % 64
        good = jnp.logical_and(row >= 0, row < grid_rows)
        if level == 0 and part == 0:
            return good
        if level == 0:
            column = iy * tile_lanes + jnp.where(lane < 32, lane - 16, lane + 80)
            side = jnp.logical_and(column >= 0, column < grid_lanes)
        else:
            column = iy * tile_lanes + lane - LANE0[level]
            side = jnp.logical_and(column >= 0, column < grid_lanes)
        return jnp.logical_and(good, side)

    return inside


def pair_rows(ref, k, start, count):
    layer = ref.at[k]
    return layer[pl.ds(start, count, stride=2), :] + layer[pl.ds(start + 1, count, stride=2), :]


def stack_rows(blocks):
    return jnp.concatenate(blocks, axis=0)


PIECES = ((5, 8, "up", 0), (8, 8, "up", 3), (16, 32, "own", 0), (48, 8, "down", 0), (51, 8, "down", 3))
REACH = 11


def piece_of(piece, field, k, own, up, down):
    first, count, source, start = piece
    if source == "own":
        return own[k, :, :]
    ref = up if source == "up" else down
    return ref[pl.ds(start * 2 * NZ + field * NZ + k, count, stride=2 * NZ), :]


def edges_kernel(f_ref, rho_ref, up_ref, dn_ref, left_ref, right_ref):
    for field, own in enumerate((f_ref, rho_ref)):
        for piece in PIECES:
            first, count = piece[:2]
            slot = lanes_of((count, LANES)) // 16
            for half in range(2):
                lefts, rights = None, None
                for q in range(8):
                    x = piece_of(piece, field, half * 8 + q, own, up_ref, dn_ref)
                    a = x if q == 0 else pltpu.roll(x, 16 * q, 1)
                    b = pltpu.roll(x, 16 * q + 16, 1) if q < 7 else x
                    lefts = a if q == 0 else jnp.where(slot == q, a, lefts)
                    rights = b if q == 0 else jnp.where(slot == q, b, rights)
                left_ref[field * 2 + half, pl.ds(first, count), :] = lefts
                right_ref[field * 2 + half, pl.ds(first, count), :] = rights


def inner_kernel(f_ref, rho_ref, fm, vm, axm, aym, dm, em, gm, rm, firstm, um, resm):
    for k in range(NZ):
        fm[k, pl.ds(16, 32), :] = f_ref[k, :, :]
        rm[k, pl.ds(16, 32), :] = rho_ref[k, :, :]
    main = Level(0, [rm], [axm], [aym], [dm], [em], [gm])
    main.faces([(17, 16), (32, 16)])
    main.factor_and_first([(17, 16), (31, 16)], None, [fm], [firstm])
    main.relax([(18, 16), (30, 16)], [fm], [firstm], [vm], u=[um])
    main.residual([(19, 16), (29, 16)], [fm], [um], [resm])


def outer_kernel(grid, index_ref, near_ref, far_ref, *refs):
    fm, vm, axm, aym, dm, em, gm, rm, firstm, um, resm = refs[11:]
    ix, iy = index_ref[0], index_ref[1]
    inside = inside_of(0, ix, iy, grid + (32, 128))
    for k in range(NZ):
        for piece in PIECES:
            if piece[2] == "own":
                continue
            first, count = piece[:2]
            fm[k, pl.ds(first, count), :] = piece_of(piece, 0, k, None, near_ref, far_ref)
            x = piece_of(piece, 1, k, None, near_ref, far_ref)
            rm[k, pl.ds(first, count), :] = jnp.where(inside(first, count), x, 0.0)
    main = Level(0, [rm], [axm], [aym], [dm], [em], [gm])
    main.faces([(1, 16), (48, 16)])
    main.factor_and_first([(1, 16), (47, 16)], inside, [fm], [firstm])
    main.relax([(2, 16), (46, 16)], [fm], [firstm], [vm], u=[um])
    main.residual([(3, 16), (45, 16)], [fm], [um], [resm])


def fine_kernel(
    grid, index_ref, rm, resm, own_left, own_right, from_left_ref, from_right_ref,
    pack_ref, fh, vh, axh, ayh, dh, eh, gh, f1, v1, ax1, ay1, d1, e1, g1,
    rh, firsth, uh, rho1, first1, u1, res1,
):
    ix, iy = index_ref[0], index_ref[1]
    grid_rows, grid_lanes = grid
    inside = inside_of(0, ix, iy, grid + (32, 128), part=1)

    lane = lanes_of((16, LANES))
    for field, side in enumerate((fh, rh)):
        for first in (4, 20):
            good = inside(first, 16)
            for half in range(2):
                g = field * 2 + half
                tiles = []
                for start in (first, first + SPLIT):
                    rows = pl.ds(start, 16)
                    tiles.append(
                        [
                            from_left_ref[g, rows, :],
                            pltpu.roll(own_left[g, rows, :], 16, 1),
                            pltpu.roll(own_right[g, rows, :], 32, 1),
                            pltpu.roll(from_right_ref[g, rows, :], 48, 1),
                        ]
                    )
                for m in range(4):
                    place = (lane - 16 * m) % 128
                    spot = place % 64
                    upper, lower = [
                        jnp.where(
                            spot < 32, jnp.where(spot < 16, t[0], t[1]), jnp.where(spot < 48, t[2], t[3])
                        )
                        for t in tiles
                    ]
                    straight = jnp.where(place < 64, upper, lower)
                    crossed = jnp.where(place < 64, lower, upper)
                    if m > 0:
                        straight = pltpu.roll(straight, LANES - 16 * m, 1)
                        crossed = pltpu.roll(crossed, LANES - 16 * m, 1)
                    crossed = pltpu.roll(crossed, 64, 1)
                    for layer, y in (
                        (m, jnp.where(lane < 64, straight, crossed)),
                        (m + 4, jnp.where(lane < 64, crossed, straight)),
                    ):
                        if field == 1:
                            y = jnp.where(good, y, 0.0)
                        side[half * 8 + layer, pl.ds(first, 16), :] = y

    sides = Level(0, [rh], [axh], [ayh], [dh], [eh], [gh])
    sides.faces([(4, 16), (20, 16)])
    sides.factor_and_first([(5, 16), (19, 16)], inside, [fh], [firsth])
    sides.relax([(6, 16), (18, 16)], [fh], [firsth], [vh], u=[uh])
    sides.residual([(8, 24)], [fh], [uh], [firsth])

    main_matrix = one_hot(LANES, lambda s, t: (s // 2 + 32 == t) & (s >= 4) & (s < 124), 0.25)
    upper_matrix, lower_matrix = [
        one_hot(
            LANES,
            lambda s, t: ((s // 2 - base // 2 + 24 == t) & (s >= base + 6) & (s < base + 20))
            | ((s // 2 - base // 2 + 72 == t) & (s >= base + 44) & (s < base + 58)),
            0.25,
        )
        for base in (0, 64)
    ]
    for first in range(0, NZ, 4):
        ks = range(first, first + 4)
        for target, main, side in ((f1, resm, firsth), (rho1, rm, rh)):
            total = split_dot(stack_rows([pair_rows(main, k, 0, 32) for k in ks]), main_matrix)
            upper = split_dot(stack_rows([pair_rows(side, k, 0, 16) for k in ks]), upper_matrix)
            lower = split_dot(stack_rows([pair_rows(side, k, 8, 16) for k in ks]), lower_matrix)
            for n, k in enumerate(ks):
                target[k, pl.ds(0, 16), :] = total[n * 32 : n * 32 + 16] + upper[n * 16 : n * 16 + 16]
                target[k, pl.ds(16, 16), :] = total[n * 32 + 16 : n * 32 + 32] + lower[n * 16 : n * 16 + 16]

    middle = Level(1, [rho1], [ax1], [ay1], [d1], [e1], [g1])
    inside = inside_of(1, ix, iy, (grid_rows // 2, grid_lanes // 2, 16, 64))
    middle.faces([(4, 24), (21, 8)])
    middle.factor_and_first([(4, 24)], inside, [f1], [first1])
    middle.relax([(4, 24)], [f1], [first1], [v1], u=[u1])
    middle.residual([(8, 16)], [f1], [u1], [res1])

    pack_matrix = one_hot(
        LANES,
        lambda s, t: jnp.logical_and(
            s // 2 - 16 == (t // LANES) * 16 + t % 16, jnp.logical_and(s >= 32, s < 96)
        ),
        0.25,
        2 * LANES,
    )
    slot = lanes_of() // 16
    for field, ref in enumerate((res1, rho1)):
        wide = split_dot(stack_rows([pair_rows(ref, k, 8, 8) for k in range(NZ)]), pack_matrix)
        for side in range(2):
            for half in range(2):
                packed = None
                for q in range(8):
                    k = half * 8 + q
                    x = wide[k * 8 : (k + 1) * 8, side * LANES : (side + 1) * LANES]
                    packed = x if q == 0 else jnp.where(slot == q, x, packed)
                pack_ref[side * 4 + field * 2 + half, :, :] = packed


def coarser_kernel(
    grid, index_ref, own_left_ref, own_right_ref, from_left_ref, from_right_ref,
    pack_ref, f2, v2, ax2, ay2, d2, e2, g2, f3, v3, ax3, ay3, d3, e3, g3,
    rho2, first2, u2, res2, rho3, first3, u3, res3,
):
    ix, iy = index_ref[0], index_ref[1]
    grid_rows, grid_lanes = grid
    lane = lanes_of()
    inside = inside_of(2, ix, iy, (grid_rows // 4, grid_lanes // 4, 8, 32))

    lane40 = lanes_of((40, LANES))
    good = inside(0, 40)
    for field, target in enumerate((f2, rho2)):
        for half in range(2):
            g = field * 2 + half
            tiles = [
                from_left_ref[g],
                pltpu.roll(own_left_ref[g], 16, 1),
                pltpu.roll(own_right_ref[g], 32, 1),
                pltpu.roll(from_right_ref[g], 48, 1),
            ]
            for m in range(4):
                place = (lane40 - 16 * m) % 64
                merged = jnp.where(
                    place < 32,
                    jnp.where(place < 16, tiles[0], tiles[1]),
                    jnp.where(place < 48, tiles[2], tiles[3]),
                )
                for q in (m, m + 4):
                    y = merged if q == 0 else pltpu.roll(merged, LANES - 16 * q, 1)
                    if field == 1:
                        y = jnp.where(good, y, 0.0)
                    target[half * 8 + q, :, :] = y

    level2 = Level(2, [rho2], [ax2], [ay2], [d2], [e2], [g2])
    level2.faces([(4, 16, 2), (29, 8)])
    level2.factor_and_first([(4, 16, 2)], inside, [f2], [first2])
    level2.relax([(4, 16, 2)], [f2], [first2], [v2], u=[u2])
    level2.residual([(4, 16, 2)], [f2], [u2], [res2])

    halve = one_hot(LANES, lambda s, t: s // 2 == t, 0.25)
    for ref, target, first, count in ((res2, f3, 4, 16), (rho2, rho3, 4, 16)):
        total = split_dot(stack_rows([pair_rows(ref, k, first, count) for k in range(NZ)]), halve)
        for k in range(NZ):
            target[k, pl.ds(first // 2, count), :] = total[k * count : (k + 1) * count]

    level3 = Level(3, [rho3], [ax3], [ay3], [d3], [e3], [g3])
    inside = inside_of(3, ix, iy, (grid_rows // 8, grid_lanes // 8, 4, 16))
    level3.faces([(2, 16)])
    level3.factor_and_first([(2, 16)], inside, [f3], [first3])
    level3.relax([(2, 16)], [f3], [first3], [v3], u=[u3])
    level3.residual([(6, 8)], [f3], [u3], [res3])

    spread = one_hot(
        LANES,
        lambda s, t: jnp.logical_and(s // 2 - 4 == t % 8, jnp.logical_and(s >= 8, s < 24)),
        0.25,
    )
    for field, ref in enumerate((res3, rho3)):
        total = split_dot(stack_rows([pair_rows(ref, k, 8, 8) for k in range(NZ)]), spread)
        merged = total[0:8]
        for k in range(1, NZ):
            merged = jnp.where(lane // 8 == k, total[k * 8 : (k + 1) * 8], merged)
        pack_ref[pl.ds(2 * field, 2), :] = pltpu.roll(merged, 8 * iy, 1)[0:2]


def prolong(coarse, first_row, count, ref, old, target, target_row, matrix):
    rows = stack_rows([coarse(k) for k in range(NZ)])
    for part in range(len(target)):
        fine = split_dot(rows, matrix[part])
        for k in range(NZ):
            x = fine[k * count : (k + 1) * count]
            for odd in range(2):
                where = pl.ds(target_row + odd, count, stride=2)
                target[part].at[k][where, :] = old[part].at[k][where, :] + x


def top_kernel(
    grid, tiles, index_ref, gathered, fm, vm, axm, aym, dm, em, gm, fh, vh, axh, ayh, dh, eh, gh,
    f1, v1, ax1, ay1, d1, e1, g1, f2, v2, ax2, ay2, d2, e2, g2, f3, v3, ax3, ay3, d3, e3, g3,
    out_ref,
    rho4, f4, ax4, ay4, d4, e4, g4, c4, a4, va4, vb4, va3, vb3, va2, vb2, va1, vb1, vam, vah, vbm, vbh,
):
    ix, iy = index_ref[0], index_ref[1]
    grid_rows, grid_lanes = grid
    lane = lanes_of()
    rows4 = grid_rows // 16
    tiles_x, tiles_y = tiles

    zero = jnp.zeros((8, LANES), jnp.float32)
    for ref in (rho4, va4, vb4):
        for k in range(NZ):
            ref[k, pl.ds(0, 8), :] = zero
            ref[k, pl.ds(8 + rows4, 8), :] = zero

    count = min(8, tiles_x)
    for field, target in enumerate((f4, rho4)):
        for r in range(2):
            for base in range(0, tiles_x, count):
                xs = [
                    gathered[pl.ds((base * tiles_y + t) * 4 + field * 2 + r, count, stride=4 * tiles_y), :]
                    for t in range(16)
                ]
                block = lanes_of((count, LANES)) // 8
                for bit in (1, 2, 4, 8):
                    moved = (block & bit) != 0
                    xs = [jnp.where(moved, xs[(i + bit) % 16], xs[i]) for i in range(16)]
                for k in range(NZ):
                    x = xs[-k % 16]
                    x = x if k == 0 else pltpu.roll(x, LANES - 8 * k, 1)
                    target.at[k][pl.ds(8 + 2 * base + r, count, stride=2), :] = x

    scale = spacing(4)
    h = min(16, rows4)
    first_lane, last_lane = lanes_of((h, LANES)) == 0, lanes_of((h, LANES)) == LANES - 1
    starts = list(range(8, 8 + rows4, h))

    def faces_x(r, h):
        for k in range(NZ):
            total = rho4[k, pl.ds(r, h), :] + rho4[k, pl.ds(r - 1, h), :]
            ax4[k, pl.ds(r, h), :] = scale * rcp(jnp.maximum(total, TINY))

    for r in starts:
        faces_x(r, h)
    faces_x(rows4 + 1, 8)

    def first_sweep(r):
        rho = rho4[0, pl.ds(r, h), :]
        upper = (2.0 * VERTICAL) * rcp(rho)
        partial, ratio = [], None
        for k in range(NZ):
            here = rho4[k, pl.ds(r, h), :]
            left = jnp.where(first_lane, 0.0, pltpu.roll(here, 1, 1))
            ay = scale * rcp(here + left)
            right = jnp.where(last_lane, scale * rcp(here), pltpu.roll(ay, LANES - 1, 1))
            ay4[k, pl.ds(r, h), :] = jnp.where(first_lane, 0.0, ay)
            center = ax4[k, pl.ds(r, h), :] + ax4[k, pl.ds(r + 1, h), :] + ay + right + upper
            if k + 1 < NZ:
                lower = (2.0 * VERTICAL) * rcp(here + rho4[k + 1, pl.ds(r, h), :])
                center = center + lower
            c4[k, pl.ds(r, h), :] = center
            a4[k, pl.ds(r, h), :] = upper
            pivot = center if k == 0 else center - upper * ratio
            inverse = rcp(pivot)
            scaled = 0.8 * inverse
            d4[k, pl.ds(r, h), :] = scaled
            value = scaled * f4[k, pl.ds(r, h), :]
            if k > 0:
                weight = upper * inverse
                e4[k, pl.ds(r, h), :] = weight
                value = value + weight * partial[-1]
            partial.append(value)
            if k + 1 < NZ:
                ratio = lower * inverse
                g4[k, pl.ds(r, h), :] = ratio
                upper = lower
        w = partial[-1]
        va4[NZ - 1, pl.ds(r, h), :] = w
        for k in range(NZ - 2, -1, -1):
            w = partial[k] + g4[k, pl.ds(r, h), :] * w
            va4[k, pl.ds(r, h), :] = w

    for r in starts:
        first_sweep(r)

    def pulled4(v, k, r):
        here = v[k, pl.ds(r, h), :]
        ay = ay4[k, pl.ds(r, h), :]
        return (
            f4[k, pl.ds(r, h), :]
            + ax4[k, pl.ds(r, h), :] * v[k, pl.ds(r - 1, h), :]
            + ax4[k, pl.ds(r + 1, h), :] * v[k, pl.ds(r + 1, h), :]
            + ay * pltpu.roll(here, 1, 1)
            + pltpu.roll(ay * here, LANES - 1, 1)
        )

    def sweep(v, out):
        for r in starts:
            partial = []
            for k in range(NZ):
                value = d4[k, pl.ds(r, h), :] * pulled4(v, k, r)
                if k > 0:
                    value = value + e4[k, pl.ds(r, h), :] * partial[-1]
                partial.append(value)
            w = None
            for k in range(NZ - 1, -1, -1):
                w = partial[k] if w is None else partial[k] + g4[k, pl.ds(r, h), :] * w
                out[k, pl.ds(r, h), :] = 0.2 * v[k, pl.ds(r, h), :] + w

    ends = [va4, vb4]
    for number in range(SWEEPS - 1):
        sweep(ends[number % 2], ends[(number + 1) % 2])
    final = ends[(SWEEPS - 1) % 2]
    shifts = []
    for k in range(NZ):
        left_over, weights = None, None
        for r in starts:
            center = c4[k, pl.ds(r, h), :]
            part = pulled4(final, k, r) - center * final[k, pl.ds(r, h), :]
            if k > 0:
                part = part + a4[k, pl.ds(r, h), :] * final[k - 1, pl.ds(r, h), :]
            if k + 1 < NZ:
                part = part + a4[k + 1, pl.ds(r, h), :] * final[k + 1, pl.ds(r, h), :]
            left_over = part if left_over is None else left_over + part
            weights = center if weights is None else weights + center
        raised = jnp.sum(left_over, axis=(0, 1), keepdims=True)
        shifts.append(raised / jnp.sum(weights, axis=(0, 1), keepdims=True))

    row = rows_of() + (ix * 2 - 4)
    column = lane + (iy * 8 - 4)
    good = jnp.logical_and(
        jnp.logical_and(row >= 0, row < rows4),
        jnp.logical_and(jnp.logical_and(column >= 0, column < grid_lanes // 16), lane < 16),
    )
    amount = lax.rem(132 - iy * 8, LANES)

    def coarsest(k):
        x = final[k, pl.ds(4 + 2 * ix, 8), :] + shifts[k]
        return jnp.where(good, pltpu.roll(x, amount, 1), 0.0)

    repeat = one_hot(LANES, lambda s, t: s == t // 2, 1.0)
    prolong(coarsest, 0, 8, None, [v3], [va3], 0, [repeat])
    level3 = Level(3, None, [ax3], [ay3], [d3], [e3], [g3])
    level3.relax([(2, 16)], [f3], [va3], [vb3])
    level3.relax([(6, 8)], [f3], [vb3], [va3])

    prolong(lambda k: va3[k, pl.ds(6, 8), :], 0, 8, None, [v2], [va2], 12, [repeat])
    level2 = Level(2, None, [ax2], [ay2], [d2], [e2], [g2])
    level2.relax([(12, 16)], [f2], [va2], [vb2])
    level2.relax([(12, 16)], [f2], [vb2], [va2])

    prolong(lambda k: va2[k, pl.ds(12, 16), :], 0, 16, None, [v1], [va1], 0, [repeat])
    level1 = Level(1, None, [ax1], [ay1], [d1], [e1], [g1])
    level1.relax([(4, 24)], [f1], [va1], [vb1])
    level1.relax([(4, 24)], [f1], [vb1], [va1])

    to_main = one_hot(LANES, lambda s, t: s == t // 2 + 32, 1.0)
    prolong(lambda k: va1[k, pl.ds(4, 24), :], 0, 24, None, [vm], [vam], 8, [to_main])
    lane = lanes_of((16, LANES))
    to_upper, to_lower = [
        one_hot(
            LANES,
            lambda s, t: ((t < base + 32) & (t >= base) & (s == (t - base) // 2 + 24))
            | ((t >= base + 32) & (t < base + 64) & (s == (t - base) // 2 + 72)),
            1.0,
        )
        for base in (0, 64)
    ]
    upper = split_dot(stack_rows([va1[k, pl.ds(2, 16), :] for k in range(NZ)]), to_upper)
    lower = split_dot(stack_rows([va1[k, pl.ds(2 + SPLIT // 2, 16), :] for k in range(NZ)]), to_lower)
    for k in range(NZ):
        x = jnp.where(lane < 64, upper[k * 16 : k * 16 + 16], lower[k * 16 : k * 16 + 16])
        for odd in range(2):
            where = pl.ds(4 + odd, 16, stride=2)
            vah.at[k][where, :] = vh.at[k][where, :] + x
    sides = Level(0, None, [axh], [ayh], [dh], [eh], [gh])
    sides.relax([(7, 16), (17, 16)], [fh], [vah], [vbh])
    sides.relax([(8, 24)], [fh], [vbh], [vah])
    main = Level(0, None, [axm], [aym], [dm], [em], [gm])
    main.relax([(15, 16, 2), (41, 8)], [fm], [vam], [vbm])
    main.relax([(16, 16, 2)], [fm], [vbm], [vam])
    for k in range(NZ):
        for row, start, low, high in ((0, 16, 112, 80), (16, 16 - SPLIT + 16, 48, 16)):
            side = vah[k, pl.ds(start, 16), :]
            side = jnp.where(lane < 64, pltpu.roll(side, low, 1), pltpu.roll(side, high, 1))
            x = vam[k, pl.ds(16 + row, 16), :]
            out_ref[k, pl.ds(row, 16), :] = jnp.where(jnp.logical_or(lane < 4, lane >= 124), side, x)


def ring(x, axis, step):
    size = lax.axis_size(axis)
    return lax.ppermute(x, axis, [(i, (i + step) % size) for i in range(size)])


def gather(x, axis):
    size = lax.axis_size(axis)
    blocks = jnp.broadcast_to(x[None], (size,) + x.shape)
    return lax.all_to_all(blocks, axis, 0, 0).reshape(size * x.shape[0], LANES)


def array(*shape):
    return jax.ShapeDtypeStruct(shape, jnp.float32)


def call(kernel, name, outs, scratch, index, *operands, aliases=None, cost=4000000):
    vmem = pl.BlockSpec(memory_space=pltpu.VMEM)
    ins = [vmem] * len(operands)
    if index is not None:
        ins, operands = [pl.BlockSpec(memory_space=pltpu.SMEM)] + ins, (index,) + operands
    return pl.pallas_call(
        kernel,
        out_shape=outs,
        in_specs=ins,
        out_specs=[vmem] * len(outs),
        scratch_shapes=[pltpu.VMEM(shape, jnp.float32) for shape in scratch],
        compiler_params=pltpu.CompilerParams(vmem_limit_bytes=VMEM_BYTES),
        input_output_aliases=aliases or {},
        cost_estimate=pl.CostEstimate(flops=cost, bytes_accessed=cost, transcendentals=0),
        name=name,
    )(*operands)


def solution(mesh):
    tiles_x, tiles_y = mesh.shape["gx"], mesh.shape["gy"]
    grid = (32 * tiles_x, 128 * tiles_y)
    big = [array(NZ, ROWS[level], LANES) for level in range(4)]

    def on_device(source, rho):
        index = jnp.stack([lax.axis_index("gx"), lax.axis_index("gy")]).astype(jnp.int32)

        both = jnp.concatenate([source, rho], axis=0).transpose(1, 0, 2)
        lows = both[:REACH].reshape(REACH * 2 * NZ, LANES)
        highs = both[-REACH:].reshape(REACH * 2 * NZ, LANES)
        up = ring(highs, "gx", 1)
        dn = ring(lows, "gx", -1)
        s0, s1, s2, s3 = [x.shape for x in big]
        sh = (NZ, SIDE_ROWS, LANES)
        inner = call(inner_kernel, "inner", [big[0]] * 11, [], None, source, rho)
        strip = array(4, ROWS[0], LANES)
        lefts, rights = call(edges_kernel, "edges", [strip, strip], [], None, source, rho, up, dn)
        from_left_strip = ring(rights, "gy", 1)
        from_right_strip = ring(lefts, "gy", -1)
        main = call(
            lambda *refs: outer_kernel(grid, *refs), "outer", [big[0]] * 11, [], index, up, dn, *inner,
            aliases={3 + n: n for n in range(11)},
        )
        main_state, rho_main, residual_main = main[:7], main[7], main[10]
        fine = call(
            lambda *refs: fine_kernel(grid, *refs),
            "fine",
            [array(8, 8, LANES)] + [array(*sh)] * 7 + [big[1]] * 7,
            [sh] * 3 + [s1] * 4,
            index, rho_main, residual_main, lefts, rights, from_left_strip, from_right_strip,
        )
        tile = fine[0]
        pieces = [ring(tile, "gx", 2), ring(tile, "gx", 1), tile, ring(tile, "gx", -1), ring(tile, "gx", -2)]
        own_left = jnp.concatenate([piece[:4] for piece in pieces], axis=1)
        own_right = jnp.concatenate([piece[4:] for piece in pieces], axis=1)
        from_left_column = ring(own_right, "gy", 1)
        from_right_column = ring(own_left, "gy", -1)
        coarser = call(
            lambda *refs: coarser_kernel(grid, *refs),
            "coarser",
            [array(4, LANES)] + [big[2]] * 7 + [big[3]] * 7,
            [s2] * 4 + [s3] * 4,
            index, own_left, own_right, from_left_column, from_right_column,
        )
        gathered = gather(gather(coarser[0], "gy"), "gx")

        s4 = (NZ, 16 + 2 * tiles_x, LANES)
        (pressure,) = call(
            lambda *refs: top_kernel(grid, (tiles_x, tiles_y), *refs),
            "top",
            [array(NZ, 32, LANES)],
            [s4] * 11 + [s3] * 2 + [s2] * 2 + [s1] * 2 + [s0, sh] * 2,
            index, gathered, *main_state, *fine[1:], *coarser[1:],
        )
        return pressure

    return jax.shard_map(
        on_device,
        mesh=mesh,
        in_specs=(P(None, "gx", "gy"), P(None, "gx", "gy")),
        out_specs=P(None, "gx", "gy"),
        check_vma=False,
    )
```

```python
import jax
import jax.numpy as jnp
from jax import lax
from jax.experimental import pallas as pl
from jax.experimental.pallas import tpu as pltpu
from jax.sharding import PartitionSpec as P

NZ = 16
LANES = 128
SWEEPS = 6
VERTICAL = 0.015625
TINY = 2.0**-20
VMEM_BYTES = 16 * 1024 * 1024

SPLIT = 24
SIDE_ROWS = 40
ROW0 = (16, 8, 16, 8)
ROWS = (64, 32, 40, 24)
LANE0 = (0, 32, 16, 8)


def spacing(level):
    return 2.0 * 0.25**level


def lanes_of(shape=(8, LANES)):
    return lax.broadcasted_iota(jnp.int32, shape, 1)


def rows_of(shape=(8, LANES)):
    return lax.broadcasted_iota(jnp.int32, shape, 0)


def rcp(x):
    guess = pl.reciprocal(x, approx=True)
    return guess * (2.0 - x * guess)


def from_left(xs):
    rolled = [pltpu.roll(x, 1, 1) for x in xs]
    if len(xs) == 1:
        return rolled
    edge = lanes_of(xs[0].shape) == 0
    return [jnp.where(edge, rolled[1], rolled[0]), jnp.where(edge, rolled[0], rolled[1])]


def from_right(xs):
    rolled = [pltpu.roll(x, LANES - 1, 1) for x in xs]
    if len(xs) == 1:
        return rolled
    edge = lanes_of(xs[0].shape) == LANES - 1
    return [jnp.where(edge, rolled[1], rolled[0]), jnp.where(edge, rolled[0], rolled[1])]


def split_dot(x, matrix, pieces=2):
    total = None
    for piece in range(pieces):
        part = x.astype(jnp.bfloat16)
        product = jnp.dot(part, matrix, preferred_element_type=jnp.float32)
        total = product if total is None else total + product
        if piece + 1 < pieces:
            x = x - part.astype(jnp.float32)
    return total


def one_hot(rows, test, value, lanes=LANES):
    shape = (rows, lanes)
    source, target = lax.broadcasted_iota(jnp.int32, shape, 0), lax.broadcasted_iota(jnp.int32, shape, 1)
    return jnp.where(test(source, target), value, 0.0).astype(jnp.bfloat16)


def run_blocks(blocks, body):
    for block in blocks:
        if len(block) == 2:
            body(*block)
        else:
            first, height, count = block

            def step(index, carry):
                body(first + height * index, height)
                return carry

            lax.fori_loop(0, count, step, 0)


TWISTED = (0, 2, 3)


class Level:
    def __init__(self, level, rho, ax, ay, d, e, g):
        self.level, self.rho, self.ax, self.ay, self.d, self.e, self.g = level, rho, ax, ay, d, e, g
        self.parts = range(len(ax))
        self.twist = level in TWISTED
        ends = [n if side == 0 else NZ - 1 - n for n in range(NZ // 2) for side in range(2)]
        self.order = ends if self.twist else list(range(NZ))

    def faces(self, blocks):
        scale = spacing(self.level)

        def body(r, h):
            for k in range(NZ):
                here = [ref[k, pl.ds(r, h), :] for ref in self.rho]
                above = [ref[k, pl.ds(r - 1, h), :] for ref in self.rho]
                left = from_left(here)
                for p in self.parts:
                    self.ax[p][k, pl.ds(r, h), :] = scale * rcp(jnp.maximum(here[p] + above[p], TINY))
                    self.ay[p][k, pl.ds(r, h), :] = scale * rcp(jnp.maximum(here[p] + left[p], TINY))

        run_blocks(blocks, body)

    def before(self, k):
        if self.twist and k >= 8:
            return k + 1 if k + 1 < NZ else None
        return k - 1 if k > 0 else None

    def substitute(self, p, r, h, partial, emit):
        def weight(k):
            return self.g[p][k, pl.ds(r, h), :]

        if not self.twist:
            w = partial[NZ - 1]
            emit(NZ - 1, w)
            for k in range(NZ - 2, -1, -1):
                w = partial[k] + weight(k) * w
                emit(k, w)
            return
        w = self.e[p][0, pl.ds(r, h), :] * (partial[7] + weight(7) * partial[8])
        emit(7, w)
        x = partial[8] + weight(8) * w
        emit(8, x)
        for k in range(6, -1, -1):
            w = partial[k] + weight(k) * w
            emit(k, w)
            x = partial[15 - k] + weight(15 - k) * x
            emit(15 - k, x)

    def factor_and_first(self, blocks, inside, f, v):
        def body(r, h):
            masks = None if inside is None else [inside(r, h) for p in self.parts]
            upper = {}

            def upper_at(k):
                if k not in upper:
                    total = [ref[k, pl.ds(r, h), :] for ref in self.rho]
                    if k > 0:
                        total = [x + ref[k - 1, pl.ds(r, h), :] for x, ref in zip(total, self.rho)]
                    upper[k] = [(2.0 * VERTICAL) * rcp(jnp.maximum(x, TINY)) for x in total]
                return upper[k]

            partial = [[None] * NZ for p in self.parts]
            back = {}
            for k in self.order:
                above = upper_at(k)
                below = upper_at(k + 1) if k + 1 < NZ else None
                ay = [ref[k, pl.ds(r, h), :] for ref in self.ay]
                right = from_right(ay)
                upwards = self.twist and k >= 8
                before = self.before(k)
                for p in self.parts:
                    center = (
                        self.ax[p][k, pl.ds(r, h), :]
                        + self.ax[p][k, pl.ds(r + 1, h), :]
                        + ay[p]
                        + right[p]
                        + above[p]
                    )
                    if k + 1 < NZ:
                        center = center + below[p]
                    toward, away = (below, above) if upwards else (above, below)
                    pivot = center if before is None else center - toward[p] * back[before, p]
                    inverse = rcp(pivot) if masks is None else jnp.where(masks[p], rcp(pivot), 0.0)
                    scaled = 0.8 * inverse
                    self.d[p][k, pl.ds(r, h), :] = scaled
                    value = scaled * f[p][k, pl.ds(r, h), :]
                    if before is not None:
                        weight = toward[p] * inverse
                        self.e[p][k, pl.ds(r, h), :] = weight
                        value = value + weight * partial[p][before]
                    partial[p][k] = value
                    if away is not None:
                        back[k, p] = away[p] * inverse
                        self.g[p][k, pl.ds(r, h), :] = back[k, p]

            for p in self.parts:
                if self.twist:
                    self.e[p][0, pl.ds(r, h), :] = rcp(1.0 - back[7, p] * back[8, p])

                def emit(k, w):
                    v[p][k, pl.ds(r, h), :] = w

                self.substitute(p, r, h, partial[p], emit)

        run_blocks(blocks, body)

    def pull(self, v, k, r, h, wanted):
        here = [ref[k, pl.ds(r, h), :] for ref in v]
        ay = [ref[k, pl.ds(r, h), :] for ref in self.ay]
        left = from_left(here)
        right = from_right([a * x for a, x in zip(ay, here)])
        return [
            self.ax[p][k, pl.ds(r, h), :] * v[p][k, pl.ds(r - 1, h), :]
            + self.ax[p][k, pl.ds(r + 1, h), :] * v[p][k, pl.ds(r + 1, h), :]
            + ay[p] * left[p]
            + right[p]
            for p in wanted
        ]

    def relax(self, blocks, f, v, out, u=None):
        def body(r, h):
            partial = [[None] * NZ for p in self.parts]
            for k in self.order:
                pulls = self.pull(v, k, r, h, self.parts)
                before = self.before(k)
                for p in self.parts:
                    value = self.d[p][k, pl.ds(r, h), :] * (f[p][k, pl.ds(r, h), :] + pulls[p])
                    if before is not None:
                        value = value + self.e[p][k, pl.ds(r, h), :] * partial[p][before]
                    partial[p][k] = value

            for p in self.parts:

                def emit(k, w):
                    old = v[p][k, pl.ds(r, h), :]
                    out[p][k, pl.ds(r, h), :] = 0.2 * old + w
                    if u is not None:
                        u[p][k, pl.ds(r, h), :] = w - 0.6 * old

                self.substitute(p, r, h, partial[p], emit)

        run_blocks(blocks, body)

    def residual(self, blocks, f, u, out):
        def body(r, h):
            for k in range(NZ):
                pulls = self.pull(u, k, r, h, self.parts)
                for p in self.parts:
                    out[p][k, pl.ds(r, h), :] = 0.04 * f[p][k, pl.ds(r, h), :] + pulls[p]

        run_blocks(blocks, body)


def inside_of(level, ix, iy, shape, part=0):
    grid_rows, grid_lanes, tile_rows, tile_lanes = shape

    def inside(r, h):
        row, lane = rows_of((h, LANES)) + (r + ix * tile_rows - ROW0[level]), lanes_of((h, LANES))
        if level == 0 and part == 1:
            row = row + jnp.where(lane < 64, 0, SPLIT)
            lane = lane % 64
        good = jnp.logical_and(row >= 0, row < grid_rows)
        if level == 0 and part == 0:
            return good
        if level == 0:
            column = iy * tile_lanes + jnp.where(lane < 32, lane - 16, lane + 80)
            side = jnp.logical_and(column >= 0, column < grid_lanes)
        else:
            column = iy * tile_lanes + lane - LANE0[level]
            side = jnp.logical_and(column >= 0, column < grid_lanes)
        return jnp.logical_and(good, side)

    return inside


def pair_rows(ref, k, start, count):
    layer = ref.at[k]
    return layer[pl.ds(start, count, stride=2), :] + layer[pl.ds(start + 1, count, stride=2), :]


def stack_rows(blocks):
    return jnp.concatenate(blocks, axis=0)


PIECES = ((5, 8, "up", 0), (8, 8, "up", 3), (16, 32, "own", 0), (48, 8, "down", 0), (51, 8, "down", 3))
REACH = 11


def piece_of(piece, field, k, own, up, down):
    first, count, source, start = piece
    if source == "own":
        return own[k, :, :]
    ref = up if source == "up" else down
    return ref[pl.ds(start * 2 * NZ + field * NZ + k, count, stride=2 * NZ), :]


def pack_rows(piece, sources, left_ref, right_ref):
    first, count = piece[:2]
    slot = lanes_of((count, LANES)) // 16
    for field in range(2):
        for half in range(2):
            lefts, rights = None, None
            for q in range(8):
                x = piece_of(piece, field, half * 8 + q, sources[field], *sources[2:])
                a = x if q == 0 else pltpu.roll(x, 16 * q, 1)
                b = pltpu.roll(x, 16 * q + 16, 1) if q < 7 else x
                lefts = a if q == 0 else jnp.where(slot == q, a, lefts)
                rights = b if q == 0 else jnp.where(slot == q, b, rights)
            left_ref[field * 2 + half, pl.ds(first, count), :] = lefts
            right_ref[field * 2 + half, pl.ds(first, count), :] = rights


def own_edges_kernel(f_ref, rho_ref, left_ref, right_ref):
    pack_rows(PIECES[2], (f_ref, rho_ref, None, None), left_ref, right_ref)


def edges_kernel(up_ref, dn_ref, _, __, left_ref, right_ref):
    for piece in PIECES:
        if piece[2] != "own":
            pack_rows(piece, (None, None, up_ref, dn_ref), left_ref, right_ref)


def inner_kernel(f_ref, rho_ref, fm, vm, axm, aym, dm, em, gm, rm, firstm, um, resm):
    for k in range(NZ):
        fm[k, pl.ds(16, 32), :] = f_ref[k, :, :]
        rm[k, pl.ds(16, 32), :] = rho_ref[k, :, :]
    main = Level(0, [rm], [axm], [aym], [dm], [em], [gm])
    main.faces([(17, 16), (32, 16)])
    main.factor_and_first([(17, 16), (31, 16)], None, [fm], [firstm])
    main.relax([(18, 16), (30, 16)], [fm], [firstm], [vm], u=[um])
    main.residual([(19, 16), (29, 16)], [fm], [um], [resm])


def outer_kernel(grid, index_ref, near_ref, far_ref, *refs):
    fm, vm, axm, aym, dm, em, gm, rm, firstm, um, resm = refs[11:]
    ix, iy = index_ref[0], index_ref[1]
    inside = inside_of(0, ix, iy, grid + (32, 128))
    for k in range(NZ):
        for piece in PIECES:
            if piece[2] == "own":
                continue
            first, count = piece[:2]
            fm[k, pl.ds(first, count), :] = piece_of(piece, 0, k, None, near_ref, far_ref)
            x = piece_of(piece, 1, k, None, near_ref, far_ref)
            rm[k, pl.ds(first, count), :] = jnp.where(inside(first, count), x, 0.0)
    main = Level(0, [rm], [axm], [aym], [dm], [em], [gm])
    main.faces([(1, 16), (48, 16)])
    main.factor_and_first([(1, 16), (47, 16)], inside, [fm], [firstm])
    main.relax([(2, 16), (46, 16)], [fm], [firstm], [vm], u=[um])
    main.residual([(3, 16), (45, 16)], [fm], [um], [resm])


def fine_kernel(
    grid, index_ref, rm, resm, own_left, own_right, from_left_ref, from_right_ref,
    pack_ref, fh, vh, axh, ayh, dh, eh, gh, f1, v1, ax1, ay1, d1, e1, g1,
    rh, firsth, uh, rho1, first1, u1, res1,
):
    ix, iy = index_ref[0], index_ref[1]
    grid_rows, grid_lanes = grid
    inside = inside_of(0, ix, iy, grid + (32, 128), part=1)

    lane = lanes_of((16, LANES))
    for field, side in enumerate((fh, rh)):
        for first in (4, 20):
            good = inside(first, 16)
            for half in range(2):
                g = field * 2 + half
                tiles = []
                for start in (first, first + SPLIT):
                    rows = pl.ds(start, 16)
                    tiles.append(
                        [
                            from_left_ref[g, rows, :],
                            pltpu.roll(own_left[g, rows, :], 16, 1),
                            pltpu.roll(own_right[g, rows, :], 32, 1),
                            pltpu.roll(from_right_ref[g, rows, :], 48, 1),
                        ]
                    )
                for m in range(4):
                    place = (lane - 16 * m) % 128
                    spot = place % 64
                    upper, lower = [
                        jnp.where(
                            spot < 32, jnp.where(spot < 16, t[0], t[1]), jnp.where(spot < 48, t[2], t[3])
                        )
                        for t in tiles
                    ]
                    straight = jnp.where(place < 64, upper, lower)
                    crossed = jnp.where(place < 64, lower, upper)
                    if m > 0:
                        straight = pltpu.roll(straight, LANES - 16 * m, 1)
                        crossed = pltpu.roll(crossed, LANES - 16 * m, 1)
                    crossed = pltpu.roll(crossed, 64, 1)
                    for layer, y in (
                        (m, jnp.where(lane < 64, straight, crossed)),
                        (m + 4, jnp.where(lane < 64, crossed, straight)),
                    ):
                        if field == 1:
                            y = jnp.where(good, y, 0.0)
                        side[half * 8 + layer, pl.ds(first, 16), :] = y

    sides = Level(0, [rh], [axh], [ayh], [dh], [eh], [gh])
    sides.faces([(4, 16), (20, 16)])
    sides.factor_and_first([(5, 16), (19, 16)], inside, [fh], [firsth])
    sides.relax([(6, 16), (18, 16)], [fh], [firsth], [vh], u=[uh])
    sides.residual([(8, 24)], [fh], [uh], [firsth])

    main_matrix = one_hot(LANES, lambda s, t: (s // 2 + 32 == t) & (s >= 4) & (s < 124), 0.25)
    upper_matrix, lower_matrix = [
        one_hot(
            LANES,
            lambda s, t: ((s // 2 - base // 2 + 24 == t) & (s >= base + 6) & (s < base + 20))
            | ((s // 2 - base // 2 + 72 == t) & (s >= base + 44) & (s < base + 58)),
            0.25,
        )
        for base in (0, 64)
    ]
    for first in range(0, NZ, 4):
        ks = range(first, first + 4)
        for target, main, side in ((f1, resm, firsth), (rho1, rm, rh)):
            total = split_dot(stack_rows([pair_rows(main, k, 0, 32) for k in ks]), main_matrix)
            upper = split_dot(stack_rows([pair_rows(side, k, 0, 16) for k in ks]), upper_matrix)
            lower = split_dot(stack_rows([pair_rows(side, k, 8, 16) for k in ks]), lower_matrix)
            for n, k in enumerate(ks):
                target[k, pl.ds(0, 16), :] = total[n * 32 : n * 32 + 16] + upper[n * 16 : n * 16 + 16]
                target[k, pl.ds(16, 16), :] = total[n * 32 + 16 : n * 32 + 32] + lower[n * 16 : n * 16 + 16]

    middle = Level(1, [rho1], [ax1], [ay1], [d1], [e1], [g1])
    inside = inside_of(1, ix, iy, (grid_rows // 2, grid_lanes // 2, 16, 64))
    middle.faces([(4, 24), (21, 8)])
    middle.factor_and_first([(4, 24)], inside, [f1], [first1])
    middle.relax([(4, 24)], [f1], [first1], [v1], u=[u1])
    middle.residual([(8, 16)], [f1], [u1], [res1])

    pack_matrix = one_hot(
        LANES,
        lambda s, t: jnp.logical_and(
            s // 2 - 16 == (t // LANES) * 16 + t % 16, jnp.logical_and(s >= 32, s < 96)
        ),
        0.25,
        2 * LANES,
    )
    slot = lanes_of() // 16
    for field, ref in enumerate((res1, rho1)):
        wide = split_dot(stack_rows([pair_rows(ref, k, 8, 8) for k in range(NZ)]), pack_matrix)
        for side in range(2):
            for half in range(2):
                packed = None
                for q in range(8):
                    k = half * 8 + q
                    x = wide[k * 8 : (k + 1) * 8, side * LANES : (side + 1) * LANES]
                    packed = x if q == 0 else jnp.where(slot == q, x, packed)
                pack_ref[side * 4 + field * 2 + half, :, :] = packed


def coarser_kernel(
    grid, index_ref, own_left_ref, own_right_ref, from_left_ref, from_right_ref,
    pack_ref, f2, v2, ax2, ay2, d2, e2, g2, f3, v3, ax3, ay3, d3, e3, g3,
    rho2, first2, u2, res2, rho3, first3, u3, res3,
):
    ix, iy = index_ref[0], index_ref[1]
    grid_rows, grid_lanes = grid
    lane = lanes_of()
    inside = inside_of(2, ix, iy, (grid_rows // 4, grid_lanes // 4, 8, 32))

    lane40 = lanes_of((40, LANES))
    good = inside(0, 40)
    for field, target in enumerate((f2, rho2)):
        for half in range(2):
            g = field * 2 + half
            tiles = [
                from_left_ref[g],
                pltpu.roll(own_left_ref[g], 16, 1),
                pltpu.roll(own_right_ref[g], 32, 1),
                pltpu.roll(from_right_ref[g], 48, 1),
            ]
            for m in range(4):
                place = (lane40 - 16 * m) % 64
                merged = jnp.where(
                    place < 32,
                    jnp.where(place < 16, tiles[0], tiles[1]),
                    jnp.where(place < 48, tiles[2], tiles[3]),
                )
                for q in (m, m + 4):
                    y = merged if q == 0 else pltpu.roll(merged, LANES - 16 * q, 1)
                    if field == 1:
                        y = jnp.where(good, y, 0.0)
                    target[half * 8 + q, :, :] = y

    level2 = Level(2, [rho2], [ax2], [ay2], [d2], [e2], [g2])
    level2.faces([(4, 16, 2), (29, 8)])
    level2.factor_and_first([(4, 16, 2)], inside, [f2], [first2])
    level2.relax([(4, 16, 2)], [f2], [first2], [v2], u=[u2])
    level2.residual([(4, 16, 2)], [f2], [u2], [res2])

    halve = one_hot(LANES, lambda s, t: s // 2 == t, 0.25)
    for ref, target, first, count in ((res2, f3, 4, 16), (rho2, rho3, 4, 16)):
        total = split_dot(stack_rows([pair_rows(ref, k, first, count) for k in range(NZ)]), halve)
        for k in range(NZ):
            target[k, pl.ds(first // 2, count), :] = total[k * count : (k + 1) * count]

    level3 = Level(3, [rho3], [ax3], [ay3], [d3], [e3], [g3])
    inside = inside_of(3, ix, iy, (grid_rows // 8, grid_lanes // 8, 4, 16))
    level3.faces([(2, 16)])
    level3.factor_and_first([(2, 16)], inside, [f3], [first3])
    level3.relax([(2, 16)], [f3], [first3], [v3], u=[u3])
    level3.residual([(6, 8)], [f3], [u3], [res3])

    spread = one_hot(
        LANES,
        lambda s, t: jnp.logical_and(s // 2 - 4 == t % 8, jnp.logical_and(s >= 8, s < 24)),
        0.25,
    )
    for field, ref in enumerate((res3, rho3)):
        total = split_dot(stack_rows([pair_rows(ref, k, 8, 8) for k in range(NZ)]), spread)
        merged = total[0:8]
        for k in range(1, NZ):
            merged = jnp.where(lane // 8 == k, total[k * 8 : (k + 1) * 8], merged)
        pack_ref[pl.ds(2 * field, 2), :] = pltpu.roll(merged, 8 * iy, 1)[0:2]


def prolong(coarse, first_row, count, ref, old, target, target_row, matrix):
    rows = stack_rows([coarse(k) for k in range(NZ)])
    for part in range(len(target)):
        fine = split_dot(rows, matrix[part])
        for k in range(NZ):
            x = fine[k * count : (k + 1) * count]
            for odd in range(2):
                where = pl.ds(target_row + odd, count, stride=2)
                target[part].at[k][where, :] = old[part].at[k][where, :] + x


def top_kernel(
    grid, tiles, index_ref, gathered, fm, vm, axm, aym, dm, em, gm, fh, vh, axh, ayh, dh, eh, gh,
    f1, v1, ax1, ay1, d1, e1, g1, f2, v2, ax2, ay2, d2, e2, g2, f3, v3, ax3, ay3, d3, e3, g3,
    out_ref,
    rho4, f4, ax4, ay4, d4, e4, g4, c4, a4, b4, v4, va3, vb3, va2, vb2, va1, vb1, vam, vah, vbm, vbh,
):
    ix, iy = index_ref[0], index_ref[1]
    grid_rows, grid_lanes = grid
    lane = lanes_of()
    rows4 = grid_rows // 16
    tiles_x, tiles_y = tiles

    zero = jnp.zeros((8, LANES), jnp.float32)
    for ref in (rho4, v4.at[0], v4.at[1]):
        for k in range(NZ):
            ref[k, pl.ds(0, 8), :] = zero
            ref[k, pl.ds(8 + rows4, 8), :] = zero

    count = min(8, tiles_x)
    for field, target in enumerate((f4, rho4)):
        for r in range(2):
            for base in range(0, tiles_x, count):
                xs = [
                    gathered[pl.ds((base * tiles_y + t) * 4 + field * 2 + r, count, stride=4 * tiles_y), :]
                    for t in range(16)
                ]
                block = lanes_of((count, LANES)) // 8
                for bit in (1, 2, 4, 8):
                    moved = (block & bit) != 0
                    xs = [jnp.where(moved, xs[(i + bit) % 16], xs[i]) for i in range(16)]
                for k in range(NZ):
                    x = xs[-k % 16]
                    x = x if k == 0 else pltpu.roll(x, LANES - 8 * k, 1)
                    target.at[k][pl.ds(8 + 2 * base + r, count, stride=2), :] = x

    scale = spacing(4)
    h = min(32, rows4)
    first_lane, last_lane = lanes_of((h, LANES)) == 0, lanes_of((h, LANES)) == LANES - 1
    starts = list(range(8, 8 + rows4, h))

    def faces_x(r, h):
        for k in range(NZ):
            total = rho4[k, pl.ds(r, h), :] + rho4[k, pl.ds(r - 1, h), :]
            ax4[k, pl.ds(r, h), :] = scale * rcp(jnp.maximum(total, TINY))

    for r in starts:
        faces_x(r, h)
    faces_x(rows4 + 1, 8)

    def first_sweep(r):
        rho = rho4[0, pl.ds(r, h), :]
        upper = (2.0 * VERTICAL) * rcp(rho)
        row = rows_of((h, LANES)) + r
        partial, ratio = [], None
        for k in range(NZ):
            here = rho4[k, pl.ds(r, h), :]
            left = jnp.where(first_lane, 0.0, pltpu.roll(here, 1, 1))
            ay = scale * rcp(here + left)
            right = jnp.where(last_lane, scale * rcp(here), pltpu.roll(ay, LANES - 1, 1))
            ay4[k, pl.ds(r, h), :] = jnp.where(first_lane, 0.0, ay)
            up, down = ax4[k, pl.ds(r, h), :], ax4[k, pl.ds(r + 1, h), :]
            center = up + down + ay + right + upper
            across = jnp.where(first_lane, ay, 0.0) + jnp.where(last_lane, right, 0.0)
            along = jnp.where(row == 8, up, 0.0) + jnp.where(row == 7 + rows4, down, 0.0)
            b4[k, pl.ds(r, h), :] = across + along
            if k + 1 < NZ:
                lower = (2.0 * VERTICAL) * rcp(here + rho4[k + 1, pl.ds(r, h), :])
                center = center + lower
            c4[k, pl.ds(r, h), :] = center
            a4[k, pl.ds(r, h), :] = upper
            pivot = center if k == 0 else center - upper * ratio
            inverse = rcp(pivot)
            scaled = 0.8 * inverse
            d4[k, pl.ds(r, h), :] = scaled
            value = scaled * f4[k, pl.ds(r, h), :]
            if k > 0:
                weight = upper * inverse
                e4[k, pl.ds(r, h), :] = weight
                value = value + weight * partial[-1]
            partial.append(value)
            if k + 1 < NZ:
                ratio = lower * inverse
                g4[k, pl.ds(r, h), :] = ratio
                upper = lower
        w = partial[-1]
        v4[0, NZ - 1, pl.ds(r, h), :] = w
        for k in range(NZ - 2, -1, -1):
            w = partial[k] + g4[k, pl.ds(r, h), :] * w
            v4[0, k, pl.ds(r, h), :] = w

    for r in starts:
        first_sweep(r)

    def pulled4(v, k, r):
        here = v[k, pl.ds(r, h), :]
        ay = ay4[k, pl.ds(r, h), :]
        return (
            f4[k, pl.ds(r, h), :]
            + ax4[k, pl.ds(r, h), :] * v[k, pl.ds(r - 1, h), :]
            + ax4[k, pl.ds(r + 1, h), :] * v[k, pl.ds(r + 1, h), :]
            + ay * pltpu.roll(here, 1, 1)
            + pltpu.roll(ay * here, LANES - 1, 1)
        )

    def sweep(v, out):
        for r in starts:
            partial = []
            for k in range(NZ):
                value = d4[k, pl.ds(r, h), :] * pulled4(v, k, r)
                if k > 0:
                    value = value + e4[k, pl.ds(r, h), :] * partial[-1]
                partial.append(value)
            w = None
            for k in range(NZ - 1, -1, -1):
                w = partial[k] if w is None else partial[k] + g4[k, pl.ds(r, h), :] * w
                out[k, pl.ds(r, h), :] = 0.2 * v[k, pl.ds(r, h), :] + w

    def one_sweep(number, carry):
        sweep(v4.at[number % 2], v4.at[1 - number % 2])
        return carry

    lax.fori_loop(0, SWEEPS - 1, one_sweep, 0)
    final = v4.at[(SWEEPS - 1) % 2]

    shifts, flux = [], [None] * len(starts)
    for k in range(NZ):
        left_over, weights = None, None
        for n, r in enumerate(starts):
            v = final[k, pl.ds(r, h), :]
            part = f4[k, pl.ds(r, h), :] - b4[k, pl.ds(r, h), :] * v
            part = part - (a4[0, pl.ds(r, h), :] * v if k == 0 else flux[n])
            if k + 1 < NZ:
                flux[n] = a4[k + 1, pl.ds(r, h), :] * (final[k + 1, pl.ds(r, h), :] - v)
                part = part + flux[n]
            center = c4[k, pl.ds(r, h), :]
            left_over = part if left_over is None else left_over + part
            weights = center if weights is None else weights + center
        raised = jnp.sum(left_over, axis=(0, 1), keepdims=True)
        shifts.append(raised / jnp.sum(weights, axis=(0, 1), keepdims=True))

    row = rows_of() + (ix * 2 - 4)
    column = lane + (iy * 8 - 4)
    good = jnp.logical_and(
        jnp.logical_and(row >= 0, row < rows4),
        jnp.logical_and(jnp.logical_and(column >= 0, column < grid_lanes // 16), lane < 16),
    )
    amount = lax.rem(132 - iy * 8, LANES)

    def coarsest(k):
        x = final[k, pl.ds(4 + 2 * ix, 8), :] + shifts[k]
        return jnp.where(good, pltpu.roll(x, amount, 1), 0.0)

    repeat = one_hot(LANES, lambda s, t: s == t // 2, 1.0)
    prolong(coarsest, 0, 8, None, [v3], [va3], 0, [repeat])
    level3 = Level(3, None, [ax3], [ay3], [d3], [e3], [g3])
    level3.relax([(2, 16)], [f3], [va3], [vb3])
    level3.relax([(6, 8)], [f3], [vb3], [va3])

    prolong(lambda k: va3[k, pl.ds(6, 8), :], 0, 8, None, [v2], [va2], 12, [repeat])
    level2 = Level(2, None, [ax2], [ay2], [d2], [e2], [g2])
    level2.relax([(12, 16)], [f2], [va2], [vb2])
    level2.relax([(12, 16)], [f2], [vb2], [va2])

    prolong(lambda k: va2[k, pl.ds(12, 16), :], 0, 16, None, [v1], [va1], 0, [repeat])
    level1 = Level(1, None, [ax1], [ay1], [d1], [e1], [g1])
    level1.relax([(4, 24)], [f1], [va1], [vb1])
    level1.relax([(4, 24)], [f1], [vb1], [va1])

    to_main = one_hot(LANES, lambda s, t: s == t // 2 + 32, 1.0)
    prolong(lambda k: va1[k, pl.ds(4, 24), :], 0, 24, None, [vm], [vam], 8, [to_main])
    lane = lanes_of((16, LANES))
    to_upper, to_lower = [
        one_hot(
            LANES,
            lambda s, t: ((t < base + 32) & (t >= base) & (s == (t - base) // 2 + 24))
            | ((t >= base + 32) & (t < base + 64) & (s == (t - base) // 2 + 72)),
            1.0,
        )
        for base in (0, 64)
    ]
    upper = split_dot(stack_rows([va1[k, pl.ds(2, 16), :] for k in range(NZ)]), to_upper)
    lower = split_dot(stack_rows([va1[k, pl.ds(2 + SPLIT // 2, 16), :] for k in range(NZ)]), to_lower)
    for k in range(NZ):
        x = jnp.where(lane < 64, upper[k * 16 : k * 16 + 16], lower[k * 16 : k * 16 + 16])
        for odd in range(2):
            where = pl.ds(4 + odd, 16, stride=2)
            vah.at[k][where, :] = vh.at[k][where, :] + x
    sides = Level(0, None, [axh], [ayh], [dh], [eh], [gh])
    sides.relax([(7, 16), (17, 16)], [fh], [vah], [vbh])
    sides.relax([(8, 24)], [fh], [vbh], [vah])
    main = Level(0, None, [axm], [aym], [dm], [em], [gm])
    main.relax([(15, 16, 2), (41, 8)], [fm], [vam], [vbm])
    main.relax([(16, 16, 2)], [fm], [vbm], [vam])
    for k in range(NZ):
        for row, start, low, high in ((0, 16, 112, 80), (16, 16 - SPLIT + 16, 48, 16)):
            side = vah[k, pl.ds(start, 16), :]
            side = jnp.where(lane < 64, pltpu.roll(side, low, 1), pltpu.roll(side, high, 1))
            x = vam[k, pl.ds(16 + row, 16), :]
            out_ref[k, pl.ds(row, 16), :] = jnp.where(jnp.logical_or(lane < 4, lane >= 124), side, x)


def ring(x, axis, step):
    size = lax.axis_size(axis)
    return lax.ppermute(x, axis, [(i, (i + step) % size) for i in range(size)])


def gather(x, axis):
    size = lax.axis_size(axis)
    blocks = jnp.broadcast_to(x[None], (size,) + x.shape)
    return lax.all_to_all(blocks, axis, 0, 0).reshape(size * x.shape[0], LANES)


def array(*shape):
    return jax.ShapeDtypeStruct(shape, jnp.float32)


def call(kernel, name, outs, scratch, index, *operands, aliases=None, cost=4000000):
    vmem = pl.BlockSpec(memory_space=pltpu.VMEM)
    ins = [vmem] * len(operands)
    if index is not None:
        ins, operands = [pl.BlockSpec(memory_space=pltpu.SMEM)] + ins, (index,) + operands
    return pl.pallas_call(
        kernel,
        out_shape=outs,
        in_specs=ins,
        out_specs=[vmem] * len(outs),
        scratch_shapes=[pltpu.VMEM(shape, jnp.float32) for shape in scratch],
        compiler_params=pltpu.CompilerParams(vmem_limit_bytes=VMEM_BYTES),
        input_output_aliases=aliases or {},
        cost_estimate=pl.CostEstimate(flops=cost, bytes_accessed=cost, transcendentals=0),
        name=name,
    )(*operands)


def solution(mesh):
    tiles_x, tiles_y = mesh.shape["gx"], mesh.shape["gy"]
    grid = (32 * tiles_x, 128 * tiles_y)
    big = [array(NZ, ROWS[level], LANES) for level in range(4)]

    def on_device(source, rho):
        index = jnp.stack([lax.axis_index("gx"), lax.axis_index("gy")]).astype(jnp.int32)

        both = jnp.concatenate([source, rho], axis=0).transpose(1, 0, 2)
        lows = both[:REACH].reshape(REACH * 2 * NZ, LANES)
        highs = both[-REACH:].reshape(REACH * 2 * NZ, LANES)
        up = ring(highs, "gx", 1)
        dn = ring(lows, "gx", -1)
        s0, s1, s2, s3 = [x.shape for x in big]
        sh = (NZ, SIDE_ROWS, LANES)
        inner = call(inner_kernel, "inner", [big[0]] * 11, [], None, source, rho)
        strip = array(4, ROWS[0], LANES)
        own_strips = call(own_edges_kernel, "own_edges", [strip, strip], [], None, source, rho)
        lefts, rights = call(
            edges_kernel, "edges", [strip, strip], [], None, up, dn, *own_strips, aliases={2: 0, 3: 1}
        )
        from_left_strip = ring(rights, "gy", 1)
        from_right_strip = ring(lefts, "gy", -1)
        main = call(
            lambda *refs: outer_kernel(grid, *refs), "outer", [big[0]] * 11, [], index, up, dn, *inner,
            aliases={3 + n: n for n in range(11)},
        )
        main_state, rho_main, residual_main = main[:7], main[7], main[10]
        fine = call(
            lambda *refs: fine_kernel(grid, *refs),
            "fine",
            [array(8, 8, LANES)] + [array(*sh)] * 7 + [big[1]] * 7,
            [sh] * 3 + [s1] * 4,
            index, rho_main, residual_main, lefts, rights, from_left_strip, from_right_strip,
        )
        tile = fine[0]
        pieces = [ring(tile, "gx", 2), ring(tile, "gx", 1), tile, ring(tile, "gx", -1), ring(tile, "gx", -2)]
        own_left = jnp.concatenate([piece[:4] for piece in pieces], axis=1)
        own_right = jnp.concatenate([piece[4:] for piece in pieces], axis=1)
        from_left_column = ring(own_right, "gy", 1)
        from_right_column = ring(own_left, "gy", -1)
        coarser = call(
            lambda *refs: coarser_kernel(grid, *refs),
            "coarser",
            [array(4, LANES)] + [big[2]] * 7 + [big[3]] * 7,
            [s2] * 4 + [s3] * 4,
            index, own_left, own_right, from_left_column, from_right_column,
        )
        gathered = gather(gather(coarser[0], "gy"), "gx")

        s4 = (NZ, 16 + 2 * tiles_x, LANES)
        (pressure,) = call(
            lambda *refs: top_kernel(grid, (tiles_x, tiles_y), *refs),
            "top",
            [array(NZ, 32, LANES)],
            [s4] * 10 + [(2,) + s4] + [s3] * 2 + [s2] * 2 + [s1] * 2 + [s0, sh] * 2,
            index, gathered, *main_state, *fine[1:], *coarser[1:],
        )
        return pressure

    return jax.shard_map(
        on_device,
        mesh=mesh,
        in_specs=(P(None, "gx", "gy"), P(None, "gx", "gy")),
        out_specs=P(None, "gx", "gy"),
        check_vma=False,
    )
```

```python
import jax
import jax.numpy as jnp
from jax import lax
from jax.experimental import pallas as pl
from jax.experimental.pallas import tpu as pltpu
from jax.sharding import PartitionSpec as P

NZ = 16
LANES = 128
SWEEPS = 6
VERTICAL = 0.015625
TINY = 2.0**-20
VMEM_BYTES = 16 * 1024 * 1024

SPLIT = 24
SIDE_ROWS = 40
ROW0 = (16, 8, 16, 8)
ROWS = (64, 32, 40, 24)
LANE0 = (0, 32, 16, 8)


def spacing(level):
    return 2.0 * 0.25**level


def lanes_of(shape=(8, LANES)):
    return lax.broadcasted_iota(jnp.int32, shape, 1)


def rows_of(shape=(8, LANES)):
    return lax.broadcasted_iota(jnp.int32, shape, 0)


def rcp(x):
    guess = pl.reciprocal(x, approx=True)
    return guess * (2.0 - x * guess)


def from_left(xs):
    rolled = [pltpu.roll(x, 1, 1) for x in xs]
    if len(xs) == 1:
        return rolled
    edge = lanes_of(xs[0].shape) == 0
    return [jnp.where(edge, rolled[1], rolled[0]), jnp.where(edge, rolled[0], rolled[1])]


def from_right(xs):
    rolled = [pltpu.roll(x, LANES - 1, 1) for x in xs]
    if len(xs) == 1:
        return rolled
    edge = lanes_of(xs[0].shape) == LANES - 1
    return [jnp.where(edge, rolled[1], rolled[0]), jnp.where(edge, rolled[0], rolled[1])]


def split_dot(x, matrix, pieces=2):
    total = None
    for piece in range(pieces):
        part = x.astype(jnp.bfloat16)
        product = jnp.dot(part, matrix, preferred_element_type=jnp.float32)
        total = product if total is None else total + product
        if piece + 1 < pieces:
            x = x - part.astype(jnp.float32)
    return total


def one_hot(rows, test, value, lanes=LANES):
    shape = (rows, lanes)
    source, target = lax.broadcasted_iota(jnp.int32, shape, 0), lax.broadcasted_iota(jnp.int32, shape, 1)
    return jnp.where(test(source, target), value, 0.0).astype(jnp.bfloat16)


def run_blocks(blocks, body):
    for block in blocks:
        if len(block) == 2:
            body(*block)
        else:
            first, height, count = block

            def step(index, carry):
                body(first + height * index, height)
                return carry

            lax.fori_loop(0, count, step, 0)


TWISTED = (0, 2, 3)


class Level:
    def __init__(self, level, rho, ax, ay, d, e, g):
        self.level, self.rho, self.ax, self.ay, self.d, self.e, self.g = level, rho, ax, ay, d, e, g
        self.parts = range(len(ax))
        self.twist = level in TWISTED
        ends = [n if side == 0 else NZ - 1 - n for n in range(NZ // 2) for side in range(2)]
        self.order = ends if self.twist else list(range(NZ))

    def faces(self, blocks):
        scale = spacing(self.level)

        def body(r, h):
            for k in range(NZ):
                here = [ref[k, pl.ds(r, h), :] for ref in self.rho]
                above = [ref[k, pl.ds(r - 1, h), :] for ref in self.rho]
                left = from_left(here)
                for p in self.parts:
                    self.ax[p][k, pl.ds(r, h), :] = scale * rcp(jnp.maximum(here[p] + above[p], TINY))
                    self.ay[p][k, pl.ds(r, h), :] = scale * rcp(jnp.maximum(here[p] + left[p], TINY))

        run_blocks(blocks, body)

    def before(self, k):
        if self.twist and k >= 8:
            return k + 1 if k + 1 < NZ else None
        return k - 1 if k > 0 else None

    def substitute(self, p, r, h, partial, emit):
        def weight(k):
            return self.g[p][k, pl.ds(r, h), :]

        if not self.twist:
            w = partial[NZ - 1]
            emit(NZ - 1, w)
            for k in range(NZ - 2, -1, -1):
                w = partial[k] + weight(k) * w
                emit(k, w)
            return
        w = self.e[p][0, pl.ds(r, h), :] * (partial[7] + weight(7) * partial[8])
        emit(7, w)
        x = partial[8] + weight(8) * w
        emit(8, x)
        for k in range(6, -1, -1):
            w = partial[k] + weight(k) * w
            emit(k, w)
            x = partial[15 - k] + weight(15 - k) * x
            emit(15 - k, x)

    def factor_and_first(self, blocks, inside, f, v):
        def body(r, h):
            masks = None if inside is None else [inside(r, h) for p in self.parts]
            upper = {}

            def upper_at(k):
                if k not in upper:
                    total = [ref[k, pl.ds(r, h), :] for ref in self.rho]
                    if k > 0:
                        total = [x + ref[k - 1, pl.ds(r, h), :] for x, ref in zip(total, self.rho)]
                    upper[k] = [(2.0 * VERTICAL) * rcp(jnp.maximum(x, TINY)) for x in total]
                return upper[k]

            partial = [[None] * NZ for p in self.parts]
            back = {}
            for k in self.order:
                above = upper_at(k)
                below = upper_at(k + 1) if k + 1 < NZ else None
                ay = [ref[k, pl.ds(r, h), :] for ref in self.ay]
                right = from_right(ay)
                upwards = self.twist and k >= 8
                before = self.before(k)
                for p in self.parts:
                    center = (
                        self.ax[p][k, pl.ds(r, h), :]
                        + self.ax[p][k, pl.ds(r + 1, h), :]
                        + ay[p]
                        + right[p]
                        + above[p]
                    )
                    if k + 1 < NZ:
                        center = center + below[p]
                    toward, away = (below, above) if upwards else (above, below)
                    pivot = center if before is None else center - toward[p] * back[before, p]
                    inverse = rcp(pivot) if masks is None else jnp.where(masks[p], rcp(pivot), 0.0)
                    scaled = 0.8 * inverse
                    self.d[p][k, pl.ds(r, h), :] = scaled
                    value = scaled * f[p][k, pl.ds(r, h), :]
                    if before is not None:
                        weight = toward[p] * inverse
                        self.e[p][k, pl.ds(r, h), :] = weight
                        value = value + weight * partial[p][before]
                    partial[p][k] = value
                    if away is not None:
                        back[k, p] = away[p] * inverse
                        self.g[p][k, pl.ds(r, h), :] = back[k, p]

            for p in self.parts:
                if self.twist:
                    self.e[p][0, pl.ds(r, h), :] = rcp(1.0 - back[7, p] * back[8, p])

                def emit(k, w):
                    v[p][k, pl.ds(r, h), :] = w

                self.substitute(p, r, h, partial[p], emit)

        run_blocks(blocks, body)

    def pull(self, v, k, r, h, wanted):
        here = [ref[k, pl.ds(r, h), :] for ref in v]
        ay = [ref[k, pl.ds(r, h), :] for ref in self.ay]
        left = from_left(here)
        right = from_right([a * x for a, x in zip(ay, here)])
        return [
            self.ax[p][k, pl.ds(r, h), :] * v[p][k, pl.ds(r - 1, h), :]
            + self.ax[p][k, pl.ds(r + 1, h), :] * v[p][k, pl.ds(r + 1, h), :]
            + ay[p] * left[p]
            + right[p]
            for p in wanted
        ]

    def relax(self, blocks, f, v, out, u=None):
        def body(r, h):
            partial = [[None] * NZ for p in self.parts]
            for k in self.order:
                pulls = self.pull(v, k, r, h, self.parts)
                before = self.before(k)
                for p in self.parts:
                    value = self.d[p][k, pl.ds(r, h), :] * (f[p][k, pl.ds(r, h), :] + pulls[p])
                    if before is not None:
                        value = value + self.e[p][k, pl.ds(r, h), :] * partial[p][before]
                    partial[p][k] = value

            for p in self.parts:

                def emit(k, w):
                    old = v[p][k, pl.ds(r, h), :]
                    out[p][k, pl.ds(r, h), :] = 0.2 * old + w
                    if u is not None:
                        u[p][k, pl.ds(r, h), :] = w - 0.6 * old

                self.substitute(p, r, h, partial[p], emit)

        run_blocks(blocks, body)

    def residual(self, blocks, f, u, out):
        def body(r, h):
            for k in range(NZ):
                pulls = self.pull(u, k, r, h, self.parts)
                for p in self.parts:
                    out[p][k, pl.ds(r, h), :] = 0.04 * f[p][k, pl.ds(r, h), :] + pulls[p]

        run_blocks(blocks, body)


def inside_of(level, ix, iy, shape, part=0):
    grid_rows, grid_lanes, tile_rows, tile_lanes = shape

    def inside(r, h):
        row, lane = rows_of((h, LANES)) + (r + ix * tile_rows - ROW0[level]), lanes_of((h, LANES))
        if level == 0 and part == 1:
            row = row + jnp.where(lane < 64, 0, SPLIT)
            lane = lane % 64
        good = jnp.logical_and(row >= 0, row < grid_rows)
        if level == 0 and part == 0:
            return good
        if level == 0:
            column = iy * tile_lanes + jnp.where(lane < 32, lane - 16, lane + 80)
            side = jnp.logical_and(column >= 0, column < grid_lanes)
        else:
            column = iy * tile_lanes + lane - LANE0[level]
            side = jnp.logical_and(column >= 0, column < grid_lanes)
        return jnp.logical_and(good, side)

    return inside


def pair_rows(ref, k, start, count):
    layer = ref.at[k]
    return layer[pl.ds(start, count, stride=2), :] + layer[pl.ds(start + 1, count, stride=2), :]


def stack_rows(blocks):
    return jnp.concatenate(blocks, axis=0)


PIECES = ((5, 8, "up", 0), (8, 8, "up", 3), (16, 32, "own", 0), (48, 8, "down", 0), (51, 8, "down", 3))
REACH = 11


def piece_of(piece, field, k, own, up, down):
    first, count, source, start = piece
    if source == "own":
        return own[k, :, :]
    ref = up if source == "up" else down
    return ref[pl.ds(start * 2 * NZ + field * NZ + k, count, stride=2 * NZ), :]


def pack_rows(piece, sources, left_ref, right_ref):
    first, count = piece[:2]
    slot = lanes_of((count, LANES)) // 16
    for field in range(2):
        for half in range(2):
            lefts, rights = None, None
            for q in range(8):
                x = piece_of(piece, field, half * 8 + q, sources[field], *sources[2:])
                a = x if q == 0 else pltpu.roll(x, 16 * q, 1)
                b = pltpu.roll(x, 16 * q + 16, 1) if q < 7 else x
                lefts = a if q == 0 else jnp.where(slot == q, a, lefts)
                rights = b if q == 0 else jnp.where(slot == q, b, rights)
            left_ref[field * 2 + half, pl.ds(first, count), :] = lefts
            right_ref[field * 2 + half, pl.ds(first, count), :] = rights


def own_edges_kernel(f_ref, rho_ref, left_ref, right_ref):
    pack_rows(PIECES[2], (f_ref, rho_ref, None, None), left_ref, right_ref)


def edges_kernel(up_ref, dn_ref, own_left, own_right, left_ref, right_ref):
    left_ref[:, pl.ds(16, 32), :] = own_left[:, pl.ds(16, 32), :]
    right_ref[:, pl.ds(16, 32), :] = own_right[:, pl.ds(16, 32), :]
    for piece in PIECES:
        if piece[2] != "own":
            pack_rows(piece, (None, None, up_ref, dn_ref), left_ref, right_ref)


def main_kernel(
    grid, index_ref, f_ref, rho_ref, up_ref, dn_ref,
    fm, vm, axm, aym, dm, em, gm, rm, resm,
    firstm, um,
):
    ix, iy = index_ref[0], index_ref[1]
    inside = inside_of(0, ix, iy, grid + (32, 128))
    for field, (own, target) in enumerate(((f_ref, fm), (rho_ref, rm))):
        for k in range(NZ):
            for piece in PIECES:
                first, count, source, _ = piece
                x = piece_of(piece, field, k, own, up_ref, dn_ref)
                if field == 1 and source != "own":
                    x = jnp.where(inside(first, count), x, 0.0)
                target[k, pl.ds(first, count), :] = x
    main = Level(0, [rm], [axm], [aym], [dm], [em], [gm])
    main.faces([(6, 16, 3), (51, 8)])
    main.factor_and_first([(6, 16, 3), (50, 8)], inside, [fm], [firstm])
    main.relax([(7, 16, 3), (49, 8)], [fm], [firstm], [vm], u=[um])
    main.residual([(8, 16, 3)], [fm], [um], [resm])


def fine_kernel(
    grid, index_ref, rm, resm, own_left, own_right, from_left_ref, from_right_ref,
    pack_ref, fh, vh, axh, ayh, dh, eh, gh, f1, v1, ax1, ay1, d1, e1, g1,
    rh, firsth, uh, rho1, first1, u1, res1,
):
    ix, iy = index_ref[0], index_ref[1]
    grid_rows, grid_lanes = grid
    inside = inside_of(0, ix, iy, grid + (32, 128), part=1)

    lane = lanes_of((16, LANES))
    for field, side in enumerate((fh, rh)):
        for first in (4, 20):
            good = inside(first, 16)
            for half in range(2):
                g = field * 2 + half
                tiles = []
                for start in (first, first + SPLIT):
                    rows = pl.ds(start, 16)
                    tiles.append(
                        [
                            from_left_ref[g, rows, :],
                            pltpu.roll(own_left[g, rows, :], 16, 1),
                            pltpu.roll(own_right[g, rows, :], 32, 1),
                            pltpu.roll(from_right_ref[g, rows, :], 48, 1),
                        ]
                    )
                for m in range(4):
                    place = (lane - 16 * m) % 128
                    spot = place % 64
                    upper, lower = [
                        jnp.where(
                            spot < 32, jnp.where(spot < 16, t[0], t[1]), jnp.where(spot < 48, t[2], t[3])
                        )
                        for t in tiles
                    ]
                    straight = jnp.where(place < 64, upper, lower)
                    crossed = jnp.where(place < 64, lower, upper)
                    if m > 0:
                        straight = pltpu.roll(straight, LANES - 16 * m, 1)
                        crossed = pltpu.roll(crossed, LANES - 16 * m, 1)
                    crossed = pltpu.roll(crossed, 64, 1)
                    for layer, y in (
                        (m, jnp.where(lane < 64, straight, crossed)),
                        (m + 4, jnp.where(lane < 64, crossed, straight)),
                    ):
                        if field == 1:
                            y = jnp.where(good, y, 0.0)
                        side[half * 8 + layer, pl.ds(first, 16), :] = y

    sides = Level(0, [rh], [axh], [ayh], [dh], [eh], [gh])
    sides.faces([(4, 16), (20, 16)])
    sides.factor_and_first([(5, 16), (19, 16)], inside, [fh], [firsth])
    sides.relax([(6, 16), (18, 16)], [fh], [firsth], [vh], u=[uh])
    sides.residual([(8, 24)], [fh], [uh], [firsth])

    main_matrix = one_hot(LANES, lambda s, t: (s // 2 + 32 == t) & (s >= 4) & (s < 124), 0.25)
    upper_matrix, lower_matrix = [
        one_hot(
            LANES,
            lambda s, t: ((s // 2 - base // 2 + 24 == t) & (s >= base + 6) & (s < base + 20))
            | ((s // 2 - base // 2 + 72 == t) & (s >= base + 44) & (s < base + 58)),
            0.25,
        )
        for base in (0, 64)
    ]
    for first in range(0, NZ, 4):
        ks = range(first, first + 4)
        for target, main, side in ((f1, resm, firsth), (rho1, rm, rh)):
            total = split_dot(stack_rows([pair_rows(main, k, 0, 32) for k in ks]), main_matrix)
            upper = split_dot(stack_rows([pair_rows(side, k, 0, 16) for k in ks]), upper_matrix)
            lower = split_dot(stack_rows([pair_rows(side, k, 8, 16) for k in ks]), lower_matrix)
            for n, k in enumerate(ks):
                target[k, pl.ds(0, 16), :] = total[n * 32 : n * 32 + 16] + upper[n * 16 : n * 16 + 16]
                target[k, pl.ds(16, 16), :] = total[n * 32 + 16 : n * 32 + 32] + lower[n * 16 : n * 16 + 16]

    middle = Level(1, [rho1], [ax1], [ay1], [d1], [e1], [g1])
    inside = inside_of(1, ix, iy, (grid_rows // 2, grid_lanes // 2, 16, 64))
    middle.faces([(4, 24), (21, 8)])
    middle.factor_and_first([(4, 24)], inside, [f1], [first1])
    middle.relax([(4, 24)], [f1], [first1], [v1], u=[u1])
    middle.residual([(8, 16)], [f1], [u1], [res1])

    pack_matrix = one_hot(
        LANES,
        lambda s, t: jnp.logical_and(
            s // 2 - 16 == (t // LANES) * 16 + t % 16, jnp.logical_and(s >= 32, s < 96)
        ),
        0.25,
        2 * LANES,
    )
    slot = lanes_of() // 16
    for field, ref in enumerate((res1, rho1)):
        wide = split_dot(stack_rows([pair_rows(ref, k, 8, 8) for k in range(NZ)]), pack_matrix)
        for side in range(2):
            for half in range(2):
                packed = None
                for q in range(8):
                    k = half * 8 + q
                    x = wide[k * 8 : (k + 1) * 8, side * LANES : (side + 1) * LANES]
                    packed = x if q == 0 else jnp.where(slot == q, x, packed)
                pack_ref[side * 4 + field * 2 + half, :, :] = packed


def coarser_kernel(
    grid, index_ref, own_left_ref, own_right_ref, from_left_ref, from_right_ref,
    pack_ref, f2, v2, ax2, ay2, d2, e2, g2, f3, v3, ax3, ay3, d3, e3, g3,
    rho2, first2, u2, res2, rho3, first3, u3, res3,
):
    ix, iy = index_ref[0], index_ref[1]
    grid_rows, grid_lanes = grid
    lane = lanes_of()
    inside = inside_of(2, ix, iy, (grid_rows // 4, grid_lanes // 4, 8, 32))

    lane40 = lanes_of((40, LANES))
    good = inside(0, 40)
    for field, target in enumerate((f2, rho2)):
        for half in range(2):
            g = field * 2 + half
            tiles = [
                from_left_ref[g],
                pltpu.roll(own_left_ref[g], 16, 1),
                pltpu.roll(own_right_ref[g], 32, 1),
                pltpu.roll(from_right_ref[g], 48, 1),
            ]
            for m in range(4):
                place = (lane40 - 16 * m) % 64
                merged = jnp.where(
                    place < 32,
                    jnp.where(place < 16, tiles[0], tiles[1]),
                    jnp.where(place < 48, tiles[2], tiles[3]),
                )
                for q in (m, m + 4):
                    y = merged if q == 0 else pltpu.roll(merged, LANES - 16 * q, 1)
                    if field == 1:
                        y = jnp.where(good, y, 0.0)
                    target[half * 8 + q, :, :] = y

    level2 = Level(2, [rho2], [ax2], [ay2], [d2], [e2], [g2])
    level2.faces([(4, 16, 2), (29, 8)])
    level2.factor_and_first([(4, 16, 2)], inside, [f2], [first2])
    level2.relax([(4, 16, 2)], [f2], [first2], [v2], u=[u2])
    level2.residual([(4, 16, 2)], [f2], [u2], [res2])

    halve = one_hot(LANES, lambda s, t: s // 2 == t, 0.25)
    for ref, target, first, count in ((res2, f3, 4, 16), (rho2, rho3, 4, 16)):
        total = split_dot(stack_rows([pair_rows(ref, k, first, count) for k in range(NZ)]), halve)
        for k in range(NZ):
            target[k, pl.ds(first // 2, count), :] = total[k * count : (k + 1) * count]

    level3 = Level(3, [rho3], [ax3], [ay3], [d3], [e3], [g3])
    inside = inside_of(3, ix, iy, (grid_rows // 8, grid_lanes // 8, 4, 16))
    level3.faces([(2, 16)])
    level3.factor_and_first([(2, 16)], inside, [f3], [first3])
    level3.relax([(2, 16)], [f3], [first3], [v3], u=[u3])
    level3.residual([(6, 8)], [f3], [u3], [res3])

    spread = one_hot(
        LANES,
        lambda s, t: jnp.logical_and(s // 2 - 4 == t % 8, jnp.logical_and(s >= 8, s < 24)),
        0.25,
    )
    for field, ref in enumerate((res3, rho3)):
        total = split_dot(stack_rows([pair_rows(ref, k, 8, 8) for k in range(NZ)]), spread)
        merged = total[0:8]
        for k in range(1, NZ):
            merged = jnp.where(lane // 8 == k, total[k * 8 : (k + 1) * 8], merged)
        pack_ref[pl.ds(2 * field, 2), :] = pltpu.roll(merged, 8 * iy, 1)[0:2]


def prolong(coarse, first_row, count, ref, old, target, target_row, matrix):
    rows = stack_rows([coarse(k) for k in range(NZ)])
    for part in range(len(target)):
        fine = split_dot(rows, matrix[part])
        for k in range(NZ):
            x = fine[k * count : (k + 1) * count]
            for odd in range(2):
                where = pl.ds(target_row + odd, count, stride=2)
                target[part].at[k][where, :] = old[part].at[k][where, :] + x


def top_kernel(
    grid, tiles, index_ref, gathered, fm, vm, axm, aym, dm, em, gm, fh, vh, axh, ayh, dh, eh, gh,
    f1, v1, ax1, ay1, d1, e1, g1, f2, v2, ax2, ay2, d2, e2, g2, f3, v3, ax3, ay3, d3, e3, g3,
    out_ref,
    rho4, f4, ax4, ay4, d4, e4, g4, c4, a4, b4, v4, va3, vb3, va2, vb2, va1, vb1, vam, vah, vbm, vbh,
):
    ix, iy = index_ref[0], index_ref[1]
    grid_rows, grid_lanes = grid
    lane = lanes_of()
    rows4 = grid_rows // 16
    tiles_x, tiles_y = tiles

    zero = jnp.zeros((8, LANES), jnp.float32)
    for ref in (rho4, v4.at[0], v4.at[1]):
        for k in range(NZ):
            ref[k, pl.ds(0, 8), :] = zero
            ref[k, pl.ds(8 + rows4, 8), :] = zero

    count = min(8, tiles_x)
    for field, target in enumerate((f4, rho4)):
        for r in range(2):
            for base in range(0, tiles_x, count):
                xs = [
                    gathered[pl.ds((base * tiles_y + t) * 4 + field * 2 + r, count, stride=4 * tiles_y), :]
                    for t in range(16)
                ]
                block = lanes_of((count, LANES)) // 8
                for bit in (1, 2, 4, 8):
                    moved = (block & bit) != 0
                    xs = [jnp.where(moved, xs[(i + bit) % 16], xs[i]) for i in range(16)]
                for k in range(NZ):
                    x = xs[-k % 16]
                    x = x if k == 0 else pltpu.roll(x, LANES - 8 * k, 1)
                    target.at[k][pl.ds(8 + 2 * base + r, count, stride=2), :] = x

    scale = spacing(4)
    h = min(32, rows4)
    first_lane, last_lane = lanes_of((h, LANES)) == 0, lanes_of((h, LANES)) == LANES - 1
    starts = list(range(8, 8 + rows4, h))

    def faces_x(r, h):
        for k in range(NZ):
            total = rho4[k, pl.ds(r, h), :] + rho4[k, pl.ds(r - 1, h), :]
            ax4[k, pl.ds(r, h), :] = scale * rcp(jnp.maximum(total, TINY))

    for r in starts:
        faces_x(r, h)
    faces_x(rows4 + 1, 8)

    def first_sweep(r):
        rho = rho4[0, pl.ds(r, h), :]
        upper = (2.0 * VERTICAL) * rcp(rho)
        row = rows_of((h, LANES)) + r
        partial, ratio = [], None
        for k in range(NZ):
            here = rho4[k, pl.ds(r, h), :]
            left = jnp.where(first_lane, 0.0, pltpu.roll(here, 1, 1))
            ay = scale * rcp(here + left)
            right = jnp.where(last_lane, scale * rcp(here), pltpu.roll(ay, LANES - 1, 1))
            ay4[k, pl.ds(r, h), :] = jnp.where(first_lane, 0.0, ay)
            up, down = ax4[k, pl.ds(r, h), :], ax4[k, pl.ds(r + 1, h), :]
            center = up + down + ay + right + upper
            across = jnp.where(first_lane, ay, 0.0) + jnp.where(last_lane, right, 0.0)
            along = jnp.where(row == 8, up, 0.0) + jnp.where(row == 7 + rows4, down, 0.0)
            b4[k, pl.ds(r, h), :] = across + along
            if k + 1 < NZ:
                lower = (2.0 * VERTICAL) * rcp(here + rho4[k + 1, pl.ds(r, h), :])
                center = center + lower
            c4[k, pl.ds(r, h), :] = center
            a4[k, pl.ds(r, h), :] = upper
            pivot = center if k == 0 else center - upper * ratio
            inverse = rcp(pivot)
            scaled = 0.8 * inverse
            d4[k, pl.ds(r, h), :] = scaled
            value = scaled * f4[k, pl.ds(r, h), :]
            if k > 0:
                weight = upper * inverse
                e4[k, pl.ds(r, h), :] = weight
                value = value + weight * partial[-1]
            partial.append(value)
            if k + 1 < NZ:
                ratio = lower * inverse
                g4[k, pl.ds(r, h), :] = ratio
                upper = lower
        w = partial[-1]
        v4[0, NZ - 1, pl.ds(r, h), :] = w
        for k in range(NZ - 2, -1, -1):
            w = partial[k] + g4[k, pl.ds(r, h), :] * w
            v4[0, k, pl.ds(r, h), :] = w

    for r in starts:
        first_sweep(r)

    def pulled4(v, k, r):
        here = v[k, pl.ds(r, h), :]
        ay = ay4[k, pl.ds(r, h), :]
        return (
            f4[k, pl.ds(r, h), :]
            + ax4[k, pl.ds(r, h), :] * v[k, pl.ds(r - 1, h), :]
            + ax4[k, pl.ds(r + 1, h), :] * v[k, pl.ds(r + 1, h), :]
            + ay * pltpu.roll(here, 1, 1)
            + pltpu.roll(ay * here, LANES - 1, 1)
        )

    def sweep(v, out):
        for r in starts:
            partial = []
            for k in range(NZ):
                value = d4[k, pl.ds(r, h), :] * pulled4(v, k, r)
                if k > 0:
                    value = value + e4[k, pl.ds(r, h), :] * partial[-1]
                partial.append(value)
            w = None
            for k in range(NZ - 1, -1, -1):
                w = partial[k] if w is None else partial[k] + g4[k, pl.ds(r, h), :] * w
                out[k, pl.ds(r, h), :] = 0.2 * v[k, pl.ds(r, h), :] + w

    def one_sweep(number, carry):
        sweep(v4.at[number % 2], v4.at[1 - number % 2])
        return carry

    lax.fori_loop(0, SWEEPS - 1, one_sweep, 0)
    final = v4.at[(SWEEPS - 1) % 2]

    shifts, flux = [], [None] * len(starts)
    for k in range(NZ):
        left_over, weights = None, None
        for n, r in enumerate(starts):
            v = final[k, pl.ds(r, h), :]
            part = f4[k, pl.ds(r, h), :] - b4[k, pl.ds(r, h), :] * v
            part = part - (a4[0, pl.ds(r, h), :] * v if k == 0 else flux[n])
            if k + 1 < NZ:
                flux[n] = a4[k + 1, pl.ds(r, h), :] * (final[k + 1, pl.ds(r, h), :] - v)
                part = part + flux[n]
            center = c4[k, pl.ds(r, h), :]
            left_over = part if left_over is None else left_over + part
            weights = center if weights is None else weights + center
        raised = jnp.sum(left_over, axis=(0, 1), keepdims=True)
        shifts.append(raised / jnp.sum(weights, axis=(0, 1), keepdims=True))

    row = rows_of() + (ix * 2 - 4)
    column = lane + (iy * 8 - 4)
    good = jnp.logical_and(
        jnp.logical_and(row >= 0, row < rows4),
        jnp.logical_and(jnp.logical_and(column >= 0, column < grid_lanes // 16), lane < 16),
    )
    amount = lax.rem(132 - iy * 8, LANES)

    def coarsest(k):
        x = final[k, pl.ds(4 + 2 * ix, 8), :] + shifts[k]
        return jnp.where(good, pltpu.roll(x, amount, 1), 0.0)

    repeat = one_hot(LANES, lambda s, t: s == t // 2, 1.0)
    prolong(coarsest, 0, 8, None, [v3], [va3], 0, [repeat])
    level3 = Level(3, None, [ax3], [ay3], [d3], [e3], [g3])
    level3.relax([(2, 16)], [f3], [va3], [vb3])
    level3.relax([(6, 8)], [f3], [vb3], [va3])

    prolong(lambda k: va3[k, pl.ds(6, 8), :], 0, 8, None, [v2], [va2], 12, [repeat])
    level2 = Level(2, None, [ax2], [ay2], [d2], [e2], [g2])
    level2.relax([(12, 16)], [f2], [va2], [vb2])
    level2.relax([(12, 16)], [f2], [vb2], [va2])

    prolong(lambda k: va2[k, pl.ds(12, 16), :], 0, 16, None, [v1], [va1], 0, [repeat])
    level1 = Level(1, None, [ax1], [ay1], [d1], [e1], [g1])
    level1.relax([(4, 24)], [f1], [va1], [vb1])
    level1.relax([(4, 24)], [f1], [vb1], [va1])

    to_main = one_hot(LANES, lambda s, t: s == t // 2 + 32, 1.0)
    prolong(lambda k: va1[k, pl.ds(4, 24), :], 0, 24, None, [vm], [vam], 8, [to_main])
    lane = lanes_of((16, LANES))
    to_upper, to_lower = [
        one_hot(
            LANES,
            lambda s, t: ((t < base + 32) & (t >= base) & (s == (t - base) // 2 + 24))
            | ((t >= base + 32) & (t < base + 64) & (s == (t - base) // 2 + 72)),
            1.0,
        )
        for base in (0, 64)
    ]
    upper = split_dot(stack_rows([va1[k, pl.ds(2, 16), :] for k in range(NZ)]), to_upper)
    lower = split_dot(stack_rows([va1[k, pl.ds(2 + SPLIT // 2, 16), :] for k in range(NZ)]), to_lower)
    for k in range(NZ):
        x = jnp.where(lane < 64, upper[k * 16 : k * 16 + 16], lower[k * 16 : k * 16 + 16])
        for odd in range(2):
            where = pl.ds(4 + odd, 16, stride=2)
            vah.at[k][where, :] = vh.at[k][where, :] + x
    sides = Level(0, None, [axh], [ayh], [dh], [eh], [gh])
    sides.relax([(7, 16), (17, 16)], [fh], [vah], [vbh])
    sides.relax([(8, 24)], [fh], [vbh], [vah])
    main = Level(0, None, [axm], [aym], [dm], [em], [gm])
    main.relax([(15, 16, 2), (41, 8)], [fm], [vam], [vbm])
    main.relax([(16, 16, 2)], [fm], [vbm], [vam])
    for k in range(NZ):
        for row, start, low, high in ((0, 16, 112, 80), (16, 16 - SPLIT + 16, 48, 16)):
            side = vah[k, pl.ds(start, 16), :]
            side = jnp.where(lane < 64, pltpu.roll(side, low, 1), pltpu.roll(side, high, 1))
            x = vam[k, pl.ds(16 + row, 16), :]
            out_ref[k, pl.ds(row, 16), :] = jnp.where(jnp.logical_or(lane < 4, lane >= 124), side, x)


def ring(x, axis, step):
    size = lax.axis_size(axis)
    return lax.ppermute(x, axis, [(i, (i + step) % size) for i in range(size)])


def gather(x, axis):
    size = lax.axis_size(axis)
    blocks = jnp.broadcast_to(x[None], (size,) + x.shape)
    return lax.all_to_all(blocks, axis, 0, 0).reshape(size * x.shape[0], LANES)


def array(*shape):
    return jax.ShapeDtypeStruct(shape, jnp.float32)


def call(kernel, name, outs, scratch, index, *operands, cost=4000000):
    vmem = pl.BlockSpec(memory_space=pltpu.VMEM)
    ins = [vmem] * len(operands)
    if index is not None:
        ins, operands = [pl.BlockSpec(memory_space=pltpu.SMEM)] + ins, (index,) + operands
    return pl.pallas_call(
        kernel,
        out_shape=outs,
        in_specs=ins,
        out_specs=[vmem] * len(outs),
        scratch_shapes=[pltpu.VMEM(shape, jnp.float32) for shape in scratch],
        compiler_params=pltpu.CompilerParams(vmem_limit_bytes=VMEM_BYTES),
        cost_estimate=pl.CostEstimate(flops=cost, bytes_accessed=cost, transcendentals=0),
        name=name,
    )(*operands)


def solution(mesh):
    tiles_x, tiles_y = mesh.shape["gx"], mesh.shape["gy"]
    grid = (32 * tiles_x, 128 * tiles_y)
    big = [array(NZ, ROWS[level], LANES) for level in range(4)]

    def on_device(source, rho):
        index = jnp.stack([lax.axis_index("gx"), lax.axis_index("gy")]).astype(jnp.int32)

        both = jnp.concatenate([source, rho], axis=0).transpose(1, 0, 2)
        lows = both[:REACH].reshape(REACH * 2 * NZ, LANES)
        highs = both[-REACH:].reshape(REACH * 2 * NZ, LANES)
        up = ring(highs, "gx", 1)
        dn = ring(lows, "gx", -1)
        s0, s1, s2, s3 = [x.shape for x in big]
        sh = (NZ, SIDE_ROWS, LANES)
        strip = array(4, ROWS[0], LANES)
        own_strips = call(own_edges_kernel, "own_edges", [strip, strip], [], None, source, rho)
        lefts, rights = call(edges_kernel, "edges", [strip, strip], [], None, up, dn, *own_strips)
        from_left_strip = ring(rights, "gy", 1)
        from_right_strip = ring(lefts, "gy", -1)
        main = call(
            lambda *refs: main_kernel(grid, *refs), "main", [big[0]] * 9, [s0] * 2, index, source, rho, up, dn
        )
        main_state, rho_main, residual_main = main[:7], main[7], main[8]
        fine = call(
            lambda *refs: fine_kernel(grid, *refs),
            "fine",
            [array(8, 8, LANES)] + [array(*sh)] * 7 + [big[1]] * 7,
            [sh] * 3 + [s1] * 4,
            index, rho_main, residual_main, lefts, rights, from_left_strip, from_right_strip,
        )
        tile = fine[0]
        pieces = [ring(tile, "gx", 2), ring(tile, "gx", 1), tile, ring(tile, "gx", -1), ring(tile, "gx", -2)]
        own_left = jnp.concatenate([piece[:4] for piece in pieces], axis=1)
        own_right = jnp.concatenate([piece[4:] for piece in pieces], axis=1)
        from_left_column = ring(own_right, "gy", 1)
        from_right_column = ring(own_left, "gy", -1)
        coarser = call(
            lambda *refs: coarser_kernel(grid, *refs),
            "coarser",
            [array(4, LANES)] + [big[2]] * 7 + [big[3]] * 7,
            [s2] * 4 + [s3] * 4,
            index, own_left, own_right, from_left_column, from_right_column,
        )
        gathered = gather(gather(coarser[0], "gy"), "gx")

        s4 = (NZ, 16 + 2 * tiles_x, LANES)
        (pressure,) = call(
            lambda *refs: top_kernel(grid, (tiles_x, tiles_y), *refs),
            "top",
            [array(NZ, 32, LANES)],
            [s4] * 10 + [(2,) + s4] + [s3] * 2 + [s2] * 2 + [s1] * 2 + [s0, sh] * 2,
            index, gathered, *main_state, *fine[1:], *coarser[1:],
        )
        return pressure

    return jax.shard_map(
        on_device,
        mesh=mesh,
        in_specs=(P(None, "gx", "gy"), P(None, "gx", "gy")),
        out_specs=P(None, "gx", "gy"),
        check_vma=False,
    )
```

```python
import jax
import jax.numpy as jnp
from jax import lax
from jax.experimental import pallas as pl
from jax.experimental.pallas import tpu as pltpu
from jax.sharding import PartitionSpec as P

NZ = 16
LANES = 128
SWEEPS = 6
VERTICAL = 0.015625
TINY = 2.0**-20
VMEM_BYTES = 16 * 1024 * 1024

SPLIT = 24
SIDE_ROWS = 40
ROW0 = (16, 8, 16, 8)
ROWS = (64, 32, 40, 24)
LANE0 = (0, 32, 16, 8)


def spacing(level):
    return 2.0 * 0.25**level


def lanes_of(shape=(8, LANES)):
    return lax.broadcasted_iota(jnp.int32, shape, 1)


def rows_of(shape=(8, LANES)):
    return lax.broadcasted_iota(jnp.int32, shape, 0)


def rcp(x):
    guess = pl.reciprocal(x, approx=True)
    return guess * (2.0 - x * guess)


def from_left(xs):
    rolled = [pltpu.roll(x, 1, 1) for x in xs]
    if len(xs) == 1:
        return rolled
    edge = lanes_of(xs[0].shape) == 0
    return [jnp.where(edge, rolled[1], rolled[0]), jnp.where(edge, rolled[0], rolled[1])]


def from_right(xs):
    rolled = [pltpu.roll(x, LANES - 1, 1) for x in xs]
    if len(xs) == 1:
        return rolled
    edge = lanes_of(xs[0].shape) == LANES - 1
    return [jnp.where(edge, rolled[1], rolled[0]), jnp.where(edge, rolled[0], rolled[1])]


def split_dot(x, matrix, pieces=2):
    total = None
    for piece in range(pieces):
        part = x.astype(jnp.bfloat16)
        product = jnp.dot(part, matrix, preferred_element_type=jnp.float32)
        total = product if total is None else total + product
        if piece + 1 < pieces:
            x = x - part.astype(jnp.float32)
    return total


def one_hot(rows, test, value, lanes=LANES):
    shape = (rows, lanes)
    source, target = lax.broadcasted_iota(jnp.int32, shape, 0), lax.broadcasted_iota(jnp.int32, shape, 1)
    return jnp.where(test(source, target), value, 0.0).astype(jnp.bfloat16)


def run_blocks(blocks, body):
    for block in blocks:
        if len(block) == 2:
            body(*block)
        else:
            first, height, count = block

            def step(index, carry):
                body(first + height * index, height)
                return carry

            lax.fori_loop(0, count, step, 0)


TWISTED = (0, 2, 3)


class Level:
    def __init__(self, level, rho, ax, ay, d, e, g):
        self.level, self.rho, self.ax, self.ay, self.d, self.e, self.g = level, rho, ax, ay, d, e, g
        self.parts = range(len(ax))
        self.twist = level in TWISTED
        ends = [n if side == 0 else NZ - 1 - n for n in range(NZ // 2) for side in range(2)]
        self.order = ends if self.twist else list(range(NZ))

    def faces(self, blocks):
        scale = spacing(self.level)

        def body(r, h):
            for k in range(NZ):
                here = [ref[k, pl.ds(r, h), :] for ref in self.rho]
                above = [ref[k, pl.ds(r - 1, h), :] for ref in self.rho]
                left = from_left(here)
                for p in self.parts:
                    self.ax[p][k, pl.ds(r, h), :] = scale * rcp(jnp.maximum(here[p] + above[p], TINY))
                    self.ay[p][k, pl.ds(r, h), :] = scale * rcp(jnp.maximum(here[p] + left[p], TINY))

        run_blocks(blocks, body)

    def before(self, k):
        if self.twist and k >= 8:
            return k + 1 if k + 1 < NZ else None
        return k - 1 if k > 0 else None

    def substitute(self, p, r, h, partial, emit):
        def weight(k):
            return self.g[p][k, pl.ds(r, h), :]

        if not self.twist:
            w = partial[NZ - 1]
            emit(NZ - 1, w)
            for k in range(NZ - 2, -1, -1):
                w = partial[k] + weight(k) * w
                emit(k, w)
            return
        w = self.e[p][0, pl.ds(r, h), :] * (partial[7] + weight(7) * partial[8])
        emit(7, w)
        x = partial[8] + weight(8) * w
        emit(8, x)
        for k in range(6, -1, -1):
            w = partial[k] + weight(k) * w
            emit(k, w)
            x = partial[15 - k] + weight(15 - k) * x
            emit(15 - k, x)

    def factor_and_first(self, blocks, inside, f, v):
        def body(r, h):
            masks = None if inside is None else [inside(r, h) for p in self.parts]
            upper = {}

            def upper_at(k):
                if k not in upper:
                    total = [ref[k, pl.ds(r, h), :] for ref in self.rho]
                    if k > 0:
                        total = [x + ref[k - 1, pl.ds(r, h), :] for x, ref in zip(total, self.rho)]
                    upper[k] = [(2.0 * VERTICAL) * rcp(jnp.maximum(x, TINY)) for x in total]
                return upper[k]

            partial = [[None] * NZ for p in self.parts]
            back = {}
            for k in self.order:
                above = upper_at(k)
                below = upper_at(k + 1) if k + 1 < NZ else None
                ay = [ref[k, pl.ds(r, h), :] for ref in self.ay]
                right = from_right(ay)
                upwards = self.twist and k >= 8
                before = self.before(k)
                for p in self.parts:
                    center = (
                        self.ax[p][k, pl.ds(r, h), :]
                        + self.ax[p][k, pl.ds(r + 1, h), :]
                        + ay[p]
                        + right[p]
                        + above[p]
                    )
                    if k + 1 < NZ:
                        center = center + below[p]
                    toward, away = (below, above) if upwards else (above, below)
                    pivot = center if before is None else center - toward[p] * back[before, p]
                    inverse = rcp(pivot) if masks is None else jnp.where(masks[p], rcp(pivot), 0.0)
                    scaled = 0.8 * inverse
                    self.d[p][k, pl.ds(r, h), :] = scaled
                    value = scaled * f[p][k, pl.ds(r, h), :]
                    if before is not None:
                        weight = toward[p] * inverse
                        self.e[p][k, pl.ds(r, h), :] = weight
                        value = value + weight * partial[p][before]
                    partial[p][k] = value
                    if away is not None:
                        back[k, p] = away[p] * inverse
                        self.g[p][k, pl.ds(r, h), :] = back[k, p]

            for p in self.parts:
                if self.twist:
                    self.e[p][0, pl.ds(r, h), :] = rcp(1.0 - back[7, p] * back[8, p])

                def emit(k, w):
                    v[p][k, pl.ds(r, h), :] = w

                self.substitute(p, r, h, partial[p], emit)

        run_blocks(blocks, body)

    def pull(self, v, k, r, h, wanted):
        here = [ref[k, pl.ds(r, h), :] for ref in v]
        ay = [ref[k, pl.ds(r, h), :] for ref in self.ay]
        left = from_left(here)
        right = from_right([a * x for a, x in zip(ay, here)])
        return [
            self.ax[p][k, pl.ds(r, h), :] * v[p][k, pl.ds(r - 1, h), :]
            + self.ax[p][k, pl.ds(r + 1, h), :] * v[p][k, pl.ds(r + 1, h), :]
            + ay[p] * left[p]
            + right[p]
            for p in wanted
        ]

    def relax(self, blocks, f, v, out, u=None):
        def body(r, h):
            partial = [[None] * NZ for p in self.parts]
            for k in self.order:
                pulls = self.pull(v, k, r, h, self.parts)
                before = self.before(k)
                for p in self.parts:
                    value = self.d[p][k, pl.ds(r, h), :] * (f[p][k, pl.ds(r, h), :] + pulls[p])
                    if before is not None:
                        value = value + self.e[p][k, pl.ds(r, h), :] * partial[p][before]
                    partial[p][k] = value

            for p in self.parts:

                def emit(k, w):
                    old = v[p][k, pl.ds(r, h), :]
                    out[p][k, pl.ds(r, h), :] = 0.2 * old + w
                    if u is not None:
                        u[p][k, pl.ds(r, h), :] = w - 0.6 * old

                self.substitute(p, r, h, partial[p], emit)

        run_blocks(blocks, body)

    def residual(self, blocks, f, u, out):
        def body(r, h):
            for k in range(NZ):
                pulls = self.pull(u, k, r, h, self.parts)
                for p in self.parts:
                    out[p][k, pl.ds(r, h), :] = 0.04 * f[p][k, pl.ds(r, h), :] + pulls[p]

        run_blocks(blocks, body)


def inside_of(level, ix, iy, shape, part=0):
    grid_rows, grid_lanes, tile_rows, tile_lanes = shape

    def inside(r, h):
        row, lane = rows_of((h, LANES)) + (r + ix * tile_rows - ROW0[level]), lanes_of((h, LANES))
        if level == 0 and part == 1:
            row = row + jnp.where(lane < 64, 0, SPLIT)
            lane = lane % 64
        good = jnp.logical_and(row >= 0, row < grid_rows)
        if level == 0 and part == 0:
            return good
        if level == 0:
            column = iy * tile_lanes + jnp.where(lane < 32, lane - 16, lane + 80)
            side = jnp.logical_and(column >= 0, column < grid_lanes)
        else:
            column = iy * tile_lanes + lane - LANE0[level]
            side = jnp.logical_and(column >= 0, column < grid_lanes)
        return jnp.logical_and(good, side)

    return inside


def pair_rows(ref, k, start, count):
    layer = ref.at[k]
    return layer[pl.ds(start, count, stride=2), :] + layer[pl.ds(start + 1, count, stride=2), :]


def stack_rows(blocks):
    return jnp.concatenate(blocks, axis=0)


PIECES = ((5, 8, "up", 0), (8, 8, "up", 3), (16, 32, "own", 0), (48, 8, "down", 0), (51, 8, "down", 3))
REACH = 11


def piece_of(piece, field, k, own, up, down):
    first, count, source, start = piece
    if source == "own":
        return own[k, :, :]
    ref = up if source == "up" else down
    return ref[pl.ds(start * 2 * NZ + field * NZ + k, count, stride=2 * NZ), :]


def pack_rows(piece, sources, left_ref, right_ref):
    first, count = piece[:2]
    slot = lanes_of((count, LANES)) // 16
    for field in range(2):
        for half in range(2):
            lefts, rights = None, None
            for q in range(8):
                x = piece_of(piece, field, half * 8 + q, sources[field], *sources[2:])
                a = x if q == 0 else pltpu.roll(x, 16 * q, 1)
                b = pltpu.roll(x, 16 * q + 16, 1) if q < 7 else x
                lefts = a if q == 0 else jnp.where(slot == q, a, lefts)
                rights = b if q == 0 else jnp.where(slot == q, b, rights)
            left_ref[field * 2 + half, pl.ds(first, count), :] = lefts
            right_ref[field * 2 + half, pl.ds(first, count), :] = rights


def own_edges_kernel(f_ref, rho_ref, left_ref, right_ref):
    pack_rows(PIECES[2], (f_ref, rho_ref, None, None), left_ref, right_ref)


def edges_kernel(up_ref, dn_ref, own_left, own_right, left_ref, right_ref):
    left_ref[:, pl.ds(16, 32), :] = own_left[:, pl.ds(16, 32), :]
    right_ref[:, pl.ds(16, 32), :] = own_right[:, pl.ds(16, 32), :]
    for piece in PIECES:
        if piece[2] != "own":
            pack_rows(piece, (None, None, up_ref, dn_ref), left_ref, right_ref)


def main_kernel(
    grid, index_ref, f_ref, rho_ref, up_ref, dn_ref,
    fm, vm, axm, aym, dm, em, gm, rm, resm,
    firstm, um,
):
    ix, iy = index_ref[0], index_ref[1]
    inside = inside_of(0, ix, iy, grid + (32, 128))
    for field, (own, target) in enumerate(((f_ref, fm), (rho_ref, rm))):
        for k in range(NZ):
            for piece in PIECES:
                first, count, source, _ = piece
                x = piece_of(piece, field, k, own, up_ref, dn_ref)
                if field == 1 and source != "own":
                    x = jnp.where(inside(first, count), x, 0.0)
                target[k, pl.ds(first, count), :] = x
    main = Level(0, [rm], [axm], [aym], [dm], [em], [gm])
    main.faces([(6, 16), (22, 16), (38, 16), (51, 8)])
    main.factor_and_first([(6, 16), (22, 16), (38, 16), (50, 8)], inside, [fm], [firstm])
    main.relax([(7, 16), (23, 16), (39, 16), (49, 8)], [fm], [firstm], [vm], u=[um])
    main.residual([(8, 16), (24, 16), (40, 16)], [fm], [um], [resm])


def fine_kernel(
    grid, index_ref, rm, resm, own_left, own_right, from_left_ref, from_right_ref,
    pack_ref, fh, vh, axh, ayh, dh, eh, gh, f1, v1, ax1, ay1, d1, e1, g1,
    rh, firsth, uh, rho1, first1, u1, res1,
):
    ix, iy = index_ref[0], index_ref[1]
    grid_rows, grid_lanes = grid
    inside = inside_of(0, ix, iy, grid + (32, 128), part=1)

    lane = lanes_of((16, LANES))
    for field, side in enumerate((fh, rh)):
        for first in (4, 20):
            good = inside(first, 16)
            for half in range(2):
                g = field * 2 + half
                tiles = []
                for start in (first, first + SPLIT):
                    rows = pl.ds(start, 16)
                    tiles.append(
                        [
                            from_left_ref[g, rows, :],
                            pltpu.roll(own_left[g, rows, :], 16, 1),
                            pltpu.roll(own_right[g, rows, :], 32, 1),
                            pltpu.roll(from_right_ref[g, rows, :], 48, 1),
                        ]
                    )
                for m in range(4):
                    place = (lane - 16 * m) % 128
                    spot = place % 64
                    upper, lower = [
                        jnp.where(
                            spot < 32, jnp.where(spot < 16, t[0], t[1]), jnp.where(spot < 48, t[2], t[3])
                        )
                        for t in tiles
                    ]
                    straight = jnp.where(place < 64, upper, lower)
                    crossed = jnp.where(place < 64, lower, upper)
                    if m > 0:
                        straight = pltpu.roll(straight, LANES - 16 * m, 1)
                        crossed = pltpu.roll(crossed, LANES - 16 * m, 1)
                    crossed = pltpu.roll(crossed, 64, 1)
                    for layer, y in (
                        (m, jnp.where(lane < 64, straight, crossed)),
                        (m + 4, jnp.where(lane < 64, crossed, straight)),
                    ):
                        if field == 1:
                            y = jnp.where(good, y, 0.0)
                        side[half * 8 + layer, pl.ds(first, 16), :] = y

    sides = Level(0, [rh], [axh], [ayh], [dh], [eh], [gh])
    sides.faces([(4, 16), (20, 16)])
    sides.factor_and_first([(5, 16), (19, 16)], inside, [fh], [firsth])
    sides.relax([(6, 16), (18, 16)], [fh], [firsth], [vh], u=[uh])
    sides.residual([(8, 24)], [fh], [uh], [firsth])

    main_matrix = one_hot(LANES, lambda s, t: (s // 2 + 32 == t) & (s >= 4) & (s < 124), 0.25)
    upper_matrix, lower_matrix = [
        one_hot(
            LANES,
            lambda s, t: ((s // 2 - base // 2 + 24 == t) & (s >= base + 6) & (s < base + 20))
            | ((s // 2 - base // 2 + 72 == t) & (s >= base + 44) & (s < base + 58)),
            0.25,
        )
        for base in (0, 64)
    ]
    for first in range(0, NZ, 4):
        ks = range(first, first + 4)
        for target, main, side in ((f1, resm, firsth), (rho1, rm, rh)):
            total = split_dot(stack_rows([pair_rows(main, k, 0, 32) for k in ks]), main_matrix)
            upper = split_dot(stack_rows([pair_rows(side, k, 0, 16) for k in ks]), upper_matrix)
            lower = split_dot(stack_rows([pair_rows(side, k, 8, 16) for k in ks]), lower_matrix)
            for n, k in enumerate(ks):
                target[k, pl.ds(0, 16), :] = total[n * 32 : n * 32 + 16] + upper[n * 16 : n * 16 + 16]
                target[k, pl.ds(16, 16), :] = total[n * 32 + 16 : n * 32 + 32] + lower[n * 16 : n * 16 + 16]

    middle = Level(1, [rho1], [ax1], [ay1], [d1], [e1], [g1])
    inside = inside_of(1, ix, iy, (grid_rows // 2, grid_lanes // 2, 16, 64))
    middle.faces([(4, 24), (21, 8)])
    middle.factor_and_first([(4, 24)], inside, [f1], [first1])
    middle.relax([(4, 24)], [f1], [first1], [v1], u=[u1])
    middle.residual([(8, 16)], [f1], [u1], [res1])

    pack_matrix = one_hot(
        LANES,
        lambda s, t: jnp.logical_and(
            s // 2 - 16 == (t // LANES) * 16 + t % 16, jnp.logical_and(s >= 32, s < 96)
        ),
        0.25,
        2 * LANES,
    )
    slot = lanes_of() // 16
    for field, ref in enumerate((res1, rho1)):
        wide = split_dot(stack_rows([pair_rows(ref, k, 8, 8) for k in range(NZ)]), pack_matrix)
        for side in range(2):
            for half in range(2):
                packed = None
                for q in range(8):
                    k = half * 8 + q
                    x = wide[k * 8 : (k + 1) * 8, side * LANES : (side + 1) * LANES]
                    packed = x if q == 0 else jnp.where(slot == q, x, packed)
                pack_ref[side * 4 + field * 2 + half, :, :] = packed


def coarser_kernel(
    grid, index_ref, own_left_ref, own_right_ref, from_left_ref, from_right_ref,
    pack_ref, f2, v2, ax2, ay2, d2, e2, g2, f3, v3, ax3, ay3, d3, e3, g3,
    rho2, first2, u2, res2, rho3, first3, u3, res3,
):
    ix, iy = index_ref[0], index_ref[1]
    grid_rows, grid_lanes = grid
    lane = lanes_of()
    inside = inside_of(2, ix, iy, (grid_rows // 4, grid_lanes // 4, 8, 32))

    lane40 = lanes_of((40, LANES))
    good = inside(0, 40)
    for field, target in enumerate((f2, rho2)):
        for half in range(2):
            g = field * 2 + half
            tiles = [
                from_left_ref[g],
                pltpu.roll(own_left_ref[g], 16, 1),
                pltpu.roll(own_right_ref[g], 32, 1),
                pltpu.roll(from_right_ref[g], 48, 1),
            ]
            for m in range(4):
                place = (lane40 - 16 * m) % 64
                merged = jnp.where(
                    place < 32,
                    jnp.where(place < 16, tiles[0], tiles[1]),
                    jnp.where(place < 48, tiles[2], tiles[3]),
                )
                for q in (m, m + 4):
                    y = merged if q == 0 else pltpu.roll(merged, LANES - 16 * q, 1)
                    if field == 1:
                        y = jnp.where(good, y, 0.0)
                    target[half * 8 + q, :, :] = y

    level2 = Level(2, [rho2], [ax2], [ay2], [d2], [e2], [g2])
    level2.faces([(4, 16, 2), (29, 8)])
    level2.factor_and_first([(4, 16, 2)], inside, [f2], [first2])
    level2.relax([(4, 16, 2)], [f2], [first2], [v2], u=[u2])
    level2.residual([(4, 16, 2)], [f2], [u2], [res2])

    halve = one_hot(LANES, lambda s, t: s // 2 == t, 0.25)
    for ref, target, first, count in ((res2, f3, 4, 16), (rho2, rho3, 4, 16)):
        total = split_dot(stack_rows([pair_rows(ref, k, first, count) for k in range(NZ)]), halve)
        for k in range(NZ):
            target[k, pl.ds(first // 2, count), :] = total[k * count : (k + 1) * count]

    level3 = Level(3, [rho3], [ax3], [ay3], [d3], [e3], [g3])
    inside = inside_of(3, ix, iy, (grid_rows // 8, grid_lanes // 8, 4, 16))
    level3.faces([(2, 16)])
    level3.factor_and_first([(2, 16)], inside, [f3], [first3])
    level3.relax([(2, 16)], [f3], [first3], [v3], u=[u3])
    level3.residual([(6, 8)], [f3], [u3], [res3])

    spread = one_hot(
        LANES,
        lambda s, t: jnp.logical_and(s // 2 - 4 == t % 8, jnp.logical_and(s >= 8, s < 24)),
        0.25,
    )
    for field, ref in enumerate((res3, rho3)):
        total = split_dot(stack_rows([pair_rows(ref, k, 8, 8) for k in range(NZ)]), spread)
        merged = total[0:8]
        for k in range(1, NZ):
            merged = jnp.where(lane // 8 == k, total[k * 8 : (k + 1) * 8], merged)
        pack_ref[pl.ds(2 * field, 2), :] = pltpu.roll(merged, 8 * iy, 1)[0:2]


def prolong(coarse, first_row, count, ref, old, target, target_row, matrix):
    rows = stack_rows([coarse(k) for k in range(NZ)])
    for part in range(len(target)):
        fine = split_dot(rows, matrix[part])
        for k in range(NZ):
            x = fine[k * count : (k + 1) * count]
            for odd in range(2):
                where = pl.ds(target_row + odd, count, stride=2)
                target[part].at[k][where, :] = old[part].at[k][where, :] + x


def top_kernel(
    grid, tiles, index_ref, gathered, fm, vm, axm, aym, dm, em, gm, fh, vh, axh, ayh, dh, eh, gh,
    f1, v1, ax1, ay1, d1, e1, g1, f2, v2, ax2, ay2, d2, e2, g2, f3, v3, ax3, ay3, d3, e3, g3,
    out_ref,
    rho4, f4, ax4, ay4, d4, e4, g4, c4, a4, b4, v4, va3, vb3, va2, vb2, va1, vb1, vam, vah, vbm, vbh,
):
    ix, iy = index_ref[0], index_ref[1]
    grid_rows, grid_lanes = grid
    lane = lanes_of()
    rows4 = grid_rows // 16
    tiles_x, tiles_y = tiles

    zero = jnp.zeros((8, LANES), jnp.float32)
    for ref in (rho4, v4.at[0], v4.at[1]):
        for k in range(NZ):
            ref[k, pl.ds(0, 8), :] = zero
            ref[k, pl.ds(8 + rows4, 8), :] = zero

    count = min(8, tiles_x)
    for field, target in enumerate((f4, rho4)):
        for r in range(2):
            for base in range(0, tiles_x, count):
                xs = [
                    gathered[pl.ds((base * tiles_y + t) * 4 + field * 2 + r, count, stride=4 * tiles_y), :]
                    for t in range(16)
                ]
                block = lanes_of((count, LANES)) // 8
                for bit in (1, 2, 4, 8):
                    moved = (block & bit) != 0
                    xs = [jnp.where(moved, xs[(i + bit) % 16], xs[i]) for i in range(16)]
                for k in range(NZ):
                    x = xs[-k % 16]
                    x = x if k == 0 else pltpu.roll(x, LANES - 8 * k, 1)
                    target.at[k][pl.ds(8 + 2 * base + r, count, stride=2), :] = x

    scale = spacing(4)
    h = min(32, rows4)
    first_lane, last_lane = lanes_of((h, LANES)) == 0, lanes_of((h, LANES)) == LANES - 1
    starts = list(range(8, 8 + rows4, h))

    def faces_x(r, h):
        for k in range(NZ):
            total = rho4[k, pl.ds(r, h), :] + rho4[k, pl.ds(r - 1, h), :]
            ax4[k, pl.ds(r, h), :] = scale * rcp(jnp.maximum(total, TINY))

    for r in starts:
        faces_x(r, h)
    faces_x(rows4 + 1, 8)

    def first_sweep(r):
        rho = rho4[0, pl.ds(r, h), :]
        upper = (2.0 * VERTICAL) * rcp(rho)
        row = rows_of((h, LANES)) + r
        partial, ratio = [], None
        for k in range(NZ):
            here = rho4[k, pl.ds(r, h), :]
            left = jnp.where(first_lane, 0.0, pltpu.roll(here, 1, 1))
            ay = scale * rcp(here + left)
            right = jnp.where(last_lane, scale * rcp(here), pltpu.roll(ay, LANES - 1, 1))
            ay4[k, pl.ds(r, h), :] = jnp.where(first_lane, 0.0, ay)
            up, down = ax4[k, pl.ds(r, h), :], ax4[k, pl.ds(r + 1, h), :]
            center = up + down + ay + right + upper
            across = jnp.where(first_lane, ay, 0.0) + jnp.where(last_lane, right, 0.0)
            along = jnp.where(row == 8, up, 0.0) + jnp.where(row == 7 + rows4, down, 0.0)
            b4[k, pl.ds(r, h), :] = across + along
            if k + 1 < NZ:
                lower = (2.0 * VERTICAL) * rcp(here + rho4[k + 1, pl.ds(r, h), :])
                center = center + lower
            c4[k, pl.ds(r, h), :] = center
            a4[k, pl.ds(r, h), :] = upper
            pivot = center if k == 0 else center - upper * ratio
            inverse = rcp(pivot)
            scaled = 0.8 * inverse
            d4[k, pl.ds(r, h), :] = scaled
            value = scaled * f4[k, pl.ds(r, h), :]
            if k > 0:
                weight = upper * inverse
                e4[k, pl.ds(r, h), :] = weight
                value = value + weight * partial[-1]
            partial.append(value)
            if k + 1 < NZ:
                ratio = lower * inverse
                g4[k, pl.ds(r, h), :] = ratio
                upper = lower
        w = partial[-1]
        v4[0, NZ - 1, pl.ds(r, h), :] = w
        for k in range(NZ - 2, -1, -1):
            w = partial[k] + g4[k, pl.ds(r, h), :] * w
            v4[0, k, pl.ds(r, h), :] = w

    for r in starts:
        first_sweep(r)

    def pulled4(v, k, r):
        here = v[k, pl.ds(r, h), :]
        ay = ay4[k, pl.ds(r, h), :]
        return (
            f4[k, pl.ds(r, h), :]
            + ax4[k, pl.ds(r, h), :] * v[k, pl.ds(r - 1, h), :]
            + ax4[k, pl.ds(r + 1, h), :] * v[k, pl.ds(r + 1, h), :]
            + ay * pltpu.roll(here, 1, 1)
            + pltpu.roll(ay * here, LANES - 1, 1)
        )

    def sweep(v, out):
        for r in starts:
            partial = []
            for k in range(NZ):
                value = d4[k, pl.ds(r, h), :] * pulled4(v, k, r)
                if k > 0:
                    value = value + e4[k, pl.ds(r, h), :] * partial[-1]
                partial.append(value)
            w = None
            for k in range(NZ - 1, -1, -1):
                w = partial[k] if w is None else partial[k] + g4[k, pl.ds(r, h), :] * w
                out[k, pl.ds(r, h), :] = 0.2 * v[k, pl.ds(r, h), :] + w

    def one_sweep(number, carry):
        sweep(v4.at[number % 2], v4.at[1 - number % 2])
        return carry

    lax.fori_loop(0, SWEEPS - 1, one_sweep, 0)
    final = v4.at[(SWEEPS - 1) % 2]

    shifts, flux = [], [None] * len(starts)
    for k in range(NZ):
        left_over, weights = None, None
        for n, r in enumerate(starts):
            v = final[k, pl.ds(r, h), :]
            part = f4[k, pl.ds(r, h), :] - b4[k, pl.ds(r, h), :] * v
            part = part - (a4[0, pl.ds(r, h), :] * v if k == 0 else flux[n])
            if k + 1 < NZ:
                flux[n] = a4[k + 1, pl.ds(r, h), :] * (final[k + 1, pl.ds(r, h), :] - v)
                part = part + flux[n]
            center = c4[k, pl.ds(r, h), :]
            left_over = part if left_over is None else left_over + part
            weights = center if weights is None else weights + center
        raised = jnp.sum(left_over, axis=(0, 1), keepdims=True)
        shifts.append(raised / jnp.sum(weights, axis=(0, 1), keepdims=True))

    row = rows_of() + (ix * 2 - 4)
    column = lane + (iy * 8 - 4)
    good = jnp.logical_and(
        jnp.logical_and(row >= 0, row < rows4),
        jnp.logical_and(jnp.logical_and(column >= 0, column < grid_lanes // 16), lane < 16),
    )
    amount = lax.rem(132 - iy * 8, LANES)

    def coarsest(k):
        x = final[k, pl.ds(4 + 2 * ix, 8), :] + shifts[k]
        return jnp.where(good, pltpu.roll(x, amount, 1), 0.0)

    repeat = one_hot(LANES, lambda s, t: s == t // 2, 1.0)
    prolong(coarsest, 0, 8, None, [v3], [va3], 0, [repeat])
    level3 = Level(3, None, [ax3], [ay3], [d3], [e3], [g3])
    level3.relax([(2, 16)], [f3], [va3], [vb3])
    level3.relax([(6, 8)], [f3], [vb3], [va3])

    prolong(lambda k: va3[k, pl.ds(6, 8), :], 0, 8, None, [v2], [va2], 12, [repeat])
    level2 = Level(2, None, [ax2], [ay2], [d2], [e2], [g2])
    level2.relax([(12, 16)], [f2], [va2], [vb2])
    level2.relax([(12, 16)], [f2], [vb2], [va2])

    prolong(lambda k: va2[k, pl.ds(12, 16), :], 0, 16, None, [v1], [va1], 0, [repeat])
    level1 = Level(1, None, [ax1], [ay1], [d1], [e1], [g1])
    level1.relax([(4, 24)], [f1], [va1], [vb1])
    level1.relax([(4, 24)], [f1], [vb1], [va1])

    to_main = one_hot(LANES, lambda s, t: s == t // 2 + 32, 1.0)
    prolong(lambda k: va1[k, pl.ds(4, 24), :], 0, 24, None, [vm], [vam], 8, [to_main])
    lane = lanes_of((16, LANES))
    to_upper, to_lower = [
        one_hot(
            LANES,
            lambda s, t: ((t < base + 32) & (t >= base) & (s == (t - base) // 2 + 24))
            | ((t >= base + 32) & (t < base + 64) & (s == (t - base) // 2 + 72)),
            1.0,
        )
        for base in (0, 64)
    ]
    upper = split_dot(stack_rows([va1[k, pl.ds(2, 16), :] for k in range(NZ)]), to_upper)
    lower = split_dot(stack_rows([va1[k, pl.ds(2 + SPLIT // 2, 16), :] for k in range(NZ)]), to_lower)
    for k in range(NZ):
        x = jnp.where(lane < 64, upper[k * 16 : k * 16 + 16], lower[k * 16 : k * 16 + 16])
        for odd in range(2):
            where = pl.ds(4 + odd, 16, stride=2)
            vah.at[k][where, :] = vh.at[k][where, :] + x
    sides = Level(0, None, [axh], [ayh], [dh], [eh], [gh])
    sides.relax([(7, 16), (17, 16)], [fh], [vah], [vbh])
    sides.relax([(8, 24)], [fh], [vbh], [vah])
    main = Level(0, None, [axm], [aym], [dm], [em], [gm])
    main.relax([(15, 16, 2), (41, 8)], [fm], [vam], [vbm])
    main.relax([(16, 16, 2)], [fm], [vbm], [vam])
    for k in range(NZ):
        for row, start, low, high in ((0, 16, 112, 80), (16, 16 - SPLIT + 16, 48, 16)):
            side = vah[k, pl.ds(start, 16), :]
            side = jnp.where(lane < 64, pltpu.roll(side, low, 1), pltpu.roll(side, high, 1))
            x = vam[k, pl.ds(16 + row, 16), :]
            out_ref[k, pl.ds(row, 16), :] = jnp.where(jnp.logical_or(lane < 4, lane >= 124), side, x)


def ring(x, axis, step):
    size = lax.axis_size(axis)
    return lax.ppermute(x, axis, [(i, (i + step) % size) for i in range(size)])


def gather(x, axis):
    size = lax.axis_size(axis)
    blocks = jnp.broadcast_to(x[None], (size,) + x.shape)
    return lax.all_to_all(blocks, axis, 0, 0).reshape(size * x.shape[0], LANES)


def array(*shape):
    return jax.ShapeDtypeStruct(shape, jnp.float32)


def call(kernel, name, outs, scratch, index, *operands, cost=4000000):
    vmem = pl.BlockSpec(memory_space=pltpu.VMEM)
    ins = [vmem] * len(operands)
    if index is not None:
        ins, operands = [pl.BlockSpec(memory_space=pltpu.SMEM)] + ins, (index,) + operands
    return pl.pallas_call(
        kernel,
        out_shape=outs,
        in_specs=ins,
        out_specs=[vmem] * len(outs),
        scratch_shapes=[pltpu.VMEM(shape, jnp.float32) for shape in scratch],
        compiler_params=pltpu.CompilerParams(vmem_limit_bytes=VMEM_BYTES),
        cost_estimate=pl.CostEstimate(flops=cost, bytes_accessed=cost, transcendentals=0),
        name=name,
    )(*operands)


def solution(mesh):
    tiles_x, tiles_y = mesh.shape["gx"], mesh.shape["gy"]
    grid = (32 * tiles_x, 128 * tiles_y)
    big = [array(NZ, ROWS[level], LANES) for level in range(4)]

    def on_device(source, rho):
        index = jnp.stack([lax.axis_index("gx"), lax.axis_index("gy")]).astype(jnp.int32)

        both = jnp.concatenate([source, rho], axis=0).transpose(1, 0, 2)
        lows = both[:REACH].reshape(REACH * 2 * NZ, LANES)
        highs = both[-REACH:].reshape(REACH * 2 * NZ, LANES)
        up = ring(highs, "gx", 1)
        dn = ring(lows, "gx", -1)
        s0, s1, s2, s3 = [x.shape for x in big]
        sh = (NZ, SIDE_ROWS, LANES)
        strip = array(4, ROWS[0], LANES)
        own_strips = call(own_edges_kernel, "own_edges", [strip, strip], [], None, source, rho)
        lefts, rights = call(edges_kernel, "edges", [strip, strip], [], None, up, dn, *own_strips)
        from_left_strip = ring(rights, "gy", 1)
        from_right_strip = ring(lefts, "gy", -1)
        main = call(
            lambda *refs: main_kernel(grid, *refs), "main", [big[0]] * 9, [s0] * 2, index, source, rho, up, dn
        )
        main_state, rho_main, residual_main = main[:7], main[7], main[8]
        fine = call(
            lambda *refs: fine_kernel(grid, *refs),
            "fine",
            [array(8, 8, LANES)] + [array(*sh)] * 7 + [big[1]] * 7,
            [sh] * 3 + [s1] * 4,
            index, rho_main, residual_main, lefts, rights, from_left_strip, from_right_strip,
        )
        tile = fine[0]
        pieces = [ring(tile, "gx", 2), ring(tile, "gx", 1), tile, ring(tile, "gx", -1), ring(tile, "gx", -2)]
        own_left = jnp.concatenate([piece[:4] for piece in pieces], axis=1)
        own_right = jnp.concatenate([piece[4:] for piece in pieces], axis=1)
        from_left_column = ring(own_right, "gy", 1)
        from_right_column = ring(own_left, "gy", -1)
        coarser = call(
            lambda *refs: coarser_kernel(grid, *refs),
            "coarser",
            [array(4, LANES)] + [big[2]] * 7 + [big[3]] * 7,
            [s2] * 4 + [s3] * 4,
            index, own_left, own_right, from_left_column, from_right_column,
        )
        gathered = gather(gather(coarser[0], "gy"), "gx")

        s4 = (NZ, 16 + 2 * tiles_x, LANES)
        (pressure,) = call(
            lambda *refs: top_kernel(grid, (tiles_x, tiles_y), *refs),
            "top",
            [array(NZ, 32, LANES)],
            [s4] * 10 + [(2,) + s4] + [s3] * 2 + [s2] * 2 + [s1] * 2 + [s0, sh] * 2,
            index, gathered, *main_state, *fine[1:], *coarser[1:],
        )
        return pressure

    return jax.shard_map(
        on_device,
        mesh=mesh,
        in_specs=(P(None, "gx", "gy"), P(None, "gx", "gy")),
        out_specs=P(None, "gx", "gy"),
        check_vma=False,
    )
```

```python
import jax
import jax.numpy as jnp
from jax import lax
from jax.experimental import pallas as pl
from jax.experimental.pallas import tpu as pltpu
from jax.sharding import PartitionSpec as P

NZ = 16
LANES = 128
SWEEPS = 6
VERTICAL = 0.015625
TINY = 2.0**-20
VMEM_BYTES = 16 * 1024 * 1024

SPLIT = 24
SIDE_ROWS = 40
ROW0 = (16, 8, 16, 8)
ROWS = (64, 32, 40, 24)
LANE0 = (0, 32, 16, 8)


def spacing(level):
    return 2.0 * 0.25**level


def lanes_of(shape=(8, LANES)):
    return lax.broadcasted_iota(jnp.int32, shape, 1)


def rows_of(shape=(8, LANES)):
    return lax.broadcasted_iota(jnp.int32, shape, 0)


def rcp(x):
    guess = pl.reciprocal(x, approx=True)
    return guess * (2.0 - x * guess)


def from_left(xs):
    rolled = [pltpu.roll(x, 1, 1) for x in xs]
    if len(xs) == 1:
        return rolled
    edge = lanes_of(xs[0].shape) == 0
    return [jnp.where(edge, rolled[1], rolled[0]), jnp.where(edge, rolled[0], rolled[1])]


def from_right(xs):
    rolled = [pltpu.roll(x, LANES - 1, 1) for x in xs]
    if len(xs) == 1:
        return rolled
    edge = lanes_of(xs[0].shape) == LANES - 1
    return [jnp.where(edge, rolled[1], rolled[0]), jnp.where(edge, rolled[0], rolled[1])]


def split_dot(x, matrix, pieces=2):
    total = None
    for piece in range(pieces):
        part = x.astype(jnp.bfloat16)
        product = jnp.dot(part, matrix, preferred_element_type=jnp.float32)
        total = product if total is None else total + product
        if piece + 1 < pieces:
            x = x - part.astype(jnp.float32)
    return total


def one_hot(rows, test, value, lanes=LANES):
    shape = (rows, lanes)
    source, target = lax.broadcasted_iota(jnp.int32, shape, 0), lax.broadcasted_iota(jnp.int32, shape, 1)
    return jnp.where(test(source, target), value, 0.0).astype(jnp.bfloat16)


def run_blocks(blocks, body):
    for block in blocks:
        if len(block) == 2:
            body(*block)
        else:
            first, height, count = block

            def step(index, carry):
                body(first + height * index, height)
                return carry

            lax.fori_loop(0, count, step, 0)


TWISTED = (0, 2, 3)


class Level:
    def __init__(self, level, rho, ax, ay, d, e, g):
        self.level, self.rho, self.ax, self.ay, self.d, self.e, self.g = level, rho, ax, ay, d, e, g
        self.parts = range(len(ax))
        self.twist = level in TWISTED
        ends = [n if side == 0 else NZ - 1 - n for n in range(NZ // 2) for side in range(2)]
        self.order = ends if self.twist else list(range(NZ))

    def faces(self, blocks):
        scale = spacing(self.level)

        def body(r, h):
            for k in range(NZ):
                here = [ref[k, pl.ds(r, h), :] for ref in self.rho]
                above = [ref[k, pl.ds(r - 1, h), :] for ref in self.rho]
                left = from_left(here)
                for p in self.parts:
                    self.ax[p][k, pl.ds(r, h), :] = scale * rcp(jnp.maximum(here[p] + above[p], TINY))
                    self.ay[p][k, pl.ds(r, h), :] = scale * rcp(jnp.maximum(here[p] + left[p], TINY))

        run_blocks(blocks, body)

    def before(self, k):
        if self.twist and k >= 8:
            return k + 1 if k + 1 < NZ else None
        return k - 1 if k > 0 else None

    def substitute(self, p, r, h, partial, emit):
        def weight(k):
            return self.g[p][k, pl.ds(r, h), :]

        if not self.twist:
            w = partial[NZ - 1]
            emit(NZ - 1, w)
            for k in range(NZ - 2, -1, -1):
                w = partial[k] + weight(k) * w
                emit(k, w)
            return
        w = self.e[p][0, pl.ds(r, h), :] * (partial[7] + weight(7) * partial[8])
        emit(7, w)
        x = partial[8] + weight(8) * w
        emit(8, x)
        for k in range(6, -1, -1):
            w = partial[k] + weight(k) * w
            emit(k, w)
            x = partial[15 - k] + weight(15 - k) * x
            emit(15 - k, x)

    def factor_and_first(self, blocks, inside, f, v):
        def body(r, h):
            masks = None if inside is None else [inside(r, h) for p in self.parts]
            upper = {}

            def upper_at(k):
                if k not in upper:
                    total = [ref[k, pl.ds(r, h), :] for ref in self.rho]
                    if k > 0:
                        total = [x + ref[k - 1, pl.ds(r, h), :] for x, ref in zip(total, self.rho)]
                    upper[k] = [(2.0 * VERTICAL) * rcp(jnp.maximum(x, TINY)) for x in total]
                return upper[k]

            partial = [[None] * NZ for p in self.parts]
            back = {}
            for k in self.order:
                above = upper_at(k)
                below = upper_at(k + 1) if k + 1 < NZ else None
                ay = [ref[k, pl.ds(r, h), :] for ref in self.ay]
                right = from_right(ay)
                upwards = self.twist and k >= 8
                before = self.before(k)
                for p in self.parts:
                    center = (
                        self.ax[p][k, pl.ds(r, h), :]
                        + self.ax[p][k, pl.ds(r + 1, h), :]
                        + ay[p]
                        + right[p]
                        + above[p]
                    )
                    if k + 1 < NZ:
                        center = center + below[p]
                    toward, away = (below, above) if upwards else (above, below)
                    pivot = center if before is None else center - toward[p] * back[before, p]
                    inverse = rcp(pivot) if masks is None else jnp.where(masks[p], rcp(pivot), 0.0)
                    scaled = 0.8 * inverse
                    self.d[p][k, pl.ds(r, h), :] = scaled
                    value = scaled * f[p][k, pl.ds(r, h), :]
                    if before is not None:
                        weight = toward[p] * inverse
                        self.e[p][k, pl.ds(r, h), :] = weight
                        value = value + weight * partial[p][before]
                    partial[p][k] = value
                    if away is not None:
                        back[k, p] = away[p] * inverse
                        self.g[p][k, pl.ds(r, h), :] = back[k, p]

            for p in self.parts:
                if self.twist:
                    self.e[p][0, pl.ds(r, h), :] = rcp(1.0 - back[7, p] * back[8, p])

                def emit(k, w):
                    v[p][k, pl.ds(r, h), :] = w

                self.substitute(p, r, h, partial[p], emit)

        run_blocks(blocks, body)

    def pull(self, v, k, r, h, wanted):
        here = [ref[k, pl.ds(r, h), :] for ref in v]
        ay = [ref[k, pl.ds(r, h), :] for ref in self.ay]
        left = from_left(here)
        right = from_right([a * x for a, x in zip(ay, here)])
        return [
            self.ax[p][k, pl.ds(r, h), :] * v[p][k, pl.ds(r - 1, h), :]
            + self.ax[p][k, pl.ds(r + 1, h), :] * v[p][k, pl.ds(r + 1, h), :]
            + ay[p] * left[p]
            + right[p]
            for p in wanted
        ]

    def relax(self, blocks, f, v, out, u=None):
        def body(r, h):
            partial = [[None] * NZ for p in self.parts]
            for k in self.order:
                pulls = self.pull(v, k, r, h, self.parts)
                before = self.before(k)
                for p in self.parts:
                    value = self.d[p][k, pl.ds(r, h), :] * (f[p][k, pl.ds(r, h), :] + pulls[p])
                    if before is not None:
                        value = value + self.e[p][k, pl.ds(r, h), :] * partial[p][before]
                    partial[p][k] = value

            for p in self.parts:

                def emit(k, w):
                    old = v[p][k, pl.ds(r, h), :]
                    out[p][k, pl.ds(r, h), :] = 0.2 * old + w
                    if u is not None:
                        u[p][k, pl.ds(r, h), :] = w - 0.6 * old

                self.substitute(p, r, h, partial[p], emit)

        run_blocks(blocks, body)

    def residual(self, blocks, f, u, out):
        def body(r, h):
            for k in range(NZ):
                pulls = self.pull(u, k, r, h, self.parts)
                for p in self.parts:
                    out[p][k, pl.ds(r, h), :] = 0.04 * f[p][k, pl.ds(r, h), :] + pulls[p]

        run_blocks(blocks, body)


def inside_of(level, ix, iy, shape, part=0):
    grid_rows, grid_lanes, tile_rows, tile_lanes = shape

    def inside(r, h):
        row, lane = rows_of((h, LANES)) + (r + ix * tile_rows - ROW0[level]), lanes_of((h, LANES))
        if level == 0 and part == 1:
            row = row + jnp.where(lane < 64, 0, SPLIT)
            lane = lane % 64
        good = jnp.logical_and(row >= 0, row < grid_rows)
        if level == 0 and part == 0:
            return good
        if level == 0:
            column = iy * tile_lanes + jnp.where(lane < 32, lane - 16, lane + 80)
            side = jnp.logical_and(column >= 0, column < grid_lanes)
        else:
            column = iy * tile_lanes + lane - LANE0[level]
            side = jnp.logical_and(column >= 0, column < grid_lanes)
        return jnp.logical_and(good, side)

    return inside


def pair_rows(ref, k, start, count):
    layer = ref.at[k]
    return layer[pl.ds(start, count, stride=2), :] + layer[pl.ds(start + 1, count, stride=2), :]


def stack_rows(blocks):
    return jnp.concatenate(blocks, axis=0)


PIECES = ((5, 8, "up", 0), (8, 8, "up", 3), (16, 32, "own", 0), (48, 8, "down", 0), (51, 8, "down", 3))
REACH = 11


def piece_of(piece, field, k, own, up, down):
    first, count, source, start = piece
    if source == "own":
        return own[k, :, :]
    ref = up if source == "up" else down
    return ref[pl.ds(start * 2 * NZ + field * NZ + k, count, stride=2 * NZ), :]


def pack_rows(piece, sources, left_ref, right_ref):
    first, count = piece[:2]
    slot = lanes_of((count, LANES)) // 16
    for field in range(2):
        for half in range(2):
            lefts, rights = None, None
            for q in range(8):
                x = piece_of(piece, field, half * 8 + q, sources[field], *sources[2:])
                a = x if q == 0 else pltpu.roll(x, 16 * q, 1)
                b = pltpu.roll(x, 16 * q + 16, 1) if q < 7 else x
                lefts = a if q == 0 else jnp.where(slot == q, a, lefts)
                rights = b if q == 0 else jnp.where(slot == q, b, rights)
            left_ref[field * 2 + half, pl.ds(first, count), :] = lefts
            right_ref[field * 2 + half, pl.ds(first, count), :] = rights


def own_edges_kernel(f_ref, rho_ref, left_ref, right_ref):
    pack_rows(PIECES[2], (f_ref, rho_ref, None, None), left_ref, right_ref)


def edges_kernel(up_ref, dn_ref, own_left, own_right, left_ref, right_ref):
    left_ref[:, pl.ds(16, 32), :] = own_left[:, pl.ds(16, 32), :]
    right_ref[:, pl.ds(16, 32), :] = own_right[:, pl.ds(16, 32), :]
    for piece in PIECES:
        if piece[2] != "own":
            pack_rows(piece, (None, None, up_ref, dn_ref), left_ref, right_ref)


def main_kernel(
    grid, index_ref, f_ref, rho_ref, up_ref, dn_ref,
    fm, vm, axm, aym, dm, em, gm, rm, resm,
    firstm, um,
):
    ix, iy = index_ref[0], index_ref[1]
    inside = inside_of(0, ix, iy, grid + (32, 128))
    for field, (own, target) in enumerate(((f_ref, fm), (rho_ref, rm))):
        for k in range(NZ):
            for piece in PIECES:
                first, count, source, _ = piece
                x = piece_of(piece, field, k, own, up_ref, dn_ref)
                if field == 1 and source != "own":
                    x = jnp.where(inside(first, count), x, 0.0)
                target[k, pl.ds(first, count), :] = x
    main = Level(0, [rm], [axm], [aym], [dm], [em], [gm])
    main.faces([(6, 16), (22, 16), (38, 16), (51, 8)])
    main.factor_and_first([(6, 16), (22, 16), (38, 16), (50, 8)], inside, [fm], [firstm])
    main.relax([(7, 16), (23, 16), (39, 16), (49, 8)], [fm], [firstm], [vm], u=[um])
    main.residual([(8, 16), (24, 16), (40, 16)], [fm], [um], [resm])


def fine_kernel(
    grid, index_ref, rm, resm, own_left, own_right, from_left_ref, from_right_ref,
    pack_ref, fh, vh, axh, ayh, dh, eh, gh, f1, v1, ax1, ay1, d1, e1, g1,
    rh, firsth, uh, rho1, first1, u1, res1,
):
    ix, iy = index_ref[0], index_ref[1]
    grid_rows, grid_lanes = grid
    inside = inside_of(0, ix, iy, grid + (32, 128), part=1)

    lane = lanes_of((16, LANES))
    for field, side in enumerate((fh, rh)):
        for first in (4, 20):
            good = inside(first, 16)
            for half in range(2):
                g = field * 2 + half
                tiles = []
                for start in (first, first + SPLIT):
                    rows = pl.ds(start, 16)
                    tiles.append(
                        [
                            from_left_ref[g, rows, :],
                            pltpu.roll(own_left[g, rows, :], 16, 1),
                            pltpu.roll(own_right[g, rows, :], 32, 1),
                            pltpu.roll(from_right_ref[g, rows, :], 48, 1),
                        ]
                    )
                for m in range(4):
                    place = (lane - 16 * m) % 128
                    spot = place % 64
                    upper, lower = [
                        jnp.where(
                            spot < 32, jnp.where(spot < 16, t[0], t[1]), jnp.where(spot < 48, t[2], t[3])
                        )
                        for t in tiles
                    ]
                    straight = jnp.where(place < 64, upper, lower)
                    crossed = jnp.where(place < 64, lower, upper)
                    if m > 0:
                        straight = pltpu.roll(straight, LANES - 16 * m, 1)
                        crossed = pltpu.roll(crossed, LANES - 16 * m, 1)
                    crossed = pltpu.roll(crossed, 64, 1)
                    for layer, y in (
                        (m, jnp.where(lane < 64, straight, crossed)),
                        (m + 4, jnp.where(lane < 64, crossed, straight)),
                    ):
                        if field == 1:
                            y = jnp.where(good, y, 0.0)
                        side[half * 8 + layer, pl.ds(first, 16), :] = y

    sides = Level(0, [rh], [axh], [ayh], [dh], [eh], [gh])
    sides.faces([(4, 16), (20, 16)])
    sides.factor_and_first([(5, 16), (19, 16)], inside, [fh], [firsth])
    sides.relax([(6, 16), (18, 16)], [fh], [firsth], [vh], u=[uh])
    sides.residual([(8, 24)], [fh], [uh], [firsth])

    main_matrix = one_hot(LANES, lambda s, t: (s // 2 + 32 == t) & (s >= 4) & (s < 124), 0.25)
    upper_matrix, lower_matrix = [
        one_hot(
            LANES,
            lambda s, t: ((s // 2 - base // 2 + 24 == t) & (s >= base + 6) & (s < base + 20))
            | ((s // 2 - base // 2 + 72 == t) & (s >= base + 44) & (s < base + 58)),
            0.25,
        )
        for base in (0, 64)
    ]
    for first in range(0, NZ, 4):
        ks = range(first, first + 4)
        for target, main, side in ((f1, resm, firsth), (rho1, rm, rh)):
            total = split_dot(stack_rows([pair_rows(main, k, 0, 32) for k in ks]), main_matrix)
            upper = split_dot(stack_rows([pair_rows(side, k, 0, 16) for k in ks]), upper_matrix)
            lower = split_dot(stack_rows([pair_rows(side, k, 8, 16) for k in ks]), lower_matrix)
            for n, k in enumerate(ks):
                target[k, pl.ds(0, 16), :] = total[n * 32 : n * 32 + 16] + upper[n * 16 : n * 16 + 16]
                target[k, pl.ds(16, 16), :] = total[n * 32 + 16 : n * 32 + 32] + lower[n * 16 : n * 16 + 16]

    middle = Level(1, [rho1], [ax1], [ay1], [d1], [e1], [g1])
    inside = inside_of(1, ix, iy, (grid_rows // 2, grid_lanes // 2, 16, 64))
    middle.faces([(4, 24), (21, 8)])
    middle.factor_and_first([(4, 24)], inside, [f1], [first1])
    middle.relax([(4, 24)], [f1], [first1], [v1], u=[u1])
    middle.residual([(8, 16)], [f1], [u1], [res1])

    pack_matrix = one_hot(
        LANES,
        lambda s, t: jnp.logical_and(
            s // 2 - 16 == (t // LANES) * 16 + t % 16, jnp.logical_and(s >= 32, s < 96)
        ),
        0.25,
        2 * LANES,
    )
    slot = lanes_of() // 16
    for field, ref in enumerate((res1, rho1)):
        wide = split_dot(stack_rows([pair_rows(ref, k, 8, 8) for k in range(NZ)]), pack_matrix)
        for side in range(2):
            for half in range(2):
                packed = None
                for q in range(8):
                    k = half * 8 + q
                    x = wide[k * 8 : (k + 1) * 8, side * LANES : (side + 1) * LANES]
                    packed = x if q == 0 else jnp.where(slot == q, x, packed)
                pack_ref[side * 4 + field * 2 + half, :, :] = packed


def coarser_kernel(
    grid, index_ref, own_left_ref, own_right_ref, from_left_ref, from_right_ref,
    pack_ref, f2, v2, ax2, ay2, d2, e2, g2, f3, v3, ax3, ay3, d3, e3, g3,
    rho2, first2, u2, res2, rho3, first3, u3, res3,
):
    ix, iy = index_ref[0], index_ref[1]
    grid_rows, grid_lanes = grid
    lane = lanes_of()
    inside = inside_of(2, ix, iy, (grid_rows // 4, grid_lanes // 4, 8, 32))

    lane40 = lanes_of((40, LANES))
    good = inside(0, 40)
    for field, target in enumerate((f2, rho2)):
        for half in range(2):
            g = field * 2 + half
            tiles = [
                from_left_ref[g],
                pltpu.roll(own_left_ref[g], 16, 1),
                pltpu.roll(own_right_ref[g], 32, 1),
                pltpu.roll(from_right_ref[g], 48, 1),
            ]
            for m in range(4):
                place = (lane40 - 16 * m) % 64
                merged = jnp.where(
                    place < 32,
                    jnp.where(place < 16, tiles[0], tiles[1]),
                    jnp.where(place < 48, tiles[2], tiles[3]),
                )
                for q in (m, m + 4):
                    y = merged if q == 0 else pltpu.roll(merged, LANES - 16 * q, 1)
                    if field == 1:
                        y = jnp.where(good, y, 0.0)
                    target[half * 8 + q, :, :] = y

    level2 = Level(2, [rho2], [ax2], [ay2], [d2], [e2], [g2])
    level2.faces([(4, 16, 2), (29, 8)])
    level2.factor_and_first([(4, 16, 2)], inside, [f2], [first2])
    level2.relax([(4, 16, 2)], [f2], [first2], [v2], u=[u2])
    level2.residual([(4, 16, 2)], [f2], [u2], [res2])

    halve = one_hot(LANES, lambda s, t: s // 2 == t, 0.25)
    for ref, target, first, count in ((res2, f3, 4, 16), (rho2, rho3, 4, 16)):
        total = split_dot(stack_rows([pair_rows(ref, k, first, count) for k in range(NZ)]), halve)
        for k in range(NZ):
            target[k, pl.ds(first // 2, count), :] = total[k * count : (k + 1) * count]

    level3 = Level(3, [rho3], [ax3], [ay3], [d3], [e3], [g3])
    inside = inside_of(3, ix, iy, (grid_rows // 8, grid_lanes // 8, 4, 16))
    level3.faces([(2, 16)])
    level3.factor_and_first([(2, 16)], inside, [f3], [first3])
    level3.relax([(2, 16)], [f3], [first3], [v3], u=[u3])
    level3.residual([(6, 8)], [f3], [u3], [res3])

    spread = one_hot(
        LANES,
        lambda s, t: jnp.logical_and(s // 2 - 4 == t % 8, jnp.logical_and(s >= 8, s < 24)),
        0.25,
    )
    for field, ref in enumerate((res3, rho3)):
        total = split_dot(stack_rows([pair_rows(ref, k, 8, 8) for k in range(NZ)]), spread)
        merged = total[0:8]
        for k in range(1, NZ):
            merged = jnp.where(lane // 8 == k, total[k * 8 : (k + 1) * 8], merged)
        pack_ref[pl.ds(2 * field, 2), :] = pltpu.roll(merged, 8 * iy, 1)[0:2]


def prolong(coarse, first_row, count, ref, old, target, target_row, matrix):
    rows = stack_rows([coarse(k) for k in range(NZ)])
    for part in range(len(target)):
        fine = split_dot(rows, matrix[part])
        for k in range(NZ):
            x = fine[k * count : (k + 1) * count]
            for odd in range(2):
                where = pl.ds(target_row + odd, count, stride=2)
                target[part].at[k][where, :] = old[part].at[k][where, :] + x


def top_kernel(
    grid, tiles, index_ref, gathered, fm, vm, axm, aym, dm, em, gm, fh, vh, axh, ayh, dh, eh, gh,
    f1, v1, ax1, ay1, d1, e1, g1, f2, v2, ax2, ay2, d2, e2, g2, f3, v3, ax3, ay3, d3, e3, g3,
    out_ref,
    rho4, f4, ax4, ay4, d4, e4, g4, c4, a4, b4, v4, va3, vb3, va2, vb2, va1, vb1, vam, vah, vbm, vbh,
):
    ix, iy = index_ref[0], index_ref[1]
    grid_rows, grid_lanes = grid
    lane = lanes_of()
    rows4 = grid_rows // 16
    tiles_x, tiles_y = tiles

    zero = jnp.zeros((8, LANES), jnp.float32)
    for ref in (rho4, v4.at[0], v4.at[1]):
        for k in range(NZ):
            ref[k, pl.ds(0, 8), :] = zero
            ref[k, pl.ds(8 + rows4, 8), :] = zero

    count = min(8, tiles_x)
    for field, target in enumerate((f4, rho4)):
        for r in range(2):
            for base in range(0, tiles_x, count):
                xs = [
                    gathered[pl.ds((base * tiles_y + t) * 4 + field * 2 + r, count, stride=4 * tiles_y), :]
                    for t in range(16)
                ]
                block = lanes_of((count, LANES)) // 8
                for bit in (1, 2, 4, 8):
                    moved = (block & bit) != 0
                    xs = [jnp.where(moved, xs[(i + bit) % 16], xs[i]) for i in range(16)]
                for k in range(NZ):
                    x = xs[-k % 16]
                    x = x if k == 0 else pltpu.roll(x, LANES - 8 * k, 1)
                    target.at[k][pl.ds(8 + 2 * base + r, count, stride=2), :] = x

    scale = spacing(4)
    h = min(32, rows4)
    first_lane, last_lane = lanes_of((h, LANES)) == 0, lanes_of((h, LANES)) == LANES - 1
    starts = list(range(8, 8 + rows4, h))

    def faces_x(r, h):
        for k in range(NZ):
            total = rho4[k, pl.ds(r, h), :] + rho4[k, pl.ds(r - 1, h), :]
            ax4[k, pl.ds(r, h), :] = scale * rcp(jnp.maximum(total, TINY))

    for r in starts:
        faces_x(r, h)
    faces_x(rows4 + 1, 8)

    def first_sweep(r):
        rho = rho4[0, pl.ds(r, h), :]
        upper = (2.0 * VERTICAL) * rcp(rho)
        row = rows_of((h, LANES)) + r
        partial, ratio = [], None
        for k in range(NZ):
            here = rho4[k, pl.ds(r, h), :]
            left = jnp.where(first_lane, 0.0, pltpu.roll(here, 1, 1))
            ay = scale * rcp(here + left)
            right = jnp.where(last_lane, scale * rcp(here), pltpu.roll(ay, LANES - 1, 1))
            ay4[k, pl.ds(r, h), :] = jnp.where(first_lane, 0.0, ay)
            up, down = ax4[k, pl.ds(r, h), :], ax4[k, pl.ds(r + 1, h), :]
            center = up + down + ay + right + upper
            across = jnp.where(first_lane, ay, 0.0) + jnp.where(last_lane, right, 0.0)
            along = jnp.where(row == 8, up, 0.0) + jnp.where(row == 7 + rows4, down, 0.0)
            b4[k, pl.ds(r, h), :] = across + along
            if k + 1 < NZ:
                lower = (2.0 * VERTICAL) * rcp(here + rho4[k + 1, pl.ds(r, h), :])
                center = center + lower
            c4[k, pl.ds(r, h), :] = center
            a4[k, pl.ds(r, h), :] = upper
            pivot = center if k == 0 else center - upper * ratio
            inverse = rcp(pivot)
            scaled = 0.8 * inverse
            d4[k, pl.ds(r, h), :] = scaled
            value = scaled * f4[k, pl.ds(r, h), :]
            if k > 0:
                weight = upper * inverse
                e4[k, pl.ds(r, h), :] = weight
                value = value + weight * partial[-1]
            partial.append(value)
            if k + 1 < NZ:
                ratio = lower * inverse
                g4[k, pl.ds(r, h), :] = ratio
                upper = lower
        w = partial[-1]
        v4[0, NZ - 1, pl.ds(r, h), :] = w
        for k in range(NZ - 2, -1, -1):
            w = partial[k] + g4[k, pl.ds(r, h), :] * w
            v4[0, k, pl.ds(r, h), :] = w

    for r in starts:
        first_sweep(r)

    def pulled4(v, k, r):
        here = v[k, pl.ds(r, h), :]
        ay = ay4[k, pl.ds(r, h), :]
        return (
            f4[k, pl.ds(r, h), :]
            + ax4[k, pl.ds(r, h), :] * v[k, pl.ds(r - 1, h), :]
            + ax4[k, pl.ds(r + 1, h), :] * v[k, pl.ds(r + 1, h), :]
            + ay * pltpu.roll(here, 1, 1)
            + pltpu.roll(ay * here, LANES - 1, 1)
        )

    def sweep(v, out):
        for r in starts:
            partial = []
            for k in range(NZ):
                value = d4[k, pl.ds(r, h), :] * pulled4(v, k, r)
                if k > 0:
                    value = value + e4[k, pl.ds(r, h), :] * partial[-1]
                partial.append(value)
            w = None
            for k in range(NZ - 1, -1, -1):
                w = partial[k] if w is None else partial[k] + g4[k, pl.ds(r, h), :] * w
                out[k, pl.ds(r, h), :] = 0.2 * v[k, pl.ds(r, h), :] + w

    def one_sweep(number, carry):
        sweep(v4.at[number % 2], v4.at[1 - number % 2])
        return carry

    lax.fori_loop(0, SWEEPS - 1, one_sweep, 0)
    final = v4.at[(SWEEPS - 1) % 2]

    shifts, flux = [], [None] * len(starts)
    for k in range(NZ):
        left_over, weights = None, None
        for n, r in enumerate(starts):
            v = final[k, pl.ds(r, h), :]
            part = f4[k, pl.ds(r, h), :] - b4[k, pl.ds(r, h), :] * v
            part = part - (a4[0, pl.ds(r, h), :] * v if k == 0 else flux[n])
            if k + 1 < NZ:
                flux[n] = a4[k + 1, pl.ds(r, h), :] * (final[k + 1, pl.ds(r, h), :] - v)
                part = part + flux[n]
            center = c4[k, pl.ds(r, h), :]
            left_over = part if left_over is None else left_over + part
            weights = center if weights is None else weights + center
        raised = jnp.sum(left_over, axis=(0, 1), keepdims=True)
        shifts.append(raised / jnp.sum(weights, axis=(0, 1), keepdims=True))

    row = rows_of() + (ix * 2 - 4)
    column = lane + (iy * 8 - 4)
    good = jnp.logical_and(
        jnp.logical_and(row >= 0, row < rows4),
        jnp.logical_and(jnp.logical_and(column >= 0, column < grid_lanes // 16), lane < 16),
    )
    amount = lax.rem(132 - iy * 8, LANES)

    def coarsest(k):
        x = final[k, pl.ds(4 + 2 * ix, 8), :] + shifts[k]
        return jnp.where(good, pltpu.roll(x, amount, 1), 0.0)

    repeat = one_hot(LANES, lambda s, t: s == t // 2, 1.0)
    prolong(coarsest, 0, 8, None, [v3], [va3], 0, [repeat])
    level3 = Level(3, None, [ax3], [ay3], [d3], [e3], [g3])
    level3.relax([(2, 16)], [f3], [va3], [vb3])
    level3.relax([(6, 8)], [f3], [vb3], [va3])

    prolong(lambda k: va3[k, pl.ds(6, 8), :], 0, 8, None, [v2], [va2], 12, [repeat])
    level2 = Level(2, None, [ax2], [ay2], [d2], [e2], [g2])
    level2.relax([(12, 16)], [f2], [va2], [vb2])
    level2.relax([(12, 16)], [f2], [vb2], [va2])

    prolong(lambda k: va2[k, pl.ds(12, 16), :], 0, 16, None, [v1], [va1], 0, [repeat])
    level1 = Level(1, None, [ax1], [ay1], [d1], [e1], [g1])
    level1.relax([(4, 24)], [f1], [va1], [vb1])
    level1.relax([(4, 24)], [f1], [vb1], [va1])

    to_main = one_hot(LANES, lambda s, t: s == t // 2 + 32, 1.0)
    prolong(lambda k: va1[k, pl.ds(4, 24), :], 0, 24, None, [vm], [vam], 8, [to_main])
    lane = lanes_of((16, LANES))
    to_upper, to_lower = [
        one_hot(
            LANES,
            lambda s, t: ((t < base + 32) & (t >= base) & (s == (t - base) // 2 + 24))
            | ((t >= base + 32) & (t < base + 64) & (s == (t - base) // 2 + 72)),
            1.0,
        )
        for base in (0, 64)
    ]
    upper = split_dot(stack_rows([va1[k, pl.ds(2, 16), :] for k in range(NZ)]), to_upper)
    lower = split_dot(stack_rows([va1[k, pl.ds(2 + SPLIT // 2, 16), :] for k in range(NZ)]), to_lower)
    for k in range(NZ):
        x = jnp.where(lane < 64, upper[k * 16 : k * 16 + 16], lower[k * 16 : k * 16 + 16])
        for odd in range(2):
            where = pl.ds(4 + odd, 16, stride=2)
            vah.at[k][where, :] = vh.at[k][where, :] + x
    sides = Level(0, None, [axh], [ayh], [dh], [eh], [gh])
    sides.relax([(7, 16), (17, 16)], [fh], [vah], [vbh])
    sides.relax([(8, 24)], [fh], [vbh], [vah])
    main = Level(0, None, [axm], [aym], [dm], [em], [gm])
    main.relax([(15, 16), (31, 16), (41, 8)], [fm], [vam], [vbm])
    main.relax([(16, 16), (32, 16)], [fm], [vbm], [vam])
    for k in range(NZ):
        for row, start, low, high in ((0, 16, 112, 80), (16, 16 - SPLIT + 16, 48, 16)):
            side = vah[k, pl.ds(start, 16), :]
            side = jnp.where(lane < 64, pltpu.roll(side, low, 1), pltpu.roll(side, high, 1))
            x = vam[k, pl.ds(16 + row, 16), :]
            out_ref[k, pl.ds(row, 16), :] = jnp.where(jnp.logical_or(lane < 4, lane >= 124), side, x)


def ring(x, axis, step):
    size = lax.axis_size(axis)
    return lax.ppermute(x, axis, [(i, (i + step) % size) for i in range(size)])


def gather(x, axis):
    size = lax.axis_size(axis)
    blocks = jnp.broadcast_to(x[None], (size,) + x.shape)
    return lax.all_to_all(blocks, axis, 0, 0).reshape(size * x.shape[0], LANES)


def array(*shape):
    return jax.ShapeDtypeStruct(shape, jnp.float32)


def call(kernel, name, outs, scratch, index, *operands, cost=4000000):
    vmem = pl.BlockSpec(memory_space=pltpu.VMEM)
    ins = [vmem] * len(operands)
    if index is not None:
        ins, operands = [pl.BlockSpec(memory_space=pltpu.SMEM)] + ins, (index,) + operands
    return pl.pallas_call(
        kernel,
        out_shape=outs,
        in_specs=ins,
        out_specs=[vmem] * len(outs),
        scratch_shapes=[pltpu.VMEM(shape, jnp.float32) for shape in scratch],
        compiler_params=pltpu.CompilerParams(vmem_limit_bytes=VMEM_BYTES),
        cost_estimate=pl.CostEstimate(flops=cost, bytes_accessed=cost, transcendentals=0),
        name=name,
    )(*operands)


def solution(mesh):
    tiles_x, tiles_y = mesh.shape["gx"], mesh.shape["gy"]
    grid = (32 * tiles_x, 128 * tiles_y)
    big = [array(NZ, ROWS[level], LANES) for level in range(4)]

    def on_device(source, rho):
        index = jnp.stack([lax.axis_index("gx"), lax.axis_index("gy")]).astype(jnp.int32)

        both = jnp.concatenate([source, rho], axis=0).transpose(1, 0, 2)
        lows = both[:REACH].reshape(REACH * 2 * NZ, LANES)
        highs = both[-REACH:].reshape(REACH * 2 * NZ, LANES)
        up = ring(highs, "gx", 1)
        dn = ring(lows, "gx", -1)
        s0, s1, s2, s3 = [x.shape for x in big]
        sh = (NZ, SIDE_ROWS, LANES)
        strip = array(4, ROWS[0], LANES)
        own_strips = call(own_edges_kernel, "own_edges", [strip, strip], [], None, source, rho)
        lefts, rights = call(edges_kernel, "edges", [strip, strip], [], None, up, dn, *own_strips)
        from_left_strip = ring(rights, "gy", 1)
        from_right_strip = ring(lefts, "gy", -1)
        main = call(
            lambda *refs: main_kernel(grid, *refs), "main", [big[0]] * 9, [s0] * 2, index, source, rho, up, dn
        )
        main_state, rho_main, residual_main = main[:7], main[7], main[8]
        fine = call(
            lambda *refs: fine_kernel(grid, *refs),
            "fine",
            [array(8, 8, LANES)] + [array(*sh)] * 7 + [big[1]] * 7,
            [sh] * 3 + [s1] * 4,
            index, rho_main, residual_main, lefts, rights, from_left_strip, from_right_strip,
        )
        tile = fine[0]
        pieces = [ring(tile, "gx", 2), ring(tile, "gx", 1), tile, ring(tile, "gx", -1), ring(tile, "gx", -2)]
        own_left = jnp.concatenate([piece[:4] for piece in pieces], axis=1)
        own_right = jnp.concatenate([piece[4:] for piece in pieces], axis=1)
        from_left_column = ring(own_right, "gy", 1)
        from_right_column = ring(own_left, "gy", -1)
        coarser = call(
            lambda *refs: coarser_kernel(grid, *refs),
            "coarser",
            [array(4, LANES)] + [big[2]] * 7 + [big[3]] * 7,
            [s2] * 4 + [s3] * 4,
            index, own_left, own_right, from_left_column, from_right_column,
        )
        gathered = gather(gather(coarser[0], "gy"), "gx")

        s4 = (NZ, 16 + 2 * tiles_x, LANES)
        (pressure,) = call(
            lambda *refs: top_kernel(grid, (tiles_x, tiles_y), *refs),
            "top",
            [array(NZ, 32, LANES)],
            [s4] * 10 + [(2,) + s4] + [s3] * 2 + [s2] * 2 + [s1] * 2 + [s0, sh] * 2,
            index, gathered, *main_state, *fine[1:], *coarser[1:],
        )
        return pressure

    return jax.shard_map(
        on_device,
        mesh=mesh,
        in_specs=(P(None, "gx", "gy"), P(None, "gx", "gy")),
        out_specs=P(None, "gx", "gy"),
        check_vma=False,
    )
```
